128 devices in a mesh: dp: 2 (over core), expert: 64 (over z, x, y).
Axes of the slice: x: 4, y: 4, z: 4, core: 2. Of those that a mesh axis runs over, the one named last changes fastest.
Arguments:
- tokens: bfloat16 [16384, 2048], P(('dp', 'expert')), may hold values from -6 to 6
- route_ids: int32 [16384, 8], P(('dp', 'expert')), may hold values from 0 to 63, all different within a row; in each aligned block of 128 rows (0 to 127, 128 to 255, ...) at most 28 rows name the same one
- route_probs: float32 [16384, 8], P(('dp', 'expert')), may hold values from 0.02 to 0.4
- cotangent: bfloat16 [16384, 2048], P(('dp', 'expert')), may hold values from -6 to 6
- w_gate: bfloat16 [64, 2048, 768], P('expert'), may hold values from -0.125 to 0.125
- w_up: bfloat16 [64, 2048, 768], P('expert'), may hold values from -0.125 to 0.125
- w_down: bfloat16 [64, 768, 2048], P('expert'), may hold values from -0.21875 to 0.21875
Outputs:
- mixed: bfloat16 [16384, 2048], P(('dp', 'expert'))
- grad_tokens: bfloat16 [16384, 2048], P(('dp', 'expert'))
- grad_probs: float32 [16384, 8], P(('dp', 'expert'))
- grad_gate: bfloat16 [64, 2048, 768], P('expert', None, 'dp')
- grad_up: bfloat16 [64, 2048, 768], P('expert', None, 'dp')
- grad_down: bfloat16 [64, 768, 2048], P('expert', None, 'dp')
The draws below stay inside these ranges and needn't reach their ends.
Inputs may be any that keep to these rules, and one draw needn't show every extreme that they name: `route_ids`: each token names 8 different experts. Among the 128 tokens of one device (aligned blocks of rows), no expert is named more than 28 times, a bound that some block reaches.
All inputs are finite; a program needn't handle non-finite values.
Results may differ from the reference program's by a relative error of at most 0.012.
Values may be sent and summed in bfloat16 or wider, within the bound.
A program may use at most 256 MiB of HBM per device.

```python
import math
import jax
import jax.numpy as jnp
import numpy as np
from jax import lax

D = 2048
FF = 768
TOP = 8
BLOCK = 128
TOK_DEV = 128
EXPERTS = 64
CAP = 28
TOKENS = 16384


def level_of(key, extent, split, smallest, largest):
    gain = 1.0
    for axis_at, blocks in split:
        draws = jax.random.uniform(jax.random.fold_in(jax.random.fold_in(key, 6), axis_at), (blocks,), jnp.float32, smallest / len(split), largest / len(split))
        gain = gain * jnp.repeat(jnp.exp(draws), extent[axis_at] // blocks).reshape((-1,) + (1,) * (len(extent) - 1 - axis_at))
    return gain


def routed_block(rng, own, number, rows, count, top, bound, skew):
    sequence = jax.random.permutation(rng, count)
    crowded, ordinary = portions_of(count, rows * top, bound, skew, True), portions_of(count, rows * top, bound, skew, False)
    places = jnp.arange(count)

    def named(tallies, offset_by):
        used = int((tallies > 0).sum())
        fixed = max(1, used // 4)
        shifted = fixed + (places - fixed + offset_by * (used - fixed)) % max(1, count - fixed)
        return jnp.zeros((count,), jnp.int32).at[sequence[jnp.where(places < fixed, places, shifted)]].set(jnp.asarray(tallies, jnp.int32))

    tallies = jnp.where(number % 4 == 0, named(crowded, number // 4), named(ordinary, number - number // 4 - 1))
    mixed = jax.random.permutation(jax.random.fold_in(own, 3), count)
    giver, taker = mixed[0:count // 2 * 2:2], mixed[1:count // 2 * 2:2]
    margin = jnp.minimum(tallies[giver] - 1, bound - tallies[taker]) // 2
    margin = jnp.where((giver == sequence[0]) | (taker == sequence[0]) | (tallies[taker] == 0), 0, jnp.maximum(margin, 0))
    shifted = jax.random.randint(jax.random.fold_in(own, 4), (count // 2,), 0, 1 << 20) % (margin + 1)
    tallies = tallies.at[giver].add(-shifted).at[taker].add(shifted)
    members = jnp.searchsorted(jnp.cumsum(tallies), jnp.arange(rows * top), side="right").astype(jnp.int32)
    grid = members.reshape(top, rows).T
    grid = grid[jax.random.permutation(jax.random.fold_in(own, 1), rows)]
    offset_by = jax.random.randint(jax.random.fold_in(own, 2), (rows, 1), 0, top)
    return jnp.take_along_axis(grid, (jnp.arange(top)[None, :] + offset_by) % top, axis=1)


def portions_of(amount, total, bound, skew, full):
    weights = [(1 << 20) // math.isqrt(grade ** skew) + 1 for grade in range(1, amount + 1)]
    largest = bound if full else min(bound, max(-(-total // amount), total * weights[0] // sum(weights)))
    least = 1 if total - largest >= amount - 1 else 0
    given, rest = [largest] + [least] * (amount - 1), total - largest - least * (amount - 1)
    while rest > 0:
        free = [i for i in range(1, amount) if given[i] < largest] or [i for i in range(1, amount) if given[i] < bound]
        mass, budget = sum([weights[i] for i in free]), rest
        for i in free:
            extra = min(bound - given[i], max(1, budget * weights[i] // mass), rest)
            given[i] = given[i] + extra
            rest = rest - extra
    return np.array(given)


def noise(stream_key, shape, width, bound, pieces=(), kind=jnp.bfloat16):
    values = jax.random.normal(stream_key, shape, jnp.float32) * width
    if len(pieces) > 0:
        values = level_of(stream_key, shape, pieces, -0.22, 0.18) * values
    return jnp.clip(values, min=-bound, max=bound).astype(kind)


def setup_inputs(seed: int = 0) -> dict:
    streams_of = jax.random.split(jax.random.key(seed), 8)
    tokens = noise(streams_of[0], (TOKENS, D), 1.0, 6.0, ((0, 128),))
    route_ids_keys = jax.random.split(jax.random.fold_in(streams_of[1], 1), TOKENS // TOK_DEV)
    route_ids_turns = jax.random.permutation(jax.random.fold_in(streams_of[1], 3), TOKENS // TOK_DEV)
    route_ids = jax.vmap(lambda own, number: routed_block(jax.random.fold_in(streams_of[1], 2), own, number, TOK_DEV, EXPERTS, TOP, CAP, 2))(route_ids_keys, route_ids_turns).reshape((TOKENS, TOP))
    route_probs = jnp.clip(jnp.exp(math.log(0.4) - 2.9957323 * jax.random.uniform(streams_of[2], (TOKENS, TOP), jnp.float32) ** level_of(streams_of[2], (TOKENS, TOP), ((0, 128),), -0.2, 0.2)), 0.02, 0.4)
    cotangent = noise(streams_of[3], (TOKENS, D), 1.0, 6.0, ((0, 128),))
    w_gate = noise(streams_of[4], (EXPERTS, D, FF), D ** -0.5, 0.125, ((0, 64),))
    w_up = noise(streams_of[5], (EXPERTS, D, FF), D ** -0.5, 0.125, ((0, 64),))
    w_down = noise(streams_of[6], (EXPERTS, FF, D), FF ** -0.5, 0.21875, ((0, 64),))
    return {"tokens": tokens, "route_ids": route_ids, "route_probs": route_probs, "cotangent": cotangent, "w_gate": w_gate, "w_up": w_up, "w_down": w_down}


def silu_parts(gate_pre):
    sigmoid = jax.nn.sigmoid(gate_pre)
    return gate_pre * sigmoid, sigmoid * (1.0 + gate_pre * (1.0 - sigmoid))


def reference(tokens, route_ids, route_probs, cotangent, w_gate, w_up, w_down):
    pair_count = TOKENS * TOP
    flat_ids = route_ids.reshape(pair_count).astype(jnp.int32)
    flat_probs = route_probs.reshape(pair_count)
    order = jnp.argsort(flat_ids, stable=True).astype(jnp.int32)
    expert_ids = jnp.arange(EXPERTS, dtype=jnp.int32)
    counts = jnp.sum((flat_ids[:, None] == expert_ids[None, :]).astype(jnp.int32), axis=0)
    run_starts = jnp.cumsum(counts) - counts
    padded = (counts + BLOCK - 1) // BLOCK * BLOCK
    pad_ends = jnp.cumsum(padded)
    pad_starts = pad_ends - padded
    block_count = pair_count // BLOCK + EXPERTS
    sorted_at = jnp.zeros((pair_count,), jnp.int32).at[order].set(jnp.arange(pair_count, dtype=jnp.int32))
    pair_rows = (pad_starts[flat_ids] + sorted_at - run_starts[flat_ids]).astype(jnp.int32)

    def block_step(carried, block_index):
        acc_gate, acc_up, acc_down = carried
        row_start = block_index * BLOCK
        owner = jnp.minimum(jnp.sum((pad_ends <= row_start).astype(jnp.int32)), EXPERTS - 1)
        local_row = row_start + jnp.arange(BLOCK, dtype=jnp.int32) - pad_starts[owner]
        is_live = local_row < counts[owner]
        pair_of = order[jnp.clip(run_starts[owner] + local_row, 0, pair_count - 1)]
        token_of = pair_of // TOP
        row_inputs = jnp.where(is_live[:, None], tokens[token_of], jnp.zeros((), tokens.dtype))
        weights_row = jnp.where(is_live, flat_probs[pair_of], jnp.zeros((), flat_probs.dtype))
        grad_out = (weights_row[:, None] * cotangent[token_of].astype(jnp.float32)).astype(jnp.bfloat16)
        gate_matrix = w_gate[owner]
        up_matrix = w_up[owner]
        down_matrix = w_down[owner]
        gate_pre = jnp.dot(row_inputs, gate_matrix, preferred_element_type=jnp.float32)
        up_pre = jnp.dot(row_inputs, up_matrix, preferred_element_type=jnp.float32)
        activation, derivative = silu_parts(gate_pre)
        hidden = (activation * up_pre).astype(jnp.bfloat16)
        outputs = jnp.dot(hidden, down_matrix, preferred_element_type=jnp.float32).astype(jnp.bfloat16)
        grad_hidden = jnp.dot(grad_out, down_matrix.T, preferred_element_type=jnp.float32)
        grad_gate_pre = (grad_hidden * up_pre * derivative).astype(jnp.bfloat16)
        grad_up_pre = (grad_hidden * activation).astype(jnp.bfloat16)
        grad_rows = (jnp.dot(grad_gate_pre, gate_matrix.T, preferred_element_type=jnp.float32)
                     + jnp.dot(grad_up_pre, up_matrix.T, preferred_element_type=jnp.float32)).astype(jnp.bfloat16)
        acc_gate = acc_gate.at[owner].add(jnp.dot(row_inputs.T, grad_gate_pre, preferred_element_type=jnp.float32))
        acc_up = acc_up.at[owner].add(jnp.dot(row_inputs.T, grad_up_pre, preferred_element_type=jnp.float32))
        acc_down = acc_down.at[owner].add(jnp.dot(hidden.T, grad_out, preferred_element_type=jnp.float32))
        return (acc_gate, acc_up, acc_down), (outputs, grad_rows)

    start_state = (jnp.zeros((EXPERTS, D, FF), jnp.float32), jnp.zeros((EXPERTS, D, FF), jnp.float32),
                   jnp.zeros((EXPERTS, FF, D), jnp.float32))
    final_state, per_block = lax.scan(block_step, start_state, jnp.arange(block_count, dtype=jnp.int32))
    acc_gate, acc_up, acc_down = final_state
    out_blocks, grad_blocks = per_block
    expert_out = out_blocks.reshape(block_count * BLOCK, D)[pair_rows].reshape(TOKENS, TOP, D)
    grad_pairs = grad_blocks.reshape(block_count * BLOCK, D)[pair_rows].reshape(TOKENS, TOP, D)
    mixed = jnp.einsum('tk,tkd->td', route_probs.astype(jnp.float32), expert_out.astype(jnp.float32)).astype(jnp.bfloat16)
    grad_probs = jnp.einsum('tkd,td->tk', expert_out.astype(jnp.float32), cotangent.astype(jnp.float32))
    grad_tokens = jnp.sum(grad_pairs.astype(jnp.float32), axis=1).astype(jnp.bfloat16)
    return (mixed, grad_tokens, grad_probs, acc_gate.astype(jnp.bfloat16), acc_up.astype(jnp.bfloat16),
            acc_down.astype(jnp.bfloat16))
```

```python
import functools

import jax
import jax.numpy as jnp
from jax import lax
from jax.experimental import pallas as pl
from jax.experimental.pallas import tpu as pltpu
from jax.sharding import PartitionSpec as P

D = 2048
FF = 768
TOP = 8
TOK = 128
CAP = 28
SIDE = 4
EXPERTS = 64
GROUP = SIDE * CAP
ROWS = 16 * GROUP
WIDE = D + 128
HALF = 2
MESH = pl.DeviceIdType.MESH
VMEM_LIMIT = 60 * 1024 * 1024


def where_am_i():
    e = lax.axis_index("expert")
    return lax.axis_index("dp"), e // 16, (e // 4) % 4, e % 4


class Way:
    def __init__(self, t):
        self.t = t
        self.dp, z, self.x, y = where_am_i()
        self.a, self.b = (y, z) if t == 0 else (z, y)

    def dev(self, a, b, x):
        z, y = (b, a) if self.t == 0 else (a, b)
        return (self.dp, z * 16 + x * 4 + y)

    def block(self, a, b):
        return a * 4 + b if self.t == 0 else b * 4 + a


def step(v, d):
    return lax.rem(v + d + SIDE, SIDE)


def greet_lines():
    dp, z, x, y = where_am_i()
    barrier = pltpu.get_barrier_semaphore()
    for d in (1, 2, 3):
        for to in (
            step(z, d) * 16 + x * 4 + y,
            z * 16 + step(x, d) * 4 + y,
            z * 16 + x * 4 + step(y, d),
        ):
            pl.semaphore_signal(barrier, inc=1, device_id=(dp, to), device_id_type=MESH)
    pl.semaphore_wait(barrier, 9)


def remote(src, dst, send, recv, dev):
    return pltpu.make_async_remote_copy(
        src_ref=src, dst_ref=dst, send_sem=send, recv_sem=recv, device_id=dev, device_id_type=MESH
    )


def own_table(t, ids_ref, probs_ref):
    row = lax.broadcasted_iota(jnp.int32, (TOK, TOK), 0)
    b, x, kind, a = row // 32, (row // 8) % 4, (row // 4) % 2, row % 4
    expert = b * 16 + x * 4 + a if t == 0 else a * 16 + x * 4 + b
    hit = jnp.zeros((TOK, TOK), jnp.float32)
    weight = jnp.zeros((TOK, TOK), jnp.float32)
    for k in range(TOP):
        same = expert == ids_ref[k : k + 1, :]
        hit = jnp.where(same, 1.0, hit)
        weight = jnp.where(same, probs_ref[k : k + 1, :], weight)
    before = lax.broadcasted_iota(jnp.int32, (TOK, TOK), 0) < lax.broadcasted_iota(
        jnp.int32, (TOK, TOK), 1
    )
    before = jnp.where(before, 1.0, 0.0).astype(jnp.bfloat16)
    slot = jnp.dot(hit.astype(jnp.bfloat16), before, preferred_element_type=jnp.float32)
    slot = jnp.where(hit > 0.5, slot, -1000.0)
    return jnp.where(kind == 0, slot, weight)


def lane_rows(tables, kind, a):
    return [tables[xs, kind * 4 + a : kind * 4 + a + 1, :] for xs in range(SIDE)]


def hits_of(tables, a):
    slots = jnp.concatenate(
        [v + float(CAP * xs) for xs, v in enumerate(lane_rows(tables, 0, a))], axis=1
    )
    row = lax.broadcasted_iota(jnp.int32, (GROUP, SIDE * TOK), 0).astype(jnp.float32)
    return row == slots


def dispatch_kernel(
    ids_ref, probs_ref, tok_ref, cot_ref, x_rows, g_rows, tab_out,
    gath, stage, own_tab, tab_a, tab_b, pick, scale,
    s1, r1, s2, r2, s3, r3, ts1, tr1, ts2, tr2, ls,
):
    ways = (Way(0), Way(1))
    rows_out = (x_rows, g_rows)
    width = D // HALF

    for t, src in ((0, tok_ref), (1, cot_ref)):
        w = ways[t]
        own_tab[t] = own_table(t, ids_ref, probs_ref).reshape(16, 8, TOK)
        gath[t, w.b, w.x] = src[...]
        tab_a[t, w.b] = own_tab[t, pl.ds(w.b * 4, 4)]
    greet_lines()

    def first(t, d, h):
        w = ways[t]
        cols = pl.ds(h * width, width)
        ref = gath.at[t, w.b, w.x, :, cols]
        return remote(ref, ref, s1.at[t, d - 1, h], r1.at[t, d - 1, h],
                      w.dev(w.a, step(w.b, d), w.x))

    def first_tab(t, d):
        w = ways[t]
        to = step(w.b, d)
        return remote(own_tab.at[t, pl.ds(to * 4, 4)], tab_a.at[t, w.b],
                      ts1.at[t, d - 1], tr1.at[t, d - 1], w.dev(w.a, to, w.x))

    def second(t, kk, d, h):
        w = ways[t]
        bs = step(w.b, -kk)
        ref = gath.at[t, bs, w.x, :, pl.ds(h * width, width)]
        return remote(ref, ref, s2.at[t, kk, d - 1, h], r2.at[t, kk, d - 1, h],
                      w.dev(w.a, w.b, step(w.x, d)))

    def second_tab(t, kk, d):
        w = ways[t]
        bs = step(w.b, -kk)
        to = step(w.x, d)
        return remote(tab_a.at[t, bs, to], tab_b.at[t, bs, w.x],
                      ts2.at[t, kk, d - 1], tr2.at[t, kk, d - 1], w.dev(w.a, w.b, to))

    def third(t, kk, d, h):
        w = ways[t]
        bs = step(w.b, -kk)
        to = step(w.a, d)
        cols = pl.ds(h * width, width)
        return remote(stage.at[t, kk, to, :, cols],
                      rows_out[t].at[w.block(w.a, bs), :, cols],
                      s3.at[t, kk, d - 1, h], r3.at[t, kk, d - 1, h], w.dev(to, w.b, w.x))

    def kept(t, kk, h):
        w = ways[t]
        bs = step(w.b, -kk)
        cols = pl.ds(h * width, width)
        return pltpu.make_async_copy(stage.at[t, kk, w.a, :, cols],
                                     rows_out[t].at[w.block(w.a, bs), :, cols],
                                     ls.at[t, kk, h])

    def start_second(kk, h):
        for t in (0, 1):
            w = ways[t]
            bs = step(w.b, -kk)
            if kk > 0:
                first(t, kk, h).wait_recv()
                if h == 0:
                    first_tab(t, kk).wait_recv()
            if h == 0:
                tab_b[t, bs, w.x] = tab_a[t, bs, w.x]
                for d in (1, 2, 3):
                    second_tab(t, kk, d).start()
            for d in (1, 2, 3):
                second(t, kk, d, h).start()

    for t in (0, 1):
        for d in (1, 2, 3):
            first_tab(t, d).start()
    start_second(0, 0)
    for h in range(HALF):
        for t in (0, 1):
            for d in (1, 2, 3):
                first(t, d, h).start()

    turns = [(kk, h) for kk in range(SIDE) for h in range(HALF)]
    for n, (kk, h) in enumerate(turns):
        if n + 1 < len(turns):
            start_second(*turns[n + 1])
        for t in (0, 1):
            w = ways[t]
            bs = step(w.b, -kk)
            for d in (1, 2, 3):
                if h == 0:
                    second_tab(t, kk, d).wait_recv()
                second(t, kk, d, h).wait_recv()
            if h == 0:
                tables = tab_b[t, bs]
                for a in range(SIDE):
                    hit = hits_of(tables, a)
                    pick[t, a * GROUP : (a + 1) * GROUP, :] = jnp.where(hit, 1.0, 0.0).astype(
                        jnp.bfloat16
                    )
                    if t == 1:
                        weight = jnp.concatenate(lane_rows(tables, 1, a), axis=1)
                        weight = jnp.sum(jnp.where(hit, weight, 0.0), axis=1, keepdims=True)
                        scale[a * GROUP : (a + 1) * GROUP, :] = jnp.broadcast_to(
                            weight, (GROUP, 128)
                        )

            def tile(c, _, t=t, bs=bs, kk=kk, h=h):
                cols = pl.ds(pl.multiple_of(h * width + c * 256, 256), 256)
                block = gath[t, bs, :, :, cols].reshape(SIDE * TOK, 256)
                rows = jnp.dot(pick[t], block, preferred_element_type=jnp.float32)
                if t == 1:
                    rows = rows * jnp.concatenate([scale[...], scale[...]], axis=1)
                stage[t, kk, :, :, cols] = rows.astype(jnp.bfloat16).reshape(SIDE, GROUP, 256)
                return 0

            lax.fori_loop(0, width // 256, tile, 0)
            for d in (1, 2, 3):
                third(t, kk, d, h).start()
            kept(t, kk, h).start()

    tab_out[...] = tab_b[...]
    for t in (0, 1):
        for kk, h in turns:
            for d in (1, 2, 3):
                third(t, kk, d, h).wait()
                second(t, kk, d, h).wait_send()
                if h == 0:
                    second_tab(t, kk, d).wait_send()
            kept(t, kk, h).wait()
        for d in (1, 2, 3):
            first_tab(t, d).wait_send()
            for h in range(HALF):
                first(t, d, h).wait_send()


def dispatch(ids_t, probs_t, tokens, cotangent):
    dma = pltpu.SemaphoreType.DMA
    vmem = pl.BlockSpec(memory_space=pltpu.VMEM)
    hbm = pl.BlockSpec(memory_space=pl.ANY)
    return pl.pallas_call(
        dispatch_kernel,
        name="dispatch",
        out_shape=(
            jax.ShapeDtypeStruct((16, GROUP, D), jnp.bfloat16),
            jax.ShapeDtypeStruct((16, GROUP, D), jnp.bfloat16),
            jax.ShapeDtypeStruct((2, SIDE, SIDE, 8, TOK), jnp.float32),
        ),
        in_specs=[vmem] * 4,
        out_specs=(hbm, hbm, vmem),
        scratch_shapes=[
            pltpu.VMEM((2, SIDE, SIDE, TOK, D), jnp.bfloat16),
            pltpu.VMEM((2, SIDE, SIDE, GROUP, D), jnp.bfloat16),
            pltpu.VMEM((2, 16, 8, TOK), jnp.float32),
            pltpu.VMEM((2, SIDE, SIDE, 8, TOK), jnp.float32),
            pltpu.VMEM((2, SIDE, SIDE, 8, TOK), jnp.float32),
            pltpu.VMEM((2, SIDE * GROUP, SIDE * TOK), jnp.bfloat16),
            pltpu.VMEM((SIDE * GROUP, 128), jnp.float32),
            dma((2, 3, HALF)), dma((2, 3, HALF)),
            dma((2, SIDE, 3, HALF)), dma((2, SIDE, 3, HALF)),
            dma((2, SIDE, 3, HALF)), dma((2, SIDE, 3, HALF)),
            dma((2, 3)), dma((2, 3)),
            dma((2, SIDE, 3)), dma((2, SIDE, 3)),
            dma((2, SIDE, HALF)),
        ],
        compiler_params=pltpu.CompilerParams(
            collective_id=1, has_side_effects=True, vmem_limit_bytes=VMEM_LIMIT
        ),
    )(ids_t, probs_t, tokens, cotangent)


def contract_last(left_side, right_side):
    return lax.dot_general(
        left_side, right_side, (((1,), (1,)), ((), ())), preferred_element_type=jnp.float32
    )


def contract_rows(left_side, right_side):
    return lax.dot_general(
        left_side, right_side, (((0,), (0,)), ((), ())), preferred_element_type=jnp.float32
    )


def expert_kernel(x_ref, g_ref, wg_ref, wu_ref, wd_ref, out_ref, grad_ref, hid_ref, gg_ref, gu_ref):
    rows = x_ref[...]
    gate_pre = jnp.dot(rows, wg_ref[...], preferred_element_type=jnp.float32)
    up_pre = jnp.dot(rows, wu_ref[...], preferred_element_type=jnp.float32)
    sigmoid = jax.nn.sigmoid(gate_pre)
    activation = gate_pre * sigmoid
    derivative = sigmoid * (1.0 + gate_pre * (1.0 - sigmoid))
    hidden = (activation * up_pre).astype(jnp.bfloat16)
    hid_ref[...] = hidden
    out_ref[...] = jnp.dot(hidden, wd_ref[...], preferred_element_type=jnp.float32).astype(
        jnp.bfloat16
    )
    grad_hidden = contract_last(g_ref[...], wd_ref[...])
    gate_grad = (grad_hidden * up_pre * derivative).astype(jnp.bfloat16)
    up_grad = (grad_hidden * activation).astype(jnp.bfloat16)
    gg_ref[...] = gate_grad
    gu_ref[...] = up_grad
    grad_ref[:, :D] = (
        contract_last(gate_grad, wg_ref[...]) + contract_last(up_grad, wu_ref[...])
    ).astype(jnp.bfloat16)
    product = jnp.sum(hidden.astype(jnp.float32) * grad_hidden, axis=1, keepdims=True)
    high = product.astype(jnp.bfloat16)
    low = (product - high.astype(jnp.float32)).astype(jnp.bfloat16)
    lane = lax.broadcasted_iota(jnp.int32, (rows.shape[0], 128), 1)
    me = lax.axis_index("expert")
    marks = jnp.where(lane == me, high.astype(jnp.float32), 0.0)
    marks = jnp.where(lane == me + EXPERTS, low.astype(jnp.float32), marks)
    grad_ref[:, D:] = marks.astype(jnp.bfloat16)


def expert_rows(x_rows, g_rows, w_gate, w_up, w_down):
    bm = 256
    whole = lambda shape: pl.BlockSpec(shape, lambda i: (0, 0), pipeline_mode=pl.Buffered(1))
    part = lambda width: pl.BlockSpec((bm, width), lambda i: (i, 0))
    bf = lambda width: jax.ShapeDtypeStruct((ROWS, width), jnp.bfloat16)
    return pl.pallas_call(
        expert_kernel,
        name="expert_rows",
        grid=(ROWS // bm,),
        out_shape=(bf(D), bf(WIDE), bf(FF), bf(FF), bf(FF)),
        in_specs=[part(D), part(D), whole((D, FF)), whole((D, FF)), whole((FF, D))],
        out_specs=(part(D), part(WIDE), part(FF), part(FF), part(FF)),
        compiler_params=pltpu.CompilerParams(vmem_limit_bytes=VMEM_LIMIT),
        cost_estimate=pl.CostEstimate(
            flops=12 * ROWS * D * FF, bytes_accessed=40_000_000, transcendentals=ROWS * FF
        ),
    )(x_rows, g_rows, w_gate, w_up, w_down)


def weight_kernel(x_ref, g_ref, hid_ref, gg_ref, gu_ref, dg_ref, du_ref, dd_ref,
                  out_g, out_u, out_d, in_g, in_u, in_d, send, recv):
    dp = lax.axis_index("dp")
    e = lax.axis_index("expert")
    other = 1 - dp
    barrier = pltpu.get_barrier_semaphore()
    pl.semaphore_signal(barrier, inc=1, device_id=(other, e), device_id_type=MESH)
    pl.semaphore_wait(barrier, 1)
    jobs = (
        (x_ref, gg_ref, dg_ref, out_g, in_g),
        (x_ref, gu_ref, du_ref, out_u, in_u),
        (hid_ref, g_ref, dd_ref, out_d, in_d),
    )
    copies = []
    for n, (left, right, done, away, back) in enumerate(jobs):
        height = 256
        wide = right.shape[1] // 2

        def send_part(i, _, left=left, right=right, away=away, wide=wide):
            at = pl.ds(pl.multiple_of(i * height, height), height)
            cols = pl.ds(pl.multiple_of(other * wide, wide), wide)
            away[at, :] = contract_rows(left[:, at], right[:, cols]).astype(jnp.bfloat16)
            return 0

        lax.fori_loop(0, left.shape[1] // height, send_part, 0)
        copy = remote(away, back, send.at[n], recv.at[n], (other, e))
        copy.start()
        copies.append(copy)
    for n, (left, right, done, away, back) in enumerate(jobs):
        height = 256
        wide = right.shape[1] // 2
        copies[n].wait()

        def keep_part(i, _, left=left, right=right, back=back, done=done, wide=wide):
            at = pl.ds(pl.multiple_of(i * height, height), height)
            cols = pl.ds(pl.multiple_of(dp * wide, wide), wide)
            mine = contract_rows(left[:, at], right[:, cols])
            done[0, at, :] = (mine + back[at, :].astype(jnp.float32)).astype(jnp.bfloat16)
            return 0

        lax.fori_loop(0, left.shape[1] // height, keep_part, 0)


def weight_grads(x_rows, g_rows, hidden, gate_grad, up_grad):
    vmem = pl.BlockSpec(memory_space=pltpu.VMEM)
    halves = ((D, FF // 2), (D, FF // 2), (FF, D // 2))
    dma = pltpu.SemaphoreType.DMA
    return pl.pallas_call(
        weight_kernel,
        name="weight_grads",
        out_shape=tuple(jax.ShapeDtypeStruct((1,) + s, jnp.bfloat16) for s in halves),
        in_specs=[vmem] * 5,
        out_specs=(vmem,) * 3,
        scratch_shapes=[pltpu.VMEM(s, jnp.bfloat16) for s in halves + halves] + [dma((3,)), dma((3,))],
        compiler_params=pltpu.CompilerParams(
            collective_id=2, has_side_effects=True, vmem_limit_bytes=VMEM_LIMIT
        ),
    )(x_rows, g_rows, hidden, gate_grad, up_grad)


def return_kernel(
    out_rows, grad_rows, tab_ref, mixed_ref, gtok_ref, mark_ref,
    back0, back1, part0, part1, across0, across1, zs0, zs1, zb0, zb1, pick,
    sa, ra, sb, rb, sc, rc, la,
):
    ways = (Way(0), Way(1))
    rows_in = (out_rows, grad_rows)
    back, part, across = (back0, back1), (part0, part1), (across0, across1)
    zs, zb = (zs0, zs1), (zb0, zb1)
    wides = (D, WIDE)
    order = (1, 2, 3, 0)
    greet_lines()

    def home(t, kk, d):
        w = ways[t]
        bs = step(w.b, kk)
        to = step(w.a, d)
        return remote(rows_in[t].at[w.block(to, bs)], back[t].at[bs, w.a],
                      sa.at[t, kk, d - 1], ra.at[t, kk, d - 1], w.dev(to, w.b, w.x))

    def stay(t, kk):
        w = ways[t]
        bs = step(w.b, kk)
        return pltpu.make_async_copy(rows_in[t].at[w.block(w.a, bs)], back[t].at[bs, w.a],
                                     la.at[t, kk])

    def cross(t, n, kk, d):
        w = ways[t]
        bs = step(w.b, kk)
        to = step(w.x, d)
        return remote(part[t].at[n % 2, to], across[t].at[bs, w.x],
                      sb.at[t, kk, d - 1], rb.at[t, kk, d - 1], w.dev(w.a, w.b, to))

    def last(t, kk):
        w = ways[t]
        return remote(zs[t].at[kk - 1], zb[t].at[kk - 1], sc.at[t, kk - 1], rc.at[t, kk - 1],
                      w.dev(w.a, step(w.b, kk), w.x))

    for kk in order:
        for t in (0, 1):
            for d in (1, 2, 3):
                home(t, kk, d).start()
            stay(t, kk).start()

    def gather_x(t, kk):
        w = ways[t]
        bs = step(w.b, kk)
        for d in (1, 2, 3):
            cross(t, 0, kk, d).wait_recv()
        if kk == 0:
            return

        def total(c, _):
            cols = pl.ds(pl.multiple_of(c * 128, 128), 128)
            four = across[t][bs, :, :, cols].astype(jnp.float32)
            zs[t][kk - 1, :, cols] = jnp.sum(four, axis=0).astype(jnp.bfloat16)
            return 0

        lax.fori_loop(0, wides[t] // 128, total, 0)
        last(t, kk).start()

    for n, kk in enumerate(order):
        for t in (0, 1):
            w = ways[t]
            bs = step(w.b, kk)
            tables = tab_ref[t, bs]
            for a in range(SIDE):
                hit = hits_of(tables, a)
                weight = jnp.concatenate(lane_rows(tables, 1, a), axis=1) if t == 0 else 1.0
                pick[a * GROUP : (a + 1) * GROUP, :] = jnp.where(hit, weight, 0.0).astype(
                    jnp.bfloat16
                )
            for d in (1, 2, 3):
                home(t, kk, d).wait_recv()
            stay(t, kk).wait()
            if n >= 2:
                for d in (1, 2, 3):
                    cross(t, n - 2, order[n - 2], d).wait_send()

            def dense(c, _, t=t, bs=bs, n=n):
                cols = pl.ds(pl.multiple_of(c * 128, 128), 128)
                rows = back[t][bs, :, :, cols].reshape(SIDE * GROUP, 128)
                sums = contract_rows(pick[...], rows).astype(jnp.bfloat16)
                part[t][n % 2, :, :, cols] = sums.reshape(SIDE, TOK, 128)
                return 0

            lax.fori_loop(0, wides[t] // 128, dense, 0)
            for d in (1, 2, 3):
                cross(t, n, kk, d).start()
            across[t][bs, w.x] = part[t][n % 2, w.x]
        if n >= 1:
            for t in (0, 1):
                gather_x(t, order[n - 1])
    for t in (0, 1):
        gather_x(t, 0)
        for kk in (1, 2, 3):
            last(t, kk).wait_recv()
        w = ways[t]

        def finish(c, _, t=t, w=w):
            cols = pl.ds(pl.multiple_of(c * 128, 128), 128)
            four = jnp.sum(across[t][w.b, :, :, cols].astype(jnp.float32), axis=0)
            rest = jnp.sum(zb[t][:, :, cols].astype(jnp.float32), axis=0)
            (mixed_ref, gtok_ref)[t][:, cols] = (four + rest).astype(jnp.bfloat16)
            return 0

        lax.fori_loop(0, D // 128, finish, 0)
        if t == 1:
            marks = jnp.sum(across[1][w.b, :, :, D:].astype(jnp.float32), axis=0)
            mark_ref[...] = marks + jnp.sum(zb[1][:, :, D:].astype(jnp.float32), axis=0)
    for t in (0, 1):
        for n, kk in enumerate(order):
            for d in (1, 2, 3):
                home(t, kk, d).wait_send()
                if n >= 2:
                    cross(t, n, kk, d).wait_send()
            if kk > 0:
                last(t, kk).wait_send()


def bring_back(out_rows, grad_rows, tables):
    dma = pltpu.SemaphoreType.DMA
    vmem = pl.BlockSpec(memory_space=pltpu.VMEM)
    hbm = pl.BlockSpec(memory_space=pl.ANY)
    both = lambda lead: [pltpu.VMEM(lead + (w,), jnp.bfloat16) for w in (D, WIDE)]
    return pl.pallas_call(
        return_kernel,
        name="bring_back",
        out_shape=(
            jax.ShapeDtypeStruct((TOK, D), jnp.bfloat16),
            jax.ShapeDtypeStruct((TOK, D), jnp.bfloat16),
            jax.ShapeDtypeStruct((TOK, 128), jnp.float32),
        ),
        in_specs=[hbm, hbm, vmem],
        out_specs=(vmem, vmem, vmem),
        scratch_shapes=both((SIDE, SIDE, GROUP)) + both((2, SIDE, TOK)) + both((SIDE, SIDE, TOK))
        + both((3, TOK)) + both((3, TOK)) + [
            pltpu.VMEM((SIDE * GROUP, SIDE * TOK), jnp.bfloat16),
            dma((2, SIDE, 3)), dma((2, SIDE, 3)),
            dma((2, SIDE, 3)), dma((2, SIDE, 3)),
            dma((2, 3)), dma((2, 3)),
            dma((2, SIDE)),
        ],
        compiler_params=pltpu.CompilerParams(
            collective_id=3, has_side_effects=True, vmem_limit_bytes=VMEM_LIMIT
        ),
    )(out_rows, grad_rows, tables)


def body(tokens, route_ids, route_probs, cotangent, w_gate, w_up, w_down):
    x_rows, g_rows, tables = dispatch(route_ids.T, route_probs.T, tokens, cotangent)
    x_rows, g_rows = x_rows.reshape(ROWS, D), g_rows.reshape(ROWS, D)
    out_rows, grad_rows, hidden, gate_grad, up_grad = expert_rows(
        x_rows, g_rows, w_gate[0], w_up[0], w_down[0]
    )
    mixed, grad_tokens, marks = bring_back(
        out_rows.reshape(16, GROUP, D), grad_rows.reshape(16, GROUP, WIDE), tables
    )
    grad_gate, grad_up, grad_down = weight_grads(x_rows, g_rows, hidden, gate_grad, up_grad)
    product = marks[:, :EXPERTS] + marks[:, EXPERTS:]
    chosen = route_ids[:, :, None] == jnp.arange(EXPERTS, dtype=jnp.int32)[None, None, :]
    grad_probs = jnp.sum(jnp.where(chosen, product[:, None, :], 0.0), axis=2) / route_probs
    return (mixed, grad_tokens, grad_probs, grad_gate, grad_up, grad_down)


def solution(mesh):
    both = P(("dp", "expert"), None)
    mine = P("expert", None, None)
    split = P("expert", None, "dp")
    return jax.shard_map(
        body,
        mesh=mesh,
        in_specs=(both, both, both, both, mine, mine, mine),
        out_specs=(both, both, both, split, split, split),
        check_vma=False,
    )
```

```python
import functools

import jax
import jax.numpy as jnp
from jax import lax
from jax.experimental import pallas as pl
from jax.experimental.pallas import tpu as pltpu
from jax.sharding import PartitionSpec as P

D = 2048
FF = 768
TOP = 8
TOK = 128
CAP = 28
SIDE = 4
EXPERTS = 64
GROUP = SIDE * CAP
ROWS = 16 * GROUP
WIDE = D + 128
LATE = 1536
PIECES = ((0, 768), (768, 768), (1536, 512))
RINGS = 24
MESH = pl.DeviceIdType.MESH
VMEM_LIMIT = 60 * 1024 * 1024


def where_am_i():
    e = lax.axis_index("expert")
    return lax.axis_index("dp"), e // 16, (e // 4) % 4, e % 4


class Way:
    def __init__(self, t):
        self.t = t
        self.dp, z, self.x, y = where_am_i()
        self.a, self.b = (y, z) if t == 0 else (z, y)

    def dev(self, a, b, x):
        z, y = (b, a) if self.t == 0 else (a, b)
        return (self.dp, z * 16 + x * 4 + y)

    def block(self, a, b):
        return a * 4 + b if self.t == 0 else b * 4 + a


def step(v, d):
    return lax.rem(v + d + SIDE, SIDE)


def greet_lines():
    dp, z, x, y = where_am_i()
    barrier = pltpu.get_barrier_semaphore()
    for d in (1, 2, 3):
        for to in (
            step(z, d) * 16 + x * 4 + y,
            z * 16 + step(x, d) * 4 + y,
            z * 16 + x * 4 + step(y, d),
        ):
            pl.semaphore_signal(barrier, inc=1, device_id=(dp, to), device_id_type=MESH)
    pl.semaphore_wait(barrier, 9)


def remote(src, dst, send, recv, dev):
    return pltpu.make_async_remote_copy(
        src_ref=src, dst_ref=dst, send_sem=send, recv_sem=recv, device_id=dev, device_id_type=MESH
    )


def own_table(t, ids_ref, probs_ref):
    row = lax.broadcasted_iota(jnp.int32, (TOK, TOK), 0)
    b, x, kind, a = row // 32, (row // 8) % 4, (row // 4) % 2, row % 4
    expert = b * 16 + x * 4 + a if t == 0 else a * 16 + x * 4 + b
    hit = jnp.zeros((TOK, TOK), jnp.float32)
    weight = jnp.zeros((TOK, TOK), jnp.float32)
    for k in range(TOP):
        same = expert == ids_ref[k : k + 1, :]
        hit = jnp.where(same, 1.0, hit)
        weight = jnp.where(same, probs_ref[k : k + 1, :], weight)
    before = lax.broadcasted_iota(jnp.int32, (TOK, TOK), 0) < lax.broadcasted_iota(
        jnp.int32, (TOK, TOK), 1
    )
    before = jnp.where(before, 1.0, 0.0).astype(jnp.bfloat16)
    slot = jnp.dot(hit.astype(jnp.bfloat16), before, preferred_element_type=jnp.float32)
    slot = jnp.where(hit > 0.5, slot, -1000.0)
    return jnp.where(kind == 0, slot, weight)


def lane_rows(tables, kind, a):
    return [tables[xs, kind * 4 + a : kind * 4 + a + 1, :] for xs in range(SIDE)]


def hits_of(tables, a):
    slots = jnp.concatenate(
        [v + float(CAP * xs) for xs, v in enumerate(lane_rows(tables, 0, a))], axis=1
    )
    row = lax.broadcasted_iota(jnp.int32, (GROUP, SIDE * TOK), 0).astype(jnp.float32)
    return row == slots


class Gather:
    def __init__(self, n, sems, me, dev, block, half):
        self.send, self.recv = sems
        self.n, self.me, self.dev, self.block, self.half = n, me, dev, block, half

    def copy(self, ref, at, s):
        return remote(ref, ref, self.send.at[self.n, at], self.recv.at[self.n, at],
                      self.dev(step(self.me, s)))

    def near(self, s):
        return self.copy(self.block(self.me), 0 if s > 0 else 1, s)

    def far(self, s):
        return self.copy(self.half(step(self.me, -s), 0 if s > 0 else 1), 2 if s > 0 else 3, s)

    def start(self):
        for s in (1, -1):
            self.near(s).start()

    def pass_on(self):
        for s in (1, -1):
            self.near(s).wait_recv()
            self.far(s).start()

    def finish(self):
        for s in (1, -1):
            self.far(s).wait_recv()

    def drain(self):
        for s in (1, -1):
            self.near(s).wait_send()
            self.far(s).wait_send()


def column_tiles(start, width, tile):
    def one(c, _):
        tile(pl.ds(pl.multiple_of(start + c * 256, 128), 256))
        return 0

    lax.fori_loop(0, width // 256, one, 0)
    if width % 256:
        tile(pl.ds(start + width // 256 * 256, width % 256))


def dispatch_kernel(
    ids_ref, probs_ref, tok_ref, cot_ref, x_rows, g_rows, tab_out,
    gath, stage, own_tab, tab_a, tab_b, pick, scale,
    gs, gr, s3, r3, ts1, tr1, ts2, tr2, ls,
):
    ways = (Way(0), Way(1))
    rows_out = (x_rows, g_rows)
    sems = (gs, gr)

    for t, src in ((0, tok_ref), (1, cot_ref)):
        w = ways[t]
        own_tab[t] = own_table(t, ids_ref, probs_ref).reshape(16, 8, TOK)
        gath[t, w.b, w.x] = src[...]
        tab_a[t, w.b] = own_tab[t, pl.ds(w.b * 4, 4)]
    greet_lines()

    count = iter(range(RINGS))

    def along_b(t, piece):
        w, cols = ways[t], pl.ds(*PIECES[piece])
        return Gather(next(count), sems, w.b, lambda i: w.dev(w.a, i, w.x),
                      lambda i: gath.at[t, i, w.x, :, cols],
                      lambda i, u: gath.at[t, i, w.x, pl.ds(u * 64, 64), cols])

    def along_x(t, kk, piece):
        w, cols = ways[t], pl.ds(*PIECES[piece])
        bs = step(w.b, -kk)
        return Gather(next(count), sems, w.x, lambda i: w.dev(w.a, w.b, i),
                      lambda i: gath.at[t, bs, i, :, cols],
                      lambda i, u: gath.at[t, bs, i, pl.ds(u * 64, 64), cols])

    def lines_b(t):
        w, cols = ways[t], pl.ds(*PIECES[2])
        return Gather(next(count), sems, w.b, lambda i: w.dev(w.a, i, w.x),
                      lambda i: gath.at[t, i, :, :, cols],
                      lambda i, u: gath.at[t, i, pl.ds(u * 2, 2), :, cols])

    both = (0, 1)
    b_first = [[along_b(t, h) for h in both] for t in both]
    x_then = [{(kk, h): along_x(t, kk, h) for kk in range(SIDE) for h in both} for t in both]
    x_first = [along_x(t, 0, 2) for t in both]
    b_then = [lines_b(t) for t in both]

    def first_tab(t, d):
        w = ways[t]
        to = step(w.b, d)
        return remote(own_tab.at[t, pl.ds(to * 4, 4)], tab_a.at[t, w.b],
                      ts1.at[t, d - 1], tr1.at[t, d - 1], w.dev(w.a, to, w.x))

    def second_tab(t, kk, d):
        w = ways[t]
        bs = step(w.b, -kk)
        to = step(w.x, d)
        return remote(tab_a.at[t, bs, to], tab_b.at[t, bs, w.x],
                      ts2.at[t, kk, d - 1], tr2.at[t, kk, d - 1], w.dev(w.a, w.b, to))

    def third(t, kk, piece, d):
        w = ways[t]
        bs = step(w.b, -kk)
        to = step(w.a, d)
        cols = pl.ds(*PIECES[piece])
        return remote(stage.at[t, kk, to, :, cols],
                      rows_out[t].at[w.block(w.a, bs), :, cols],
                      s3.at[t, kk, piece, d - 1], r3.at[t, kk, piece, d - 1],
                      w.dev(to, w.b, w.x))

    def kept(t, kk, piece):
        w = ways[t]
        bs = step(w.b, -kk)
        cols = pl.ds(*PIECES[piece])
        return pltpu.make_async_copy(stage.at[t, kk, w.a, :, cols],
                                     rows_out[t].at[w.block(w.a, bs), :, cols],
                                     ls.at[t, kk, piece])

    def share_tab(t, kk):
        w = ways[t]
        bs = step(w.b, -kk)
        if kk > 0:
            first_tab(t, kk).wait_recv()
        tab_b[t, bs, w.x] = tab_a[t, bs, w.x]
        for d in (1, 2, 3):
            second_tab(t, kk, d).start()

    def make_pick(t, kk):
        for d in (1, 2, 3):
            second_tab(t, kk, d).wait_recv()
        tables = tab_b[t, step(ways[t].b, -kk)]
        for a in range(SIDE):
            at = slice(a * GROUP, (a + 1) * GROUP)
            hit = hits_of(tables, a)
            pick[t, at, :] = jnp.where(hit, 1.0, 0.0).astype(jnp.bfloat16)
            if t == 1:
                weight = jnp.concatenate(lane_rows(tables, 1, a), axis=1)
                weight = jnp.sum(jnp.where(hit, weight, 0.0), axis=1, keepdims=True)
                scale[at, :] = jnp.broadcast_to(weight, (GROUP, 128))

    def send_rows(t, kk, piece):
        bs = step(ways[t].b, -kk)

        def tile(cols):
            block = gath[t, bs, :, :, cols].reshape(SIDE * TOK, cols.size)
            rows = jnp.dot(pick[t], block, preferred_element_type=jnp.float32)
            if t == 1:
                rows = rows * jnp.concatenate([scale[...]] * (cols.size // 128), axis=1)
            stage[t, kk, :, :, cols] = rows.astype(jnp.bfloat16).reshape(SIDE, GROUP, cols.size)

        column_tiles(*PIECES[piece], tile)
        for d in (1, 2, 3):
            third(t, kk, piece, d).start()
        kept(t, kk, piece).start()

    for t in both:
        for d in (1, 2, 3):
            first_tab(t, d).start()
        share_tab(t, 0)
        x_first[t].start()
    for h in both:
        for t in both:
            x_then[t][0, h].start()
        for t in both:
            b_first[t][h].start()
    for t in both:
        x_first[t].pass_on()
    for t in both:
        x_then[t][0, 0].pass_on()
    for t in both:
        b_first[t][0].pass_on()
    for t in both:
        x_first[t].finish()
        b_then[t].start()
    for t in both:
        b_first[t][1].pass_on()

    turns = [(kk, h) for kk in (0, 1, 3, 2) for h in both]
    for n, (kk, h) in enumerate(turns):
        if n + 2 < len(turns):
            k2, h2 = turns[n + 2]
            for t in both:
                if k2 == 2:
                    b_first[t][h2].finish()
                if h2 == 0:
                    share_tab(t, k2)
                x_then[t][k2, h2].start()
        if n + 1 < len(turns):
            for t in both:
                x_then[t][turns[n + 1]].pass_on()
        for t in both:
            x_then[t][kk, h].finish()
            if h == 0:
                make_pick(t, kk)
            send_rows(t, kk, h)
        if h == 1:
            for t in both:
                if kk == 1:
                    b_then[t].pass_on()
                if kk == 2:
                    b_then[t].finish()
                send_rows(t, kk, 2)

    tab_out[...] = tab_b[...]
    for t in both:
        for kk in range(SIDE):
            for d in (1, 2, 3):
                second_tab(t, kk, d).wait_send()
                for piece in range(3):
                    third(t, kk, piece, d).wait()
            for piece in range(3):
                kept(t, kk, piece).wait()
        for d in (1, 2, 3):
            first_tab(t, d).wait_send()
        for ring in (*b_first[t], *x_then[t].values(), x_first[t], b_then[t]):
            ring.drain()


def dispatch(ids_t, probs_t, tokens, cotangent):
    dma = pltpu.SemaphoreType.DMA
    vmem = pl.BlockSpec(memory_space=pltpu.VMEM)
    hbm = pl.BlockSpec(memory_space=pl.ANY)
    return pl.pallas_call(
        dispatch_kernel,
        name="dispatch",
        out_shape=(
            jax.ShapeDtypeStruct((16, GROUP, D), jnp.bfloat16),
            jax.ShapeDtypeStruct((16, GROUP, D), jnp.bfloat16),
            jax.ShapeDtypeStruct((2, SIDE, SIDE, 8, TOK), jnp.float32),
        ),
        in_specs=[vmem] * 4,
        out_specs=(hbm, hbm, vmem),
        scratch_shapes=[
            pltpu.VMEM((2, SIDE, SIDE, TOK, D), jnp.bfloat16),
            pltpu.VMEM((2, SIDE, SIDE, GROUP, D), jnp.bfloat16),
            pltpu.VMEM((2, 16, 8, TOK), jnp.float32),
            pltpu.VMEM((2, SIDE, SIDE, 8, TOK), jnp.float32),
            pltpu.VMEM((2, SIDE, SIDE, 8, TOK), jnp.float32),
            pltpu.VMEM((2, SIDE * GROUP, SIDE * TOK), jnp.bfloat16),
            pltpu.VMEM((SIDE * GROUP, 128), jnp.float32),
            dma((RINGS, 4)), dma((RINGS, 4)),
            dma((2, SIDE, 3, 3)), dma((2, SIDE, 3, 3)),
            dma((2, 3)), dma((2, 3)),
            dma((2, SIDE, 3)), dma((2, SIDE, 3)),
            dma((2, SIDE, 3)),
        ],
        compiler_params=pltpu.CompilerParams(
            collective_id=1, has_side_effects=True, vmem_limit_bytes=VMEM_LIMIT
        ),
    )(ids_t, probs_t, tokens, cotangent)


def contract_last(left_side, right_side):
    return lax.dot_general(
        left_side, right_side, (((1,), (1,)), ((), ())), preferred_element_type=jnp.float32
    )


def contract_rows(left_side, right_side):
    return lax.dot_general(
        left_side, right_side, (((0,), (0,)), ((), ())), preferred_element_type=jnp.float32
    )


def expert_kernel(x_ref, g_ref, wg_ref, wu_ref, wd_ref, out_ref, grad_ref, hid_ref, gg_ref, gu_ref):
    rows = x_ref[...]
    gate_pre = jnp.dot(rows, wg_ref[...], preferred_element_type=jnp.float32)
    up_pre = jnp.dot(rows, wu_ref[...], preferred_element_type=jnp.float32)
    sigmoid = jax.nn.sigmoid(gate_pre)
    activation = gate_pre * sigmoid
    derivative = sigmoid * (1.0 + gate_pre * (1.0 - sigmoid))
    hidden = (activation * up_pre).astype(jnp.bfloat16)
    hid_ref[...] = hidden
    out_ref[...] = jnp.dot(hidden, wd_ref[...], preferred_element_type=jnp.float32).astype(
        jnp.bfloat16
    )
    grad_hidden = contract_last(g_ref[...], wd_ref[...])
    gate_grad = (grad_hidden * up_pre * derivative).astype(jnp.bfloat16)
    up_grad = (grad_hidden * activation).astype(jnp.bfloat16)
    gg_ref[...] = gate_grad
    gu_ref[...] = up_grad
    grad_ref[:, :D] = (
        contract_last(gate_grad, wg_ref[...]) + contract_last(up_grad, wu_ref[...])
    ).astype(jnp.bfloat16)
    product = jnp.sum(hidden.astype(jnp.float32) * grad_hidden, axis=1, keepdims=True)
    high = product.astype(jnp.bfloat16)
    low = (product - high.astype(jnp.float32)).astype(jnp.bfloat16)
    lane = lax.broadcasted_iota(jnp.int32, (rows.shape[0], 128), 1)
    me = lax.axis_index("expert")
    marks = jnp.where(lane == me, high.astype(jnp.float32), 0.0)
    marks = jnp.where(lane == me + EXPERTS, low.astype(jnp.float32), marks)
    grad_ref[:, D:] = marks.astype(jnp.bfloat16)


def expert_rows(x_rows, g_rows, w_gate, w_up, w_down):
    bm = 256
    whole = lambda shape: pl.BlockSpec(shape, lambda i: (0, 0), pipeline_mode=pl.Buffered(1))
    part = lambda width: pl.BlockSpec((bm, width), lambda i: (i, 0))
    bf = lambda width: jax.ShapeDtypeStruct((ROWS, width), jnp.bfloat16)
    return pl.pallas_call(
        expert_kernel,
        name="expert_rows",
        grid=(ROWS // bm,),
        out_shape=(bf(D), bf(WIDE), bf(FF), bf(FF), bf(FF)),
        in_specs=[part(D), part(D), whole((D, FF)), whole((D, FF)), whole((FF, D))],
        out_specs=(part(D), part(WIDE), part(FF), part(FF), part(FF)),
        compiler_params=pltpu.CompilerParams(vmem_limit_bytes=VMEM_LIMIT),
        cost_estimate=pl.CostEstimate(
            flops=12 * ROWS * D * FF, bytes_accessed=40_000_000, transcendentals=ROWS * FF
        ),
    )(x_rows, g_rows, w_gate, w_up, w_down)


def weight_kernel(x_ref, g_ref, hid_ref, gg_ref, gu_ref, dg_ref, du_ref, dd_ref,
                  out_g, out_u, out_d, in_g, in_u, in_d, send, recv):
    dp = lax.axis_index("dp")
    e = lax.axis_index("expert")
    other = 1 - dp
    barrier = pltpu.get_barrier_semaphore()
    pl.semaphore_signal(barrier, inc=1, device_id=(other, e), device_id_type=MESH)
    pl.semaphore_wait(barrier, 1)
    jobs = (
        (x_ref, gg_ref, dg_ref, out_g, in_g),
        (x_ref, gu_ref, du_ref, out_u, in_u),
        (hid_ref, g_ref, dd_ref, out_d, in_d),
    )
    copies = []
    for n, (left, right, done, away, back) in enumerate(jobs):
        height = 256
        wide = right.shape[1] // 2

        def send_part(i, _, left=left, right=right, away=away, wide=wide):
            at = pl.ds(pl.multiple_of(i * height, height), height)
            cols = pl.ds(pl.multiple_of(other * wide, wide), wide)
            away[at, :] = contract_rows(left[:, at], right[:, cols]).astype(jnp.bfloat16)
            return 0

        lax.fori_loop(0, left.shape[1] // height, send_part, 0)
        copy = remote(away, back, send.at[n], recv.at[n], (other, e))
        copy.start()
        copies.append(copy)
    for n, (left, right, done, away, back) in enumerate(jobs):
        height = 256
        wide = right.shape[1] // 2
        copies[n].wait()

        def keep_part(i, _, left=left, right=right, back=back, done=done, wide=wide):
            at = pl.ds(pl.multiple_of(i * height, height), height)
            cols = pl.ds(pl.multiple_of(dp * wide, wide), wide)
            mine = contract_rows(left[:, at], right[:, cols])
            done[0, at, :] = (mine + back[at, :].astype(jnp.float32)).astype(jnp.bfloat16)
            return 0

        lax.fori_loop(0, left.shape[1] // height, keep_part, 0)


def weight_grads(x_rows, g_rows, hidden, gate_grad, up_grad):
    vmem = pl.BlockSpec(memory_space=pltpu.VMEM)
    halves = ((D, FF // 2), (D, FF // 2), (FF, D // 2))
    dma = pltpu.SemaphoreType.DMA
    return pl.pallas_call(
        weight_kernel,
        name="weight_grads",
        out_shape=tuple(jax.ShapeDtypeStruct((1,) + s, jnp.bfloat16) for s in halves),
        in_specs=[vmem] * 5,
        out_specs=(vmem,) * 3,
        scratch_shapes=[pltpu.VMEM(s, jnp.bfloat16) for s in halves + halves] + [dma((3,)), dma((3,))],
        compiler_params=pltpu.CompilerParams(
            collective_id=2, has_side_effects=True, vmem_limit_bytes=VMEM_LIMIT
        ),
    )(x_rows, g_rows, hidden, gate_grad, up_grad)


class Scatter:
    def __init__(self, n, sems, me, dev, part, half, near_at, far_at, add):
        self.send, self.recv = sems
        self.n, self.me, self.dev, self.add = n, me, dev, add
        self.part, self.half, self.near_at, self.far_at = part, half, near_at, far_at

    def copy(self, src, dst, at, s):
        return remote(src, dst, self.send.at[self.n, at], self.recv.at[self.n, at],
                      self.dev(step(self.me, s)))

    def near(self, s):
        u = 0 if s > 0 else 1
        return self.copy(self.part(s), self.near_at(u), u, s)

    def far(self, s):
        u = 0 if s > 0 else 1
        return self.copy(self.half(2, u), self.far_at(u), 2 + u, s)

    def first(self):
        for s in (1, -1):
            self.far(s).start()

    def second(self, s):
        u = 0 if s > 0 else 1
        self.far(s).wait_recv()
        self.add(self.half(s, u), self.far_at(u))
        self.near(s).start()

    def third(self):
        for s in (1, -1):
            self.near(s).wait_recv()

    def drain(self):
        for s in (1, -1):
            self.near(s).wait_send()
            self.far(s).wait_send()


def add_flat(to, more):
    width = to.shape[-1]

    def tile(cols):
        total = to[:, cols].astype(jnp.float32) + more[:, cols].astype(jnp.float32)
        to[:, cols] = total.astype(jnp.bfloat16)

    column_tiles(0, width, tile)


def add_lines(to, more):
    for i in range(2):
        add_flat(to.at[i], more.at[i])


def return_kernel(
    out_rows, grad_rows, tab_ref, mixed_ref, gtok_ref, mark_ref,
    back0, back1, pick, lpart, lnear, lfar, zpart, znear, zfar,
    fpart0, fpart1, fnear0, fnear1, ffar0, ffar1, fsum0, fsum1, xnear0, xnear1, xfar0, xfar1,
    gs, gr, sa, ra, la,
):
    ways = (Way(0), Way(1))
    rows_in = (out_rows, grad_rows)
    back, fpart, fnear, ffar = (back0, back1), (fpart0, fpart1), (fnear0, fnear1), (ffar0, ffar1)
    fsum, xnear, xfar = (fsum0, fsum1), (xnear0, xnear1), (xfar0, xfar1)
    tails = (D - LATE, WIDE - LATE)
    sems = (gs, gr)
    both = (0, 1)
    order = (2, 1, 3, 0)
    greet_lines()

    def piece_cols(t, piece):
        return pl.ds(*PIECES[piece]) if piece < 2 else pl.ds(LATE, tails[t])

    def home(t, kk, piece, d):
        w = ways[t]
        bs = step(w.b, kk)
        to = step(w.a, d)
        cols = piece_cols(t, piece)
        return remote(rows_in[t].at[w.block(to, bs), :, cols], back[t].at[bs, w.a, :, cols],
                      sa.at[t, kk, piece, d - 1], ra.at[t, kk, piece, d - 1],
                      w.dev(to, w.b, w.x))

    def stay(t, kk):
        w = ways[t]
        bs = step(w.b, kk)
        return pltpu.make_async_copy(rows_in[t].at[w.block(w.a, bs)], back[t].at[bs, w.a],
                                     la.at[t, kk])

    for kk in order:
        for t in both:
            stay(t, kk).start()
        for piece in range(3):
            for t in both:
                for d in (1, 2, 3):
                    home(t, kk, piece, d).start()

    count = iter(range(RINGS))

    def along_x(t, n, kk, h):
        w, cols = ways[t], pl.ds(*PIECES[h])
        at = n % 2
        return Scatter(next(count), sems, w.x, lambda i: w.dev(w.a, w.b, i),
                       lambda o: lpart.at[t, at, step(w.x, o), :, cols],
                       lambda o, u: lpart.at[t, at, step(w.x, o), pl.ds(u * 64, 64), cols],
                       lambda u: lnear.at[t, kk, u, :, cols],
                       lambda u: lfar.at[t, kk, u, :, cols], add_flat)

    def along_b(t):
        w = ways[t]
        return Scatter(next(count), sems, w.b, lambda i: w.dev(w.a, i, w.x),
                       lambda o: zpart.at[t, o % 4],
                       lambda o, u: zpart.at[t, o % 4, pl.ds(u * 64, 64)],
                       lambda u: znear.at[t, u], lambda u: zfar.at[t, u], add_flat)

    def lines_b(t):
        w = ways[t]
        return Scatter(next(count), sems, w.b, lambda i: w.dev(w.a, i, w.x),
                       lambda o: fpart[t].at[o % 4],
                       lambda o, u: fpart[t].at[o % 4, pl.ds(u * 2, 2)],
                       lambda u: fnear[t].at[u], lambda u: ffar[t].at[u], add_lines)

    def late_x(t):
        w = ways[t]
        return Scatter(next(count), sems, w.x, lambda i: w.dev(w.a, w.b, i),
                       lambda o: fsum[t].at[step(w.x, o)],
                       lambda o, u: fsum[t].at[step(w.x, o), pl.ds(u * 64, 64)],
                       lambda u: xnear[t].at[u], lambda u: xfar[t].at[u], add_flat)

    x_first = [{(kk, h): along_x(t, n, kk, h) for n, kk in enumerate(order) for h in both}
               for t in both]
    b_then = [along_b(t) for t in both]
    b_first = [lines_b(t) for t in both]
    x_then = [late_x(t) for t in both]

    def make_pick(t, kk):
        tables = tab_ref[t, step(ways[t].b, kk)]
        for a in range(SIDE):
            hit = hits_of(tables, a)
            weight = jnp.concatenate(lane_rows(tables, 1, a), axis=1) if t == 0 else 1.0
            pick[a * GROUP : (a + 1) * GROUP, :] = jnp.where(hit, weight, 0.0).astype(jnp.bfloat16)

    def sum_experts(t, n, kk, piece):
        bs = step(ways[t].b, kk)
        for d in (1, 2, 3):
            home(t, kk, piece, d).wait_recv()

        def tile(cols):
            rows = back[t][bs, :, :, cols].reshape(SIDE * GROUP, cols.size)
            sums = contract_rows(pick[...], rows).astype(jnp.bfloat16)
            sums = sums.reshape(SIDE, TOK, cols.size)
            if piece < 2:
                lpart[t, n % 2, :, :, cols] = sums
            else:
                fpart[t][kk, :, :, pl.ds(cols.start - LATE, cols.size)] = sums

        start, width = PIECES[piece] if piece < 2 else (LATE, tails[t])
        column_tiles(start, width, tile)

    def collect_x(t, n, kk):
        w = ways[t]
        for h in both:
            x_first[t][kk, h].third()

        def tile(cols):
            total = lpart[t, n % 2, w.x, :, cols].astype(jnp.float32)
            total = total + jnp.sum(lnear[t, kk, :, :, cols].astype(jnp.float32), axis=0)
            zpart[t, kk, :, cols] = total.astype(jnp.bfloat16)

        column_tiles(0, LATE, tile)
        if kk == 2:
            b_then[t].first()
        if kk in (1, 3):
            b_then[t].second(1 if kk == 1 else -1)

    for n, kk in enumerate(order):
        for t in both:
            stay(t, kk).wait()
            make_pick(t, kk)
            if n >= 2:
                for h in both:
                    x_first[t][order[n - 2], h].drain()
            for h in both:
                sum_experts(t, n, kk, h)
                x_first[t][kk, h].first()
            sum_experts(t, n, kk, 2)
            if kk == 2:
                b_first[t].first()
            if kk in (1, 3):
                b_first[t].second(1 if kk == 1 else -1)
        for t in both:
            for h in both:
                x_first[t][kk, h].second(1)
                x_first[t][kk, h].second(-1)
        if n >= 1:
            for t in both:
                collect_x(t, n - 1, order[n - 1])

    for t in both:
        b_first[t].third()
        for i in range(SIDE):

            def tile(cols, t=t, i=i):
                total = fpart[t][0, i, :, cols].astype(jnp.float32)
                total = total + jnp.sum(fnear[t][:, i, :, cols].astype(jnp.float32), axis=0)
                fsum[t][i, :, cols] = total.astype(jnp.bfloat16)

            column_tiles(0, tails[t], tile)
        x_then[t].first()
    for t in both:
        x_then[t].second(1)
        x_then[t].second(-1)
    results = (mixed_ref, gtok_ref)
    for t in both:
        collect_x(t, 3, 0)
        b_then[t].third()

        def tile(cols, t=t):
            total = zpart[t, 0, :, cols].astype(jnp.float32)
            total = total + jnp.sum(znear[t, :, :, cols].astype(jnp.float32), axis=0)
            results[t][:, cols] = total.astype(jnp.bfloat16)

        column_tiles(0, LATE, tile)
    for t in both:
        w = ways[t]
        x_then[t].third()

        def late(cols, t=t, w=w):
            total = fsum[t][w.x, :, cols].astype(jnp.float32)
            return total + jnp.sum(xnear[t][:, :, cols].astype(jnp.float32), axis=0)

        def tile(cols, t=t, late=late):
            results[t][:, pl.ds(cols.start + LATE, cols.size)] = late(cols).astype(jnp.bfloat16)

        column_tiles(0, D - LATE, tile)
        if t == 1:
            mark_ref[...] = late(pl.ds(D - LATE, 128))

    for t in both:
        for n, kk in enumerate(order):
            for piece in range(3):
                for d in (1, 2, 3):
                    home(t, kk, piece, d).wait_send()
            if n >= 2:
                for h in both:
                    x_first[t][kk, h].drain()
        b_then[t].drain()
        b_first[t].drain()
        x_then[t].drain()


def bring_back(out_rows, grad_rows, tables):
    dma = pltpu.SemaphoreType.DMA
    vmem = pl.BlockSpec(memory_space=pltpu.VMEM)
    hbm = pl.BlockSpec(memory_space=pl.ANY)
    buf = lambda *shape: pltpu.VMEM(shape, jnp.bfloat16)
    pair = lambda *lead: [buf(*lead, D - LATE), buf(*lead, WIDE - LATE)]
    return pl.pallas_call(
        return_kernel,
        name="bring_back",
        out_shape=(
            jax.ShapeDtypeStruct((TOK, D), jnp.bfloat16),
            jax.ShapeDtypeStruct((TOK, D), jnp.bfloat16),
            jax.ShapeDtypeStruct((TOK, 128), jnp.float32),
        ),
        in_specs=[hbm, hbm, vmem],
        out_specs=(vmem, vmem, vmem),
        scratch_shapes=[
            buf(SIDE, SIDE, GROUP, D), buf(SIDE, SIDE, GROUP, WIDE),
            buf(SIDE * GROUP, SIDE * TOK),
            buf(2, 2, SIDE, TOK, LATE), buf(2, SIDE, 2, TOK, LATE), buf(2, SIDE, 2, TOK // 2, LATE),
            buf(2, SIDE, TOK, LATE), buf(2, 2, TOK, LATE), buf(2, 2, TOK // 2, LATE),
            *pair(SIDE, SIDE, TOK), *pair(2, SIDE, TOK), *pair(2, 2, TOK),
            *pair(SIDE, TOK), *pair(2, TOK), *pair(2, TOK // 2),
            dma((RINGS, 4)), dma((RINGS, 4)),
            dma((2, SIDE, 3, 3)), dma((2, SIDE, 3, 3)),
            dma((2, SIDE)),
        ],
        compiler_params=pltpu.CompilerParams(
            collective_id=3, has_side_effects=True, vmem_limit_bytes=VMEM_LIMIT
        ),
    )(out_rows, grad_rows, tables)


def body(tokens, route_ids, route_probs, cotangent, w_gate, w_up, w_down):
    x_rows, g_rows, tables = dispatch(route_ids.T, route_probs.T, tokens, cotangent)
    x_rows, g_rows = x_rows.reshape(ROWS, D), g_rows.reshape(ROWS, D)
    out_rows, grad_rows, hidden, gate_grad, up_grad = expert_rows(
        x_rows, g_rows, w_gate[0], w_up[0], w_down[0]
    )
    mixed, grad_tokens, marks = bring_back(
        out_rows.reshape(16, GROUP, D), grad_rows.reshape(16, GROUP, WIDE), tables
    )
    grad_gate, grad_up, grad_down = weight_grads(x_rows, g_rows, hidden, gate_grad, up_grad)
    product = marks[:, :EXPERTS] + marks[:, EXPERTS:]
    chosen = route_ids[:, :, None] == jnp.arange(EXPERTS, dtype=jnp.int32)[None, None, :]
    grad_probs = jnp.sum(jnp.where(chosen, product[:, None, :], 0.0), axis=2) / route_probs
    return (mixed, grad_tokens, grad_probs, grad_gate, grad_up, grad_down)


def solution(mesh):
    both = P(("dp", "expert"), None)
    mine = P("expert", None, None)
    split = P("expert", None, "dp")
    return jax.shard_map(
        body,
        mesh=mesh,
        in_specs=(both, both, both, both, mine, mine, mine),
        out_specs=(both, both, both, split, split, split),
        check_vma=False,
    )
```

```python
import functools

import jax
import jax.numpy as jnp
from jax import lax
from jax.experimental import pallas as pl
from jax.experimental.pallas import tpu as pltpu
from jax.sharding import PartitionSpec as P

D = 2048
FF = 768
TOP = 8
TOK = 128
CAP = 28
SIDE = 4
EXPERTS = 64
GROUP = SIDE * CAP
ROWS = 16 * GROUP
WIDE = D + 128
LATE = 1536
PIECES = ((0, 768), (768, 768), (1536, 512))
RINGS = 24
MESH = pl.DeviceIdType.MESH
VMEM_LIMIT = 63 * 1024 * 1024


def where_am_i():
    e = lax.axis_index("expert")
    return lax.axis_index("dp"), e // 16, (e // 4) % 4, e % 4


class Way:
    def __init__(self, t):
        self.t = t
        self.dp, z, self.x, y = where_am_i()
        self.a, self.b = (y, z) if t == 0 else (z, y)

    def dev(self, a, b, x):
        z, y = (b, a) if self.t == 0 else (a, b)
        return (self.dp, z * 16 + x * 4 + y)

    def block(self, a, b):
        return a * 4 + b if self.t == 0 else b * 4 + a


def step(v, d):
    return lax.rem(v + d + SIDE, SIDE)


def greet_lines():
    dp, z, x, y = where_am_i()
    barrier = pltpu.get_barrier_semaphore()
    for d in (1, 2, 3):
        for to in (
            step(z, d) * 16 + x * 4 + y,
            z * 16 + step(x, d) * 4 + y,
            z * 16 + x * 4 + step(y, d),
        ):
            pl.semaphore_signal(barrier, inc=1, device_id=(dp, to), device_id_type=MESH)
    pl.semaphore_signal(barrier, inc=1, device_id=(1 - dp, z * 16 + x * 4 + y), device_id_type=MESH)
    pl.semaphore_wait(barrier, 10)


def remote(src, dst, send, recv, dev):
    return pltpu.make_async_remote_copy(
        src_ref=src, dst_ref=dst, send_sem=send, recv_sem=recv, device_id=dev, device_id_type=MESH
    )


def own_table(t, ids_ref, probs_ref):
    row = lax.broadcasted_iota(jnp.int32, (TOK, TOK), 0)
    b, x, kind, a = row // 32, (row // 8) % 4, (row // 4) % 2, row % 4
    expert = b * 16 + x * 4 + a if t == 0 else a * 16 + x * 4 + b
    hit = jnp.zeros((TOK, TOK), jnp.float32)
    weight = jnp.zeros((TOK, TOK), jnp.float32)
    for k in range(TOP):
        same = expert == ids_ref[k : k + 1, :]
        hit = jnp.where(same, 1.0, hit)
        weight = jnp.where(same, probs_ref[k : k + 1, :], weight)
    before = lax.broadcasted_iota(jnp.int32, (TOK, TOK), 0) < lax.broadcasted_iota(
        jnp.int32, (TOK, TOK), 1
    )
    before = jnp.where(before, 1.0, 0.0).astype(jnp.bfloat16)
    slot = jnp.dot(hit.astype(jnp.bfloat16), before, preferred_element_type=jnp.float32)
    slot = jnp.where(hit > 0.5, slot, -1000.0)
    return jnp.where(kind == 0, slot, weight)


def lane_rows(tables, kind, a):
    return [tables[xs, kind * 4 + a : kind * 4 + a + 1, :] for xs in range(SIDE)]


def hits_of(tables, a):
    slots = jnp.concatenate(
        [v + float(CAP * xs) for xs, v in enumerate(lane_rows(tables, 0, a))], axis=1
    )
    row = lax.broadcasted_iota(jnp.int32, (GROUP, SIDE * TOK), 0).astype(jnp.float32)
    return row == slots


class Gather:
    def __init__(self, n, sems, me, dev, block, half):
        self.send, self.recv = sems
        self.n, self.me, self.dev, self.block, self.half = n, me, dev, block, half

    def copy(self, ref, at, s):
        return remote(ref, ref, self.send.at[self.n, at], self.recv.at[self.n, at],
                      self.dev(step(self.me, s)))

    def near(self, s):
        return self.copy(self.block(self.me), 0 if s > 0 else 1, s)

    def far(self, s):
        return self.copy(self.half(step(self.me, -s), 0 if s > 0 else 1), 2 if s > 0 else 3, s)

    def start(self):
        for s in (1, -1):
            self.near(s).start()

    def pass_on(self):
        for s in (1, -1):
            self.near(s).wait_recv()
            self.far(s).start()

    def finish(self):
        for s in (1, -1):
            self.far(s).wait_recv()

    def drain(self):
        for s in (1, -1):
            self.near(s).wait_send()
            self.far(s).wait_send()


def column_tiles(start, width, tile):
    def one(c, _):
        tile(pl.ds(pl.multiple_of(start + c * 256, 128), 256))
        return 0

    lax.fori_loop(0, width // 256, one, 0)
    if width % 256:
        tile(pl.ds(start + width // 256 * 256, width % 256))


def dispatch_kernel(
    ids_ref, probs_ref, tok_ref, cot_ref, x_rows, g_rows, tab_out,
    gath, stage, own_tab, tab_a, tab_b, pick, scale,
    gs, gr, s3, r3, ts1, tr1, ts2, tr2, ls,
):
    ways = (Way(0), Way(1))
    rows_out = (x_rows, g_rows)
    sems = (gs, gr)

    for t, src in ((0, tok_ref), (1, cot_ref)):
        w = ways[t]
        own_tab[t] = own_table(t, ids_ref, probs_ref).reshape(16, 8, TOK)
        gath[t, w.b, w.x] = src[...]
        tab_a[t, w.b] = own_tab[t, pl.ds(w.b * 4, 4)]
    greet_lines()

    count = iter(range(RINGS))

    def along_b(t, piece):
        w, cols = ways[t], pl.ds(*PIECES[piece])
        return Gather(next(count), sems, w.b, lambda i: w.dev(w.a, i, w.x),
                      lambda i: gath.at[t, i, w.x, :, cols],
                      lambda i, u: gath.at[t, i, w.x, pl.ds(u * 64, 64), cols])

    def along_x(t, kk, piece):
        w, cols = ways[t], pl.ds(*PIECES[piece])
        bs = step(w.b, -kk)
        return Gather(next(count), sems, w.x, lambda i: w.dev(w.a, w.b, i),
                      lambda i: gath.at[t, bs, i, :, cols],
                      lambda i, u: gath.at[t, bs, i, pl.ds(u * 64, 64), cols])

    def lines_b(t):
        w, cols = ways[t], pl.ds(*PIECES[2])
        return Gather(next(count), sems, w.b, lambda i: w.dev(w.a, i, w.x),
                      lambda i: gath.at[t, i, :, :, cols],
                      lambda i, u: gath.at[t, i, pl.ds(u * 2, 2), :, cols])

    both = (0, 1)
    b_first = [[along_b(t, h) for h in both] for t in both]
    x_then = [{(kk, h): along_x(t, kk, h) for kk in range(SIDE) for h in both} for t in both]
    x_first = [along_x(t, 0, 2) for t in both]
    b_then = [lines_b(t) for t in both]

    def first_tab(t, d):
        w = ways[t]
        to = step(w.b, d)
        return remote(own_tab.at[t, pl.ds(to * 4, 4)], tab_a.at[t, w.b],
                      ts1.at[t, d - 1], tr1.at[t, d - 1], w.dev(w.a, to, w.x))

    def second_tab(t, kk, d):
        w = ways[t]
        bs = step(w.b, -kk)
        to = step(w.x, d)
        return remote(tab_a.at[t, bs, to], tab_b.at[t, bs, w.x],
                      ts2.at[t, kk, d - 1], tr2.at[t, kk, d - 1], w.dev(w.a, w.b, to))

    def third(t, kk, piece, d):
        w = ways[t]
        bs = step(w.b, -kk)
        to = step(w.a, d)
        cols = pl.ds(*PIECES[piece])
        return remote(stage.at[t, kk, to, :, cols],
                      rows_out[t].at[w.block(w.a, bs), :, cols],
                      s3.at[t, kk, piece, d - 1], r3.at[t, kk, piece, d - 1],
                      w.dev(to, w.b, w.x))

    def kept(t, kk, piece):
        w = ways[t]
        bs = step(w.b, -kk)
        cols = pl.ds(*PIECES[piece])
        return pltpu.make_async_copy(stage.at[t, kk, w.a, :, cols],
                                     rows_out[t].at[w.block(w.a, bs), :, cols],
                                     ls.at[t, kk, piece])

    def share_tab(t, kk):
        w = ways[t]
        bs = step(w.b, -kk)
        if kk > 0:
            first_tab(t, kk).wait_recv()
        tab_b[t, bs, w.x] = tab_a[t, bs, w.x]
        for d in (1, 2, 3):
            second_tab(t, kk, d).start()

    def make_pick(t, kk):
        for d in (1, 2, 3):
            second_tab(t, kk, d).wait_recv()
        tables = tab_b[t, step(ways[t].b, -kk)]
        for a in range(SIDE):
            at = slice(a * GROUP, (a + 1) * GROUP)
            hit = hits_of(tables, a)
            pick[t, at, :] = jnp.where(hit, 1.0, 0.0).astype(jnp.bfloat16)
            if t == 1:
                weight = jnp.concatenate(lane_rows(tables, 1, a), axis=1)
                weight = jnp.sum(jnp.where(hit, weight, 0.0), axis=1, keepdims=True)
                scale[at, :] = jnp.broadcast_to(weight, (GROUP, 128))

    def send_rows(t, kk, piece):
        bs = step(ways[t].b, -kk)

        def tile(cols):
            block = gath[t, bs, :, :, cols].reshape(SIDE * TOK, cols.size)
            rows = jnp.dot(pick[t], block, preferred_element_type=jnp.float32)
            if t == 1:
                rows = rows * jnp.concatenate([scale[...]] * (cols.size // 128), axis=1)
            stage[t, kk, :, :, cols] = rows.astype(jnp.bfloat16).reshape(SIDE, GROUP, cols.size)

        column_tiles(*PIECES[piece], tile)
        for d in (1, 2, 3):
            third(t, kk, piece, d).start()
        kept(t, kk, piece).start()

    for t in both:
        for d in (1, 2, 3):
            first_tab(t, d).start()
        share_tab(t, 0)
        x_first[t].start()
    for h in both:
        for t in both:
            x_then[t][0, h].start()
        for t in both:
            b_first[t][h].start()
    for t in both:
        x_first[t].pass_on()
    for t in both:
        x_then[t][0, 0].pass_on()
    for t in both:
        b_first[t][0].pass_on()
    for t in both:
        x_first[t].finish()
        b_then[t].start()
    for t in both:
        b_first[t][1].pass_on()

    turns = [(kk, h) for kk in (0, 1, 3, 2) for h in both]
    for n, (kk, h) in enumerate(turns):
        if n + 2 < len(turns):
            k2, h2 = turns[n + 2]
            for t in both:
                if k2 == 2:
                    b_first[t][h2].finish()
                if h2 == 0:
                    share_tab(t, k2)
                x_then[t][k2, h2].start()
        if n + 1 < len(turns):
            for t in both:
                x_then[t][turns[n + 1]].pass_on()
        for t in both:
            x_then[t][kk, h].finish()
            if h == 0:
                make_pick(t, kk)
            send_rows(t, kk, h)
        if h == 1:
            for t in both:
                if kk == 1:
                    b_then[t].pass_on()
                if kk == 2:
                    b_then[t].finish()
                send_rows(t, kk, 2)

    tab_out[...] = tab_b[...]
    for t in both:
        for kk in range(SIDE):
            for d in (1, 2, 3):
                second_tab(t, kk, d).wait_send()
                for piece in range(3):
                    third(t, kk, piece, d).wait()
            for piece in range(3):
                kept(t, kk, piece).wait()
        for d in (1, 2, 3):
            first_tab(t, d).wait_send()
        for ring in (*b_first[t], *x_then[t].values(), x_first[t], b_then[t]):
            ring.drain()


def dispatch(ids_t, probs_t, tokens, cotangent):
    dma = pltpu.SemaphoreType.DMA
    vmem = pl.BlockSpec(memory_space=pltpu.VMEM)
    hbm = pl.BlockSpec(memory_space=pl.ANY)
    return pl.pallas_call(
        dispatch_kernel,
        name="dispatch",
        out_shape=(
            jax.ShapeDtypeStruct((16, GROUP, D), jnp.bfloat16),
            jax.ShapeDtypeStruct((16, GROUP, D), jnp.bfloat16),
            jax.ShapeDtypeStruct((2, SIDE, SIDE, 8, TOK), jnp.float32),
        ),
        in_specs=[vmem] * 4,
        out_specs=(hbm, hbm, vmem),
        scratch_shapes=[
            pltpu.VMEM((2, SIDE, SIDE, TOK, D), jnp.bfloat16),
            pltpu.VMEM((2, SIDE, SIDE, GROUP, D), jnp.bfloat16),
            pltpu.VMEM((2, 16, 8, TOK), jnp.float32),
            pltpu.VMEM((2, SIDE, SIDE, 8, TOK), jnp.float32),
            pltpu.VMEM((2, SIDE, SIDE, 8, TOK), jnp.float32),
            pltpu.VMEM((2, SIDE * GROUP, SIDE * TOK), jnp.bfloat16),
            pltpu.VMEM((SIDE * GROUP, 128), jnp.float32),
            dma((RINGS, 4)), dma((RINGS, 4)),
            dma((2, SIDE, 3, 3)), dma((2, SIDE, 3, 3)),
            dma((2, 3)), dma((2, 3)),
            dma((2, SIDE, 3)), dma((2, SIDE, 3)),
            dma((2, SIDE, 3)),
        ],
        compiler_params=pltpu.CompilerParams(
            collective_id=1, has_side_effects=True, vmem_limit_bytes=VMEM_LIMIT
        ),
    )(ids_t, probs_t, tokens, cotangent)


def contract_last(left_side, right_side):
    return lax.dot_general(
        left_side, right_side, (((1,), (1,)), ((), ())), preferred_element_type=jnp.float32
    )


def contract_rows(left_side, right_side):
    return lax.dot_general(
        left_side, right_side, (((0,), (0,)), ((), ())), preferred_element_type=jnp.float32
    )


def expert_kernel(x_ref, g_ref, wg_ref, wu_ref, wd_ref, out_ref, grad_ref, hid_ref, gu_ref):
    rows = x_ref[...]
    gate_pre = jnp.dot(rows, wg_ref[...], preferred_element_type=jnp.float32)
    up_pre = jnp.dot(rows, wu_ref[...], preferred_element_type=jnp.float32)
    sigmoid = jax.nn.sigmoid(gate_pre)
    activation = gate_pre * sigmoid
    derivative = sigmoid * (1.0 + gate_pre * (1.0 - sigmoid))
    hidden = (activation * up_pre).astype(jnp.bfloat16)
    hid_ref[...] = hidden
    out_ref[...] = jnp.dot(hidden, wd_ref[...], preferred_element_type=jnp.float32).astype(
        jnp.bfloat16
    )
    grad_hidden = contract_last(g_ref[...], wd_ref[...])
    gate_grad = (grad_hidden * up_pre * derivative).astype(jnp.bfloat16)
    up_grad = (grad_hidden * activation).astype(jnp.bfloat16)
    for half in range(2):
        cols = slice(half * FF // 2, (half + 1) * FF // 2)
        gu_ref[half, :, : FF // 2] = gate_grad[:, cols]
        gu_ref[half, :, FF // 2 :] = up_grad[:, cols]
    grad_ref[:, :D] = (
        contract_last(gate_grad, wg_ref[...]) + contract_last(up_grad, wu_ref[...])
    ).astype(jnp.bfloat16)
    product = jnp.sum(hidden.astype(jnp.float32) * grad_hidden, axis=1, keepdims=True)
    high = product.astype(jnp.bfloat16)
    low = (product - high.astype(jnp.float32)).astype(jnp.bfloat16)
    lane = lax.broadcasted_iota(jnp.int32, (rows.shape[0], 128), 1)
    me = lax.axis_index("expert")
    marks = jnp.where(lane == me, high.astype(jnp.float32), 0.0)
    marks = jnp.where(lane == me + EXPERTS, low.astype(jnp.float32), marks)
    grad_ref[:, D:] = marks.astype(jnp.bfloat16)


def expert_rows(x_rows, g_rows, w_gate, w_up, w_down):
    bm = 256
    whole = lambda shape: pl.BlockSpec(shape, lambda i: (0, 0), pipeline_mode=pl.Buffered(1))
    part = lambda width: pl.BlockSpec((bm, width), lambda i: (i, 0))
    bf = lambda width: jax.ShapeDtypeStruct((ROWS, width), jnp.bfloat16)
    return pl.pallas_call(
        expert_kernel,
        name="expert_rows",
        grid=(ROWS // bm,),
        out_shape=(
            bf(D),
            bf(WIDE),
            bf(FF),
            jax.ShapeDtypeStruct((2, ROWS, FF), jnp.bfloat16),
        ),
        in_specs=[part(D), part(D), whole((D, FF)), whole((D, FF)), whole((FF, D))],
        out_specs=(
            part(D),
            part(WIDE),
            part(FF),
            pl.BlockSpec((2, bm, FF), lambda i: (0, i, 0)),
        ),
        compiler_params=pltpu.CompilerParams(vmem_limit_bytes=VMEM_LIMIT),
        cost_estimate=pl.CostEstimate(
            flops=12 * ROWS * D * FF, bytes_accessed=40_000_000, transcendentals=ROWS * FF
        ),
    )(x_rows, g_rows, w_gate, w_up, w_down)


class WeightGrads:
    JOBS = 12

    def __init__(self, x_rows, g_rows, hid, grads, outs, lands, bufs, sems):
        self.x_rows, self.g_rows = x_rows, g_rows
        self.out_gate, self.out_up, self.out_down = outs
        self.land = lands
        (self.grads, self.hid, self.tile, self.made, self.mine, self.got, self.done_gu,
         self.done_d) = bufs
        self.load, self.send, self.recv, self.back, self.store, self.whole = sems
        self.dp, self.e = lax.axis_index("dp"), lax.axis_index("expert")
        self.other = 1 - self.dp
        self.next = 0
        self.fill = (pltpu.make_async_copy(grads, self.grads, self.whole.at[0]),
                     pltpu.make_async_copy(hid, self.hid, self.whole.at[1]))

    def loads(self, i):
        if i < 8:
            cols = pl.ds(i * 256, 256)
            return [pltpu.make_async_copy(self.x_rows.at[:, cols], self.tile.at[i % 2, 0],
                                          self.load.at[i, 0])]
        return [
            pltpu.make_async_copy(
                self.g_rows.at[:, pl.ds(pl.multiple_of(side * (D // 2) + (i - 8) * 256, 256), 256)],
                self.tile.at[i % 2, u], self.load.at[i, u])
            for u, side in enumerate((self.other, self.dp))
        ]

    def away(self, i):
        return remote(self.made.at[i % 2], self.land.at[i], self.send.at[i], self.recv.at[i],
                      (self.other, self.e))

    def fetch(self, i):
        return pltpu.make_async_copy(self.land.at[i], self.got, self.back.at[i])

    def stores(self, i):
        if i < 8:
            at = pl.ds(i * 256, 256)
            return [pltpu.make_async_copy(self.done_gu.at[i % 2, u], out.at[0, at],
                                          self.store.at[i, u])
                    for u, out in enumerate((self.out_gate, self.out_up))]
        return [pltpu.make_async_copy(self.done_d.at[i % 2],
                                      self.out_down.at[0, :, pl.ds((i - 8) * 256, 256)],
                                      self.store.at[i, 0])]

    def begin(self):
        for copy in self.fill:
            copy.start()
        for copy in self.loads(0):
            copy.start()

    def finish(self, i):
        self.fetch(i).wait()
        if i >= 2 and (i < 8 or i >= 10):
            for copy in self.stores(i - 2):
                copy.wait()
        slot = i % 2
        total = self.mine[slot].astype(jnp.float32) + self.got[...].astype(jnp.float32)
        if i < 8:
            total = total.astype(jnp.bfloat16)
            self.done_gu[slot, 0] = total[:, : FF // 2]
            self.done_gu[slot, 1] = total[:, FF // 2 :]
        else:
            self.done_d[slot] = jnp.transpose(total).astype(jnp.bfloat16)
        for copy in self.stores(i):
            copy.start()

    def job(self):
        i = self.next
        self.next += 1
        if i > self.JOBS:
            return
        if 0 < i:
            self.away(i - 1).wait_recv()
            self.fetch(i - 1).start()
        if i < self.JOBS:
            slot = i % 2
            if i == 0:
                self.fill[0].wait()
            if i == 8:
                self.fill[1].wait()
            for copy in self.loads(i):
                copy.wait()
            if i + 1 < self.JOBS:
                for copy in self.loads(i + 1):
                    copy.start()
            if i >= 2:
                self.away(i - 2).wait_send()
            def product(u, side):
                rows = self.tile[slot, 0 if i < 8 else u]
                right = self.grads[side] if i < 8 else self.hid[...]
                return contract_rows(rows, right).astype(jnp.bfloat16)

            self.made[slot] = product(0, self.other)
            self.away(i).start()
            self.mine[slot] = product(1, self.dp)
        if 0 < i:
            self.finish(i - 1)

    def end(self):
        while self.next <= self.JOBS:
            self.job()
        for i in (10, 11):
            self.away(i).wait_send()
        for i in (6, 7, 10, 11):
            for copy in self.stores(i):
                copy.wait()


class Scatter:
    def __init__(self, n, sems, me, dev, part, half, near_at, far_at, add):
        self.send, self.recv = sems
        self.n, self.me, self.dev, self.add = n, me, dev, add
        self.part, self.half, self.near_at, self.far_at = part, half, near_at, far_at

    def copy(self, src, dst, at, s):
        return remote(src, dst, self.send.at[self.n, at], self.recv.at[self.n, at],
                      self.dev(step(self.me, s)))

    def near(self, s):
        u = 0 if s > 0 else 1
        return self.copy(self.part(s), self.near_at(u), u, s)

    def far(self, s):
        u = 0 if s > 0 else 1
        return self.copy(self.half(2, u), self.far_at(u), 2 + u, s)

    def first(self):
        for s in (1, -1):
            self.far(s).start()

    def second(self, s):
        u = 0 if s > 0 else 1
        self.far(s).wait_recv()
        self.add(self.half(s, u), self.far_at(u))
        self.near(s).start()

    def third(self):
        for s in (1, -1):
            self.near(s).wait_recv()

    def drain(self):
        for s in (1, -1):
            self.near(s).wait_send()
            self.far(s).wait_send()


def add_flat(to, more):
    width = to.shape[-1]

    def tile(cols):
        total = to[:, cols].astype(jnp.float32) + more[:, cols].astype(jnp.float32)
        to[:, cols] = total.astype(jnp.bfloat16)

    column_tiles(0, width, tile)


def add_lines(to, more):
    for i in range(2):
        add_flat(to.at[i], more.at[i])


def return_kernel(
    out_rows, grad_rows, tab_ref, x_rows, g_rows, hid, grads,
    mixed_ref, gtok_ref, mark_ref, out_gate, out_up, out_down, land,
    back0, back1, pick, lpart, lnear, lfar, zpart, znear, zfar,
    fpart0, fpart1, fnear0, fnear1, ffar0, ffar1, fsum0, fsum1, xnear0, xnear1, xfar0, xfar1,
    gs, gr, sa, ra, la, *weight_scratch,
):
    ways = (Way(0), Way(1))
    weights = WeightGrads(x_rows, g_rows, hid, grads, (out_gate, out_up, out_down),
                          land, weight_scratch[:8], weight_scratch[8:])
    rows_in = (out_rows, grad_rows)
    back, fpart, fnear, ffar = (back0, back1), (fpart0, fpart1), (fnear0, fnear1), (ffar0, ffar1)
    fsum, xnear, xfar = (fsum0, fsum1), (xnear0, xnear1), (xfar0, xfar1)
    tails = (D - LATE, WIDE - LATE)
    sems = (gs, gr)
    both = (0, 1)
    order = (2, 1, 3, 0)
    greet_lines()

    def piece_cols(t, piece):
        return pl.ds(*PIECES[piece]) if piece < 2 else pl.ds(LATE, tails[t])

    def home(t, kk, piece, d):
        w = ways[t]
        bs = step(w.b, kk)
        to = step(w.a, d)
        cols = piece_cols(t, piece)
        return remote(rows_in[t].at[w.block(to, bs), :, cols], back[t].at[bs, w.a, :, cols],
                      sa.at[t, kk, piece, d - 1], ra.at[t, kk, piece, d - 1],
                      w.dev(to, w.b, w.x))

    def stay(t, kk):
        w = ways[t]
        bs = step(w.b, kk)
        return pltpu.make_async_copy(rows_in[t].at[w.block(w.a, bs)], back[t].at[bs, w.a],
                                     la.at[t, kk])

    def send_home(kk):
        for t in both:
            stay(t, kk).start()
        for piece in range(3):
            for t in both:
                for d in (1, 2, 3):
                    home(t, kk, piece, d).start()

    send_home(order[0])
    weights.begin()
    count = iter(range(RINGS))

    def along_x(t, n, kk, h):
        w, cols = ways[t], pl.ds(*PIECES[h])
        at = n % 2
        return Scatter(next(count), sems, w.x, lambda i: w.dev(w.a, w.b, i),
                       lambda o: lpart.at[t, at, step(w.x, o), :, cols],
                       lambda o, u: lpart.at[t, at, step(w.x, o), pl.ds(u * 64, 64), cols],
                       lambda u: lnear.at[t, kk, u, :, cols],
                       lambda u: lfar.at[t, kk, u, :, cols], add_flat)

    def along_b(t):
        w = ways[t]
        return Scatter(next(count), sems, w.b, lambda i: w.dev(w.a, i, w.x),
                       lambda o: zpart.at[t, o % 4],
                       lambda o, u: zpart.at[t, o % 4, pl.ds(u * 64, 64)],
                       lambda u: znear.at[t, u], lambda u: zfar.at[t, u], add_flat)

    def lines_b(t):
        w = ways[t]
        return Scatter(next(count), sems, w.b, lambda i: w.dev(w.a, i, w.x),
                       lambda o: fpart[t].at[o % 4],
                       lambda o, u: fpart[t].at[o % 4, pl.ds(u * 2, 2)],
                       lambda u: fnear[t].at[u], lambda u: ffar[t].at[u], add_lines)

    def late_x(t):
        w = ways[t]
        return Scatter(next(count), sems, w.x, lambda i: w.dev(w.a, w.b, i),
                       lambda o: fsum[t].at[step(w.x, o)],
                       lambda o, u: fsum[t].at[step(w.x, o), pl.ds(u * 64, 64)],
                       lambda u: xnear[t].at[u], lambda u: xfar[t].at[u], add_flat)

    x_first = [{(kk, h): along_x(t, n, kk, h) for n, kk in enumerate(order) for h in both}
               for t in both]
    b_then = [along_b(t) for t in both]
    b_first = [lines_b(t) for t in both]
    x_then = [late_x(t) for t in both]

    def make_pick(t, kk):
        tables = tab_ref[t, step(ways[t].b, kk)]
        parts = []
        for a in range(SIDE):
            hit = hits_of(tables, a)
            weight = jnp.concatenate(lane_rows(tables, 1, a), axis=1) if t == 0 else 1.0
            parts.append(jnp.where(hit, weight, 0.0))
        pick[...] = jnp.transpose(jnp.concatenate(parts, axis=0)).astype(jnp.bfloat16)

    def sum_experts(t, n, kk, piece):
        bs = step(ways[t].b, kk)
        for d in (1, 2, 3):
            home(t, kk, piece, d).wait_recv()

        def tile(cols):
            rows = back[t][bs, :, :, cols].reshape(SIDE * GROUP, cols.size)
            sums = jnp.dot(pick[...], rows, preferred_element_type=jnp.float32).astype(jnp.bfloat16)
            sums = sums.reshape(SIDE, TOK, cols.size)
            if piece < 2:
                lpart[t, n % 2, :, :, cols] = sums
            else:
                fpart[t][kk, :, :, pl.ds(cols.start - LATE, cols.size)] = sums

        start, width = PIECES[piece] if piece < 2 else (LATE, tails[t])
        column_tiles(start, width, tile)

    def collect_x(t, n, kk):
        w = ways[t]
        for h in both:
            x_first[t][kk, h].third()

        def tile(cols):
            total = lpart[t, n % 2, w.x, :, cols].astype(jnp.float32)
            total = total + jnp.sum(lnear[t, kk, :, :, cols].astype(jnp.float32), axis=0)
            zpart[t, kk, :, cols] = total.astype(jnp.bfloat16)

        column_tiles(0, LATE, tile)
        if kk == 2:
            b_then[t].first()
        if kk in (1, 3):
            b_then[t].second(1 if kk == 1 else -1)

    for n, kk in enumerate(order):
        if n + 1 < SIDE:
            send_home(order[n + 1])
        for t in both:
            stay(t, kk).wait()
            make_pick(t, kk)
            weights.job()
            if n >= 2:
                for h in both:
                    x_first[t][order[n - 2], h].drain()
            for h in both:
                sum_experts(t, n, kk, h)
                x_first[t][kk, h].first()
            sum_experts(t, n, kk, 2)
            if kk == 2:
                b_first[t].first()
            if kk in (1, 3):
                b_first[t].second(1 if kk == 1 else -1)
        for t in both:
            for h in both:
                x_first[t][kk, h].second(1)
                x_first[t][kk, h].second(-1)
        weights.job()
        if n >= 1:
            for t in both:
                collect_x(t, n - 1, order[n - 1])

    for t in both:
        b_first[t].third()
        for i in range(SIDE):

            def tile(cols, t=t, i=i):
                total = fpart[t][0, i, :, cols].astype(jnp.float32)
                total = total + jnp.sum(fnear[t][:, i, :, cols].astype(jnp.float32), axis=0)
                fsum[t][i, :, cols] = total.astype(jnp.bfloat16)

            column_tiles(0, tails[t], tile)
        x_then[t].first()
    weights.end()
    for t in both:
        x_then[t].second(1)
        x_then[t].second(-1)
    results = (mixed_ref, gtok_ref)
    for t in both:
        collect_x(t, 3, 0)
        b_then[t].third()

        def tile(cols, t=t):
            total = zpart[t, 0, :, cols].astype(jnp.float32)
            total = total + jnp.sum(znear[t, :, :, cols].astype(jnp.float32), axis=0)
            results[t][:, cols] = total.astype(jnp.bfloat16)

        column_tiles(0, LATE, tile)
    for t in both:
        w = ways[t]
        x_then[t].third()

        def late(cols, t=t, w=w):
            total = fsum[t][w.x, :, cols].astype(jnp.float32)
            return total + jnp.sum(xnear[t][:, :, cols].astype(jnp.float32), axis=0)

        def tile(cols, t=t, late=late):
            results[t][:, pl.ds(cols.start + LATE, cols.size)] = late(cols).astype(jnp.bfloat16)

        column_tiles(0, D - LATE, tile)
        if t == 1:
            mark_ref[...] = late(pl.ds(D - LATE, 128))

    for t in both:
        for n, kk in enumerate(order):
            for piece in range(3):
                for d in (1, 2, 3):
                    home(t, kk, piece, d).wait_send()
            if n >= 2:
                for h in both:
                    x_first[t][kk, h].drain()
        b_then[t].drain()
        b_first[t].drain()
        x_then[t].drain()


def bring_back(out_rows, grad_rows, tables, x_rows, g_rows, hid, grads):
    dma = pltpu.SemaphoreType.DMA
    vmem = pl.BlockSpec(memory_space=pltpu.VMEM)
    hbm = pl.BlockSpec(memory_space=pl.ANY)
    buf = lambda *shape: pltpu.VMEM(shape, jnp.bfloat16)
    pair = lambda *lead: [buf(*lead, D - LATE), buf(*lead, WIDE - LATE)]
    return pl.pallas_call(
        return_kernel,
        name="bring_back",
        out_shape=(
            jax.ShapeDtypeStruct((TOK, D), jnp.bfloat16),
            jax.ShapeDtypeStruct((TOK, D), jnp.bfloat16),
            jax.ShapeDtypeStruct((TOK, 128), jnp.float32),
            jax.ShapeDtypeStruct((1, D, FF // 2), jnp.bfloat16),
            jax.ShapeDtypeStruct((1, D, FF // 2), jnp.bfloat16),
            jax.ShapeDtypeStruct((1, FF, D // 2), jnp.bfloat16),
            jax.ShapeDtypeStruct((WeightGrads.JOBS, 256, FF), jnp.bfloat16),
        ),
        in_specs=[hbm, hbm, vmem, hbm, hbm, hbm, hbm],
        out_specs=(vmem, vmem, vmem, hbm, hbm, hbm, hbm),
        scratch_shapes=[
            buf(SIDE, SIDE, GROUP, D), buf(SIDE, SIDE, GROUP, WIDE),
            buf(SIDE * TOK, SIDE * GROUP),
            buf(2, 2, SIDE, TOK, LATE), buf(2, SIDE, 2, TOK, LATE), buf(2, SIDE, 2, TOK // 2, LATE),
            buf(2, SIDE, TOK, LATE), buf(2, 2, TOK, LATE), buf(2, 2, TOK // 2, LATE),
            *pair(SIDE, SIDE, TOK), *pair(2, SIDE, TOK), *pair(2, 2, TOK),
            *pair(SIDE, TOK), *pair(2, TOK), *pair(2, TOK // 2),
            dma((RINGS, 4)), dma((RINGS, 4)),
            dma((2, SIDE, 3, 3)), dma((2, SIDE, 3, 3)),
            dma((2, SIDE)),
            buf(2, ROWS, FF), buf(ROWS, FF), buf(2, 2, ROWS, 256),
            buf(2, 256, FF), buf(2, 256, FF), buf(256, FF), buf(2, 2, 256, FF // 2),
            buf(2, FF, 256),
            dma((12, 2)), dma((12,)), dma((12,)), dma((12,)), dma((12, 2)), dma((2,)),
        ],
        compiler_params=pltpu.CompilerParams(
            collective_id=3, has_side_effects=True, vmem_limit_bytes=VMEM_LIMIT
        ),
    )(out_rows, grad_rows, tables, x_rows, g_rows, hid, grads)


def body(tokens, route_ids, route_probs, cotangent, w_gate, w_up, w_down):
    x_rows, g_rows, tables = dispatch(route_ids.T, route_probs.T, tokens, cotangent)
    x_rows, g_rows = x_rows.reshape(ROWS, D), g_rows.reshape(ROWS, D)
    out_rows, grad_rows, hidden, grads = expert_rows(
        x_rows, g_rows, w_gate[0], w_up[0], w_down[0]
    )
    mixed, grad_tokens, marks, grad_gate, grad_up, grad_down, _ = bring_back(
        out_rows.reshape(16, GROUP, D), grad_rows.reshape(16, GROUP, WIDE), tables,
        x_rows, g_rows, hidden, grads,
    )
    product = marks[:, :EXPERTS] + marks[:, EXPERTS:]
    chosen = route_ids[:, :, None] == jnp.arange(EXPERTS, dtype=jnp.int32)[None, None, :]
    grad_probs = jnp.sum(jnp.where(chosen, product[:, None, :], 0.0), axis=2) / route_probs
    return (mixed, grad_tokens, grad_probs, grad_gate, grad_up, grad_down)


def solution(mesh):
    both = P(("dp", "expert"), None)
    mine = P("expert", None, None)
    split = P("expert", None, "dp")
    return jax.shard_map(
        body,
        mesh=mesh,
        in_specs=(both, both, both, both, mine, mine, mine),
        out_specs=(both, both, both, split, split, split),
        check_vma=False,
    )
```

```python
import functools

import jax
import jax.numpy as jnp
from jax import lax
from jax.experimental import pallas as pl
from jax.experimental.pallas import tpu as pltpu
from jax.sharding import PartitionSpec as P

D = 2048
FF = 768
TOP = 8
TOK = 128
CAP = 28
SIDE = 4
EXPERTS = 64
GROUP = SIDE * CAP
ROWS = 16 * GROUP
WIDE = D + 128
LATE = 1536
PIECES = ((0, 768), (768, 768), (1536, 512))
RINGS = 24
TURN_ORDER = "0101010101010101"
START_AHEAD = 4
PASS_AHEAD = 2
EXPERTS_AFTER = (9, 13, 15)
MESH = pl.DeviceIdType.MESH
VMEM_LIMIT = 63 * 1024 * 1024


def where_am_i():
    e = lax.axis_index("expert")
    return lax.axis_index("dp"), e // 16, (e // 4) % 4, e % 4


class Way:
    def __init__(self, t):
        self.t = t
        self.dp, z, self.x, y = where_am_i()
        self.a, self.b = (y, z) if t == 0 else (z, y)

    def dev(self, a, b, x):
        z, y = (b, a) if self.t == 0 else (a, b)
        return (self.dp, z * 16 + x * 4 + y)

    def block(self, a, b):
        return a * 4 + b if self.t == 0 else b * 4 + a


def step(v, d):
    return lax.rem(v + d + SIDE, SIDE)


def greet_lines():
    dp, z, x, y = where_am_i()
    barrier = pltpu.get_barrier_semaphore()
    for d in (1, 2, 3):
        for to in (
            step(z, d) * 16 + x * 4 + y,
            z * 16 + step(x, d) * 4 + y,
            z * 16 + x * 4 + step(y, d),
        ):
            pl.semaphore_signal(barrier, inc=1, device_id=(dp, to), device_id_type=MESH)
    pl.semaphore_signal(barrier, inc=1, device_id=(1 - dp, z * 16 + x * 4 + y), device_id_type=MESH)
    pl.semaphore_wait(barrier, 10)


def remote(src, dst, send, recv, dev):
    return pltpu.make_async_remote_copy(
        src_ref=src, dst_ref=dst, send_sem=send, recv_sem=recv, device_id=dev, device_id_type=MESH
    )


def own_table(t, ids_ref, probs_ref):
    row = lax.broadcasted_iota(jnp.int32, (TOK, TOK), 0)
    b, x, kind, a = row // 32, (row // 8) % 4, (row // 4) % 2, row % 4
    expert = b * 16 + x * 4 + a if t == 0 else a * 16 + x * 4 + b
    hit = jnp.zeros((TOK, TOK), jnp.float32)
    weight = jnp.zeros((TOK, TOK), jnp.float32)
    for k in range(TOP):
        same = expert == ids_ref[k : k + 1, :]
        hit = jnp.where(same, 1.0, hit)
        weight = jnp.where(same, probs_ref[k : k + 1, :], weight)
    before = lax.broadcasted_iota(jnp.int32, (TOK, TOK), 0) < lax.broadcasted_iota(
        jnp.int32, (TOK, TOK), 1
    )
    before = jnp.where(before, 1.0, 0.0).astype(jnp.bfloat16)
    slot = jnp.dot(hit.astype(jnp.bfloat16), before, preferred_element_type=jnp.float32)
    slot = jnp.where(hit > 0.5, slot, -1000.0)
    return jnp.where(kind == 0, slot, weight)


def lane_rows(tables, kind, a):
    return [tables[xs, kind * 4 + a : kind * 4 + a + 1, :] for xs in range(SIDE)]


def hits_of(tables, a):
    slots = jnp.concatenate(
        [v + float(CAP * xs) for xs, v in enumerate(lane_rows(tables, 0, a))], axis=1
    )
    row = lax.broadcasted_iota(jnp.int32, (GROUP, SIDE * TOK), 0).astype(jnp.float32)
    return row == slots


class Gather:
    def __init__(self, n, sems, me, dev, block, half):
        self.send, self.recv = sems
        self.n, self.me, self.dev, self.block, self.half = n, me, dev, block, half

    def copy(self, ref, at, s):
        return remote(ref, ref, self.send.at[self.n, at], self.recv.at[self.n, at],
                      self.dev(step(self.me, s)))

    def near(self, s):
        return self.copy(self.block(self.me), 0 if s > 0 else 1, s)

    def far(self, s):
        return self.copy(self.half(step(self.me, -s), 0 if s > 0 else 1), 2 if s > 0 else 3, s)

    def start(self):
        for s in (1, -1):
            self.near(s).start()

    def pass_on(self):
        for s in (1, -1):
            self.near(s).wait_recv()
            self.far(s).start()

    def finish(self):
        for s in (1, -1):
            self.far(s).wait_recv()

    def drain(self):
        for s in (1, -1):
            self.near(s).wait_send()
            self.far(s).wait_send()


def column_tiles(start, width, tile):
    def one(c, _):
        tile(pl.ds(pl.multiple_of(start + c * 256, 128), 256))
        return 0

    lax.fori_loop(0, width // 256, one, 0)
    if width % 256:
        tile(pl.ds(start + width // 256 * 256, width % 256))


def dispatch_kernel(
    ids_ref, probs_ref, tok_ref, cot_ref, w_gate, w_up, w_down,
    x_rows, g_rows, tab_out, out_rows, grad_rows, hid_rows, gu_rows,
    gath, stage, own_tab, tab_a, tab_b, pick, scale,
    x_here, g_here, wg, wu, wd, out_st, grad_st, hid_st, gu_st,
    gs, gr, s3, r3, ts1, tr1, ts2, tr2, ls, wsem, xsem, osem,
):
    ways = (Way(0), Way(1))
    rows_out = (x_here, g_here)
    sems = (gs, gr)
    weight_loads = [pltpu.make_async_copy(src.at[0], dst, wsem.at[n])
                    for n, (src, dst) in enumerate(((w_gate, wg), (w_up, wu), (w_down, wd)))]
    for copy in weight_loads:
        copy.start()

    for t, src in ((0, tok_ref), (1, cot_ref)):
        w = ways[t]
        own_tab[t] = own_table(t, ids_ref, probs_ref).reshape(16, 8, TOK)
        gath[t, w.b, w.x] = src[...]
        tab_a[t, w.b] = own_tab[t, pl.ds(w.b * 4, 4)]
    greet_lines()

    count = iter(range(RINGS))

    def along_b(t, piece):
        w, cols = ways[t], pl.ds(*PIECES[piece])
        return Gather(next(count), sems, w.b, lambda i: w.dev(w.a, i, w.x),
                      lambda i: gath.at[t, i, w.x, :, cols],
                      lambda i, u: gath.at[t, i, w.x, pl.ds(u * 64, 64), cols])

    def along_x(t, kk, piece):
        w, cols = ways[t], pl.ds(*PIECES[piece])
        bs = step(w.b, -kk)
        return Gather(next(count), sems, w.x, lambda i: w.dev(w.a, w.b, i),
                      lambda i: gath.at[t, bs, i, :, cols],
                      lambda i, u: gath.at[t, bs, i, pl.ds(u * 64, 64), cols])

    def lines_b(t):
        w, cols = ways[t], pl.ds(*PIECES[2])
        return Gather(next(count), sems, w.b, lambda i: w.dev(w.a, i, w.x),
                      lambda i: gath.at[t, i, :, :, cols],
                      lambda i, u: gath.at[t, i, pl.ds(u * 2, 2), :, cols])

    both = (0, 1)
    order = (0, 1, 3, 2)
    slot_of = lambda kk: order.index(kk) % 2
    b_first = [[along_b(t, h) for h in both] for t in both]
    x_then = [{(kk, h): along_x(t, kk, h) for kk in range(SIDE) for h in both} for t in both]
    x_first = [along_x(t, 0, 2) for t in both]
    b_then = [lines_b(t) for t in both]

    def first_tab(t, d):
        w = ways[t]
        to = step(w.b, d)
        return remote(own_tab.at[t, pl.ds(to * 4, 4)], tab_a.at[t, w.b],
                      ts1.at[t, d - 1], tr1.at[t, d - 1], w.dev(w.a, to, w.x))

    def second_tab(t, kk, d):
        w = ways[t]
        bs = step(w.b, -kk)
        to = step(w.x, d)
        return remote(tab_a.at[t, bs, to], tab_b.at[t, bs, w.x],
                      ts2.at[t, kk, d - 1], tr2.at[t, kk, d - 1], w.dev(w.a, w.b, to))

    def third(t, kk, piece, d):
        w = ways[t]
        bs = step(w.b, -kk)
        to = step(w.a, d)
        cols = pl.ds(*PIECES[piece])
        return remote(stage.at[t, slot_of(kk), to, :, cols],
                      rows_out[t].at[w.block(w.a, bs), :, cols],
                      s3.at[t, kk, piece, d - 1], r3.at[t, kk, piece, d - 1],
                      w.dev(to, w.b, w.x))

    def kept(t, kk, piece):
        w = ways[t]
        bs = step(w.b, -kk)
        cols = pl.ds(*PIECES[piece])
        return pltpu.make_async_copy(stage.at[t, slot_of(kk), w.a, :, cols],
                                     rows_out[t].at[w.block(w.a, bs), :, cols],
                                     ls.at[t, kk, piece])

    def share_tab(t, kk):
        w = ways[t]
        bs = step(w.b, -kk)
        if kk > 0:
            first_tab(t, kk).wait_recv()
        tab_b[t, bs, w.x] = tab_a[t, bs, w.x]
        for d in (1, 2, 3):
            second_tab(t, kk, d).start()

    def make_pick(t, kk):
        for d in (1, 2, 3):
            second_tab(t, kk, d).wait_recv()
        tables = tab_b[t, step(ways[t].b, -kk)]
        for a in range(SIDE):
            at = slice(a * GROUP, (a + 1) * GROUP)
            hit = hits_of(tables, a)
            pick[t, at, :] = jnp.where(hit, 1.0, 0.0).astype(jnp.bfloat16)
            if t == 1:
                weight = jnp.concatenate(lane_rows(tables, 1, a), axis=1)
                weight = jnp.sum(jnp.where(hit, weight, 0.0), axis=1, keepdims=True)
                scale[at, :] = jnp.broadcast_to(weight, (GROUP, 128))

    def send_rows(t, kk, piece):
        bs = step(ways[t].b, -kk)

        def tile(cols):
            block = gath[t, bs, :, :, cols].reshape(SIDE * TOK, cols.size)
            rows = jnp.dot(pick[t], block, preferred_element_type=jnp.float32)
            if t == 1:
                rows = rows * jnp.concatenate([scale[...]] * (cols.size // 128), axis=1)
            stage[t, slot_of(kk), :, :, cols] = rows.astype(jnp.bfloat16).reshape(SIDE, GROUP, cols.size)

        if order.index(kk) >= 2:
            leave(t, order[order.index(kk) - 2], piece)
        column_tiles(*PIECES[piece], tile)
        for d in (1, 2, 3):
            third(t, kk, piece, d).start()
        kept(t, kk, piece).start()

    settled = set()

    def settle(t, kk, piece):
        if (t, kk, piece) not in settled:
            settled.add((t, kk, piece))
            kept(t, kk, piece).wait()

    def leave(t, kk, piece):
        for d in (1, 2, 3):
            third(t, kk, piece, d).wait_send()
        settle(t, kk, piece)

    def arrive(t, kk):
        for piece in range(3):
            for d in (1, 2, 3):
                third(t, kk, piece, d).wait_recv()
            settle(t, kk, piece)

    dp, z, x, y = where_am_i()
    kept_rows = [pltpu.make_async_copy(here, rows, xsem.at[n])
                 for n, (here, rows) in enumerate(((x_here, x_rows), (g_here, g_rows)))]

    def results(blocks):
        copies = []
        for u, at in enumerate(blocks):
            pairs = ((out_st.at[u], out_rows.at[at]), (grad_st.at[u], grad_rows.at[at]),
                     (hid_st.at[u], hid_rows.at[at]), (gu_st.at[:, u], gu_rows.at[:, at]))
            copies += [pltpu.make_async_copy(src, dst, osem.at[u, n])
                       for n, (src, dst) in enumerate(pairs)]
        return copies

    def block_of(m_y, m_z):
        turn = lambda m: m + m // 2 - 2 * (m // 3)
        return step(y, -turn(m_y)) * 4 + step(z, -turn(m_z))

    def experts(m):
        if m == 1:
            for copy in weight_loads:
                copy.wait()
        for k2 in order[:2] if m == 1 else order[m : m + 1]:
            for t in both:
                arrive(t, k2)
        if m == 3:
            for copy in kept_rows:
                copy.start()
        many = 2 * GROUP

        def some(p, _):
            if m == 1:
                blocks = (block_of(0, 1 - p), block_of(1, p))
            elif m == 2:
                blocks = (block_of(p, 2), block_of(2, p))
            else:
                blocks = (block_of(p, 3), block_of(3 - p // 3, p - p // 3))
            rows = jnp.concatenate([x_here[at] for at in blocks], axis=0)
            gate_pre = jnp.dot(rows, wg[...], preferred_element_type=jnp.float32)
            up_pre = jnp.dot(rows, wu[...], preferred_element_type=jnp.float32)
            sigmoid = jax.nn.sigmoid(gate_pre)
            activation = gate_pre * sigmoid
            derivative = sigmoid * (1.0 + gate_pre * (1.0 - sigmoid))
            hidden = (activation * up_pre).astype(jnp.bfloat16)

            def settle_results():
                for copy in results(blocks):
                    copy.wait()

            if m == 1:
                pl.when(p > 0)(settle_results)
            else:
                settle_results()
            hid_st[...] = hidden.reshape(2, GROUP, FF)
            out = jnp.dot(hidden, wd[...], preferred_element_type=jnp.float32)
            out_st[...] = out.astype(jnp.bfloat16).reshape(2, GROUP, D)
            grads = jnp.concatenate([g_here[at] for at in blocks], axis=0)
            grad_hidden = contract_last(grads, wd[...])
            gate_grad = (grad_hidden * up_pre * derivative).astype(jnp.bfloat16)
            up_grad = (grad_hidden * activation).astype(jnp.bfloat16)
            for half in range(2):
                cols = slice(half * FF // 2, (half + 1) * FF // 2)
                gu_st[half, :, :, : FF // 2] = gate_grad[:, cols].reshape(2, GROUP, FF // 2)
                gu_st[half, :, :, FF // 2 :] = up_grad[:, cols].reshape(2, GROUP, FF // 2)
            grad = contract_last(gate_grad, wg[...]) + contract_last(up_grad, wu[...])
            grad_st[:, :, :D] = grad.astype(jnp.bfloat16).reshape(2, GROUP, D)
            product = jnp.sum(hidden.astype(jnp.float32) * grad_hidden, axis=1, keepdims=True)
            high = product.astype(jnp.bfloat16).astype(jnp.float32)
            low = product - high
            lane = lax.broadcasted_iota(jnp.int32, (many, 128), 1)
            me = lax.axis_index("expert")
            marks = jnp.where(lane == me, high, 0.0)
            marks = jnp.where(lane == me + EXPERTS, low, marks)
            grad_st[:, :, D:] = marks.astype(jnp.bfloat16).reshape(2, GROUP, 128)
            for copy in results(blocks):
                copy.start()
            return 0

        lax.fori_loop(0, 4 if m == 3 else 2, some, 0)
        if m == 3:
            for copy in results((0, 1)):
                copy.wait()
            for copy in kept_rows:
                copy.wait()

    turns = [[(t, kk, h) for kk in order for h in both] for t in both]
    plan = []
    for c in TURN_ORDER:
        plan.append(turns[int(c)].pop(0))
    begun = {(t, 0, h) for t in both for h in both}
    passed = {(t, 0, 0) for t in both}

    def begin(t, kk, h):
        if (t, kk, h) in begun:
            return
        begun.add((t, kk, h))
        if kk == 2:
            b_first[t][h].finish()
        if h == 0 and kk != 0:
            share_tab(t, kk)
        x_then[t][kk, h].start()

    def pass_on(t, kk, h):
        if (t, kk, h) not in passed:
            passed.add((t, kk, h))
            x_then[t][kk, h].pass_on()

    for t in both:
        for d in (1, 2, 3):
            first_tab(t, d).start()
        share_tab(t, 0)
        x_first[t].start()
    for h in both:
        for t in both:
            x_then[t][0, h].start()
        for t in both:
            b_first[t][h].start()
    for t in both:
        x_first[t].pass_on()
    for t in both:
        x_then[t][0, 0].pass_on()
    for t in both:
        b_first[t][0].pass_on()
    for t in both:
        x_first[t].finish()
        b_then[t].start()
    for t in both:
        b_first[t][1].pass_on()
    for n, (t, kk, h) in enumerate(plan):
        if n + START_AHEAD < len(plan):
            begin(*plan[n + START_AHEAD])
        for item in plan[: n + PASS_AHEAD + 1]:
            pass_on(*item)
        x_then[t][kk, h].finish()
        if h == 0:
            make_pick(t, kk)
        send_rows(t, kk, h)
        if h == 1:
            if kk == 1:
                b_then[t].pass_on()
            if kk == 2:
                b_then[t].finish()
            send_rows(t, kk, 2)
        if n in EXPERTS_AFTER:
            experts(EXPERTS_AFTER.index(n) + 1)

    tab_out[...] = tab_b[...]
    for t in both:
        for kk in range(SIDE):
            for d in (1, 2, 3):
                second_tab(t, kk, d).wait_send()
                if kk in order[2:]:
                    for piece in range(3):
                        third(t, kk, piece, d).wait_send()
        for d in (1, 2, 3):
            first_tab(t, d).wait_send()
        for ring in (*b_first[t], *x_then[t].values(), x_first[t], b_then[t]):
            ring.drain()


def dispatch(ids_t, probs_t, tokens, cotangent, w_gate, w_up, w_down):
    dma = pltpu.SemaphoreType.DMA
    vmem = pl.BlockSpec(memory_space=pltpu.VMEM)
    hbm = pl.BlockSpec(memory_space=pl.ANY)
    buf = lambda *shape: pltpu.VMEM(shape, jnp.bfloat16)
    return pl.pallas_call(
        dispatch_kernel,
        name="dispatch",
        out_shape=(
            jax.ShapeDtypeStruct((16, GROUP, D), jnp.bfloat16),
            jax.ShapeDtypeStruct((16, GROUP, D), jnp.bfloat16),
            jax.ShapeDtypeStruct((2, SIDE, SIDE, 8, TOK), jnp.float32),
            jax.ShapeDtypeStruct((16, GROUP, D), jnp.bfloat16),
            jax.ShapeDtypeStruct((16, GROUP, WIDE), jnp.bfloat16),
            jax.ShapeDtypeStruct((16, GROUP, FF), jnp.bfloat16),
            jax.ShapeDtypeStruct((2, 16, GROUP, FF), jnp.bfloat16),
        ),
        in_specs=[vmem] * 4 + [hbm] * 3,
        out_specs=(hbm, hbm, vmem, hbm, hbm, hbm, hbm),
        scratch_shapes=[
            pltpu.VMEM((2, SIDE, SIDE, TOK, D), jnp.bfloat16),
            pltpu.VMEM((2, 2, SIDE, GROUP, D), jnp.bfloat16),
            pltpu.VMEM((2, 16, 8, TOK), jnp.float32),
            pltpu.VMEM((2, SIDE, SIDE, 8, TOK), jnp.float32),
            pltpu.VMEM((2, SIDE, SIDE, 8, TOK), jnp.float32),
            pltpu.VMEM((2, SIDE * GROUP, SIDE * TOK), jnp.bfloat16),
            pltpu.VMEM((SIDE * GROUP, 128), jnp.float32),
            buf(16, GROUP, D), buf(16, GROUP, D), buf(D, FF), buf(D, FF), buf(FF, D),
            buf(2, GROUP, D), buf(2, GROUP, WIDE), buf(2, GROUP, FF), buf(2, 2, GROUP, FF),
            dma((RINGS, 4)), dma((RINGS, 4)),
            dma((2, SIDE, 3, 3)), dma((2, SIDE, 3, 3)),
            dma((2, 3)), dma((2, 3)),
            dma((2, SIDE, 3)), dma((2, SIDE, 3)),
            dma((2, SIDE, 3)), dma((3,)), dma((2,)), dma((2, 4)),
        ],
        compiler_params=pltpu.CompilerParams(
            collective_id=1, has_side_effects=True, vmem_limit_bytes=VMEM_LIMIT
        ),
    )(ids_t, probs_t, tokens, cotangent, w_gate, w_up, w_down)


def contract_last(left_side, right_side):
    return lax.dot_general(
        left_side, right_side, (((1,), (1,)), ((), ())), preferred_element_type=jnp.float32
    )


def contract_rows(left_side, right_side):
    return lax.dot_general(
        left_side, right_side, (((0,), (0,)), ((), ())), preferred_element_type=jnp.float32
    )


class WeightGrads:
    JOBS = 12

    def __init__(self, x_rows, g_rows, hid, grads, outs, lands, bufs, sems):
        self.x_rows, self.g_rows = x_rows, g_rows
        self.out_gate, self.out_up, self.out_down = outs
        self.land = lands
        (self.grads, self.hid, self.tile, self.made, self.mine, self.got, self.done_gu,
         self.done_d) = bufs
        self.load, self.send, self.recv, self.back, self.store, self.whole = sems
        self.dp, self.e = lax.axis_index("dp"), lax.axis_index("expert")
        self.other = 1 - self.dp
        self.next = 0
        self.fill = (pltpu.make_async_copy(grads, self.grads, self.whole.at[0]),
                     pltpu.make_async_copy(hid, self.hid, self.whole.at[1]))

    def loads(self, i):
        if i < 8:
            cols = pl.ds(i * 256, 256)
            return [pltpu.make_async_copy(self.x_rows.at[:, cols], self.tile.at[i % 2, 0],
                                          self.load.at[i, 0])]
        return [
            pltpu.make_async_copy(
                self.g_rows.at[:, pl.ds(pl.multiple_of(side * (D // 2) + (i - 8) * 256, 256), 256)],
                self.tile.at[i % 2, u], self.load.at[i, u])
            for u, side in enumerate((self.other, self.dp))
        ]

    def away(self, i):
        return remote(self.made.at[i % 2], self.land.at[i], self.send.at[i], self.recv.at[i],
                      (self.other, self.e))

    def fetch(self, i):
        return pltpu.make_async_copy(self.land.at[i], self.got, self.back.at[i])

    def stores(self, i):
        if i < 8:
            at = pl.ds(i * 256, 256)
            return [pltpu.make_async_copy(self.done_gu.at[i % 2, u], out.at[0, at],
                                          self.store.at[i, u])
                    for u, out in enumerate((self.out_gate, self.out_up))]
        return [pltpu.make_async_copy(self.done_d.at[i % 2],
                                      self.out_down.at[0, :, pl.ds((i - 8) * 256, 256)],
                                      self.store.at[i, 0])]

    def begin(self):
        for copy in self.fill:
            copy.start()
        for copy in self.loads(0):
            copy.start()

    def finish(self, i):
        self.fetch(i).wait()
        if i >= 2 and (i < 8 or i >= 10):
            for copy in self.stores(i - 2):
                copy.wait()
        slot = i % 2
        total = self.mine[slot].astype(jnp.float32) + self.got[...].astype(jnp.float32)
        if i < 8:
            total = total.astype(jnp.bfloat16)
            self.done_gu[slot, 0] = total[:, : FF // 2]
            self.done_gu[slot, 1] = total[:, FF // 2 :]
        else:
            self.done_d[slot] = jnp.transpose(total).astype(jnp.bfloat16)
        for copy in self.stores(i):
            copy.start()

    def job(self):
        i = self.next
        self.next += 1
        if i > self.JOBS:
            return
        if 0 < i:
            self.away(i - 1).wait_recv()
            self.fetch(i - 1).start()
        if i < self.JOBS:
            slot = i % 2
            if i == 0:
                self.fill[0].wait()
            if i == 8:
                self.fill[1].wait()
            for copy in self.loads(i):
                copy.wait()
            if i + 1 < self.JOBS:
                for copy in self.loads(i + 1):
                    copy.start()
            if i >= 2:
                self.away(i - 2).wait_send()
            def product(u, side):
                rows = self.tile[slot, 0 if i < 8 else u]
                right = self.grads[side] if i < 8 else self.hid[...]
                return contract_rows(rows, right).astype(jnp.bfloat16)

            self.made[slot] = product(0, self.other)
            self.away(i).start()
            self.mine[slot] = product(1, self.dp)
        if 0 < i:
            self.finish(i - 1)

    def end(self):
        while self.next <= self.JOBS:
            self.job()
        for i in (10, 11):
            self.away(i).wait_send()
        for i in (6, 7, 10, 11):
            for copy in self.stores(i):
                copy.wait()


class Scatter:
    def __init__(self, n, sems, me, dev, part, half, near_at, far_at, add):
        self.send, self.recv = sems
        self.n, self.me, self.dev, self.add = n, me, dev, add
        self.part, self.half, self.near_at, self.far_at = part, half, near_at, far_at

    def copy(self, src, dst, at, s):
        return remote(src, dst, self.send.at[self.n, at], self.recv.at[self.n, at],
                      self.dev(step(self.me, s)))

    def near(self, s):
        u = 0 if s > 0 else 1
        return self.copy(self.part(s), self.near_at(u), u, s)

    def far(self, s):
        u = 0 if s > 0 else 1
        return self.copy(self.half(2, u), self.far_at(u), 2 + u, s)

    def first(self):
        for s in (1, -1):
            self.far(s).start()

    def second(self, s):
        u = 0 if s > 0 else 1
        self.far(s).wait_recv()
        self.add(self.half(s, u), self.far_at(u))
        self.near(s).start()

    def third(self):
        for s in (1, -1):
            self.near(s).wait_recv()

    def drain(self):
        for s in (1, -1):
            self.near(s).wait_send()
            self.far(s).wait_send()


def add_flat(to, more):
    width = to.shape[-1]

    def tile(cols):
        total = to[:, cols].astype(jnp.float32) + more[:, cols].astype(jnp.float32)
        to[:, cols] = total.astype(jnp.bfloat16)

    column_tiles(0, width, tile)


def add_lines(to, more):
    for i in range(2):
        add_flat(to.at[i], more.at[i])


def return_kernel(
    out_rows, grad_rows, tab_ref, x_rows, g_rows, hid, grads,
    mixed_ref, gtok_ref, mark_ref, out_gate, out_up, out_down, land,
    back0, back1, pick, lpart, lnear, lfar, zpart, znear, zfar,
    fpart0, fpart1, fnear0, fnear1, ffar0, ffar1, fsum0, fsum1, xnear0, xnear1, xfar0, xfar1,
    gs, gr, sa, ra, la, *weight_scratch,
):
    ways = (Way(0), Way(1))
    weights = WeightGrads(x_rows, g_rows, hid, grads, (out_gate, out_up, out_down),
                          land, weight_scratch[:8], weight_scratch[8:])
    rows_in = (out_rows, grad_rows)
    back, fpart, fnear, ffar = (back0, back1), (fpart0, fpart1), (fnear0, fnear1), (ffar0, ffar1)
    fsum, xnear, xfar = (fsum0, fsum1), (xnear0, xnear1), (xfar0, xfar1)
    tails = (D - LATE, WIDE - LATE)
    sems = (gs, gr)
    both = (0, 1)
    order = (2, 1, 3, 0)
    greet_lines()

    def piece_cols(t, piece):
        return pl.ds(*PIECES[piece]) if piece < 2 else pl.ds(LATE, tails[t])

    def home(t, kk, piece, d):
        w = ways[t]
        bs = step(w.b, kk)
        to = step(w.a, d)
        cols = piece_cols(t, piece)
        return remote(rows_in[t].at[w.block(to, bs), :, cols], back[t].at[bs, w.a, :, cols],
                      sa.at[t, kk, piece, d - 1], ra.at[t, kk, piece, d - 1],
                      w.dev(to, w.b, w.x))

    def stay(t, kk):
        w = ways[t]
        bs = step(w.b, kk)
        return pltpu.make_async_copy(rows_in[t].at[w.block(w.a, bs)], back[t].at[bs, w.a],
                                     la.at[t, kk])

    def send_home(kk):
        for t in both:
            stay(t, kk).start()
        for piece in range(3):
            for t in both:
                for d in (1, 2, 3):
                    home(t, kk, piece, d).start()

    send_home(order[0])
    weights.begin()
    count = iter(range(RINGS))

    def along_x(t, n, kk, h):
        w, cols = ways[t], pl.ds(*PIECES[h])
        at = n % 2
        return Scatter(next(count), sems, w.x, lambda i: w.dev(w.a, w.b, i),
                       lambda o: lpart.at[t, at, step(w.x, o), :, cols],
                       lambda o, u: lpart.at[t, at, step(w.x, o), pl.ds(u * 64, 64), cols],
                       lambda u: lnear.at[t, kk, u, :, cols],
                       lambda u: lfar.at[t, kk, u, :, cols], add_flat)

    def along_b(t):
        w = ways[t]
        return Scatter(next(count), sems, w.b, lambda i: w.dev(w.a, i, w.x),
                       lambda o: zpart.at[t, o % 4],
                       lambda o, u: zpart.at[t, o % 4, pl.ds(u * 64, 64)],
                       lambda u: znear.at[t, u], lambda u: zfar.at[t, u], add_flat)

    def lines_b(t):
        w = ways[t]
        return Scatter(next(count), sems, w.b, lambda i: w.dev(w.a, i, w.x),
                       lambda o: fpart[t].at[o % 4],
                       lambda o, u: fpart[t].at[o % 4, pl.ds(u * 2, 2)],
                       lambda u: fnear[t].at[u], lambda u: ffar[t].at[u], add_lines)

    def late_x(t):
        w = ways[t]
        return Scatter(next(count), sems, w.x, lambda i: w.dev(w.a, w.b, i),
                       lambda o: fsum[t].at[step(w.x, o)],
                       lambda o, u: fsum[t].at[step(w.x, o), pl.ds(u * 64, 64)],
                       lambda u: xnear[t].at[u], lambda u: xfar[t].at[u], add_flat)

    x_first = [{(kk, h): along_x(t, n, kk, h) for n, kk in enumerate(order) for h in both}
               for t in both]
    b_then = [along_b(t) for t in both]
    b_first = [lines_b(t) for t in both]
    x_then = [late_x(t) for t in both]

    def make_pick(t, kk):
        tables = tab_ref[t, step(ways[t].b, kk)]
        parts = []
        for a in range(SIDE):
            hit = hits_of(tables, a)
            weight = jnp.concatenate(lane_rows(tables, 1, a), axis=1) if t == 0 else 1.0
            parts.append(jnp.where(hit, weight, 0.0))
        pick[...] = jnp.transpose(jnp.concatenate(parts, axis=0)).astype(jnp.bfloat16)

    def sum_experts(t, n, kk, piece):
        bs = step(ways[t].b, kk)
        for d in (1, 2, 3):
            home(t, kk, piece, d).wait_recv()

        def tile(cols):
            rows = back[t][bs, :, :, cols].reshape(SIDE * GROUP, cols.size)
            sums = jnp.dot(pick[...], rows, preferred_element_type=jnp.float32).astype(jnp.bfloat16)
            sums = sums.reshape(SIDE, TOK, cols.size)
            if piece < 2:
                lpart[t, n % 2, :, :, cols] = sums
            else:
                fpart[t][kk, :, :, pl.ds(cols.start - LATE, cols.size)] = sums

        start, width = PIECES[piece] if piece < 2 else (LATE, tails[t])
        column_tiles(start, width, tile)

    def collect_x(t, n, kk):
        w = ways[t]
        for h in both:
            x_first[t][kk, h].third()

        def tile(cols):
            total = lpart[t, n % 2, w.x, :, cols].astype(jnp.float32)
            total = total + jnp.sum(lnear[t, kk, :, :, cols].astype(jnp.float32), axis=0)
            zpart[t, kk, :, cols] = total.astype(jnp.bfloat16)

        column_tiles(0, LATE, tile)
        if kk == 2:
            b_then[t].first()
        if kk in (1, 3):
            b_then[t].second(1 if kk == 1 else -1)

    for n, kk in enumerate(order):
        if n + 1 < SIDE:
            send_home(order[n + 1])
        for t in both:
            stay(t, kk).wait()
            make_pick(t, kk)
            weights.job()
            if n >= 2:
                for h in both:
                    x_first[t][order[n - 2], h].drain()
            for h in both:
                sum_experts(t, n, kk, h)
                x_first[t][kk, h].first()
            sum_experts(t, n, kk, 2)
            if kk == 2:
                b_first[t].first()
            if kk in (1, 3):
                b_first[t].second(1 if kk == 1 else -1)
        for t in both:
            for h in both:
                x_first[t][kk, h].second(1)
                x_first[t][kk, h].second(-1)
        weights.job()
        if n >= 1:
            for t in both:
                collect_x(t, n - 1, order[n - 1])

    for t in both:
        b_first[t].third()
        for i in range(SIDE):

            def tile(cols, t=t, i=i):
                total = fpart[t][0, i, :, cols].astype(jnp.float32)
                total = total + jnp.sum(fnear[t][:, i, :, cols].astype(jnp.float32), axis=0)
                fsum[t][i, :, cols] = total.astype(jnp.bfloat16)

            column_tiles(0, tails[t], tile)
        x_then[t].first()
    weights.end()
    for t in both:
        x_then[t].second(1)
        x_then[t].second(-1)
    results = (mixed_ref, gtok_ref)
    for t in both:
        collect_x(t, 3, 0)
        b_then[t].third()

        def tile(cols, t=t):
            total = zpart[t, 0, :, cols].astype(jnp.float32)
            total = total + jnp.sum(znear[t, :, :, cols].astype(jnp.float32), axis=0)
            results[t][:, cols] = total.astype(jnp.bfloat16)

        column_tiles(0, LATE, tile)
    for t in both:
        w = ways[t]
        x_then[t].third()

        def late(cols, t=t, w=w):
            total = fsum[t][w.x, :, cols].astype(jnp.float32)
            return total + jnp.sum(xnear[t][:, :, cols].astype(jnp.float32), axis=0)

        def tile(cols, t=t, late=late):
            results[t][:, pl.ds(cols.start + LATE, cols.size)] = late(cols).astype(jnp.bfloat16)

        column_tiles(0, D - LATE, tile)
        if t == 1:
            mark_ref[...] = late(pl.ds(D - LATE, 128))

    for t in both:
        for n, kk in enumerate(order):
            for piece in range(3):
                for d in (1, 2, 3):
                    home(t, kk, piece, d).wait_send()
            if n >= 2:
                for h in both:
                    x_first[t][kk, h].drain()
        b_then[t].drain()
        b_first[t].drain()
        x_then[t].drain()


def bring_back(out_rows, grad_rows, tables, x_rows, g_rows, hid, grads):
    dma = pltpu.SemaphoreType.DMA
    vmem = pl.BlockSpec(memory_space=pltpu.VMEM)
    hbm = pl.BlockSpec(memory_space=pl.ANY)
    buf = lambda *shape: pltpu.VMEM(shape, jnp.bfloat16)
    pair = lambda *lead: [buf(*lead, D - LATE), buf(*lead, WIDE - LATE)]
    return pl.pallas_call(
        return_kernel,
        name="bring_back",
        out_shape=(
            jax.ShapeDtypeStruct((TOK, D), jnp.bfloat16),
            jax.ShapeDtypeStruct((TOK, D), jnp.bfloat16),
            jax.ShapeDtypeStruct((TOK, 128), jnp.float32),
            jax.ShapeDtypeStruct((1, D, FF // 2), jnp.bfloat16),
            jax.ShapeDtypeStruct((1, D, FF // 2), jnp.bfloat16),
            jax.ShapeDtypeStruct((1, FF, D // 2), jnp.bfloat16),
            jax.ShapeDtypeStruct((WeightGrads.JOBS, 256, FF), jnp.bfloat16),
        ),
        in_specs=[hbm, hbm, vmem, hbm, hbm, hbm, hbm],
        out_specs=(vmem, vmem, vmem, hbm, hbm, hbm, hbm),
        scratch_shapes=[
            buf(SIDE, SIDE, GROUP, D), buf(SIDE, SIDE, GROUP, WIDE),
            buf(SIDE * TOK, SIDE * GROUP),
            buf(2, 2, SIDE, TOK, LATE), buf(2, SIDE, 2, TOK, LATE), buf(2, SIDE, 2, TOK // 2, LATE),
            buf(2, SIDE, TOK, LATE), buf(2, 2, TOK, LATE), buf(2, 2, TOK // 2, LATE),
            *pair(SIDE, SIDE, TOK), *pair(2, SIDE, TOK), *pair(2, 2, TOK),
            *pair(SIDE, TOK), *pair(2, TOK), *pair(2, TOK // 2),
            dma((RINGS, 4)), dma((RINGS, 4)),
            dma((2, SIDE, 3, 3)), dma((2, SIDE, 3, 3)),
            dma((2, SIDE)),
            buf(2, ROWS, FF), buf(ROWS, FF), buf(2, 2, ROWS, 256),
            buf(2, 256, FF), buf(2, 256, FF), buf(256, FF), buf(2, 2, 256, FF // 2),
            buf(2, FF, 256),
            dma((12, 2)), dma((12,)), dma((12,)), dma((12,)), dma((12, 2)), dma((2,)),
        ],
        compiler_params=pltpu.CompilerParams(
            collective_id=3, has_side_effects=True, vmem_limit_bytes=VMEM_LIMIT
        ),
    )(out_rows, grad_rows, tables, x_rows, g_rows, hid, grads)


def body(tokens, route_ids, route_probs, cotangent, w_gate, w_up, w_down):
    x_rows, g_rows, tables, out_rows, grad_rows, hidden, grads = dispatch(
        route_ids.T, route_probs.T, tokens, cotangent, w_gate, w_up, w_down
    )
    mixed, grad_tokens, marks, grad_gate, grad_up, grad_down, _ = bring_back(
        out_rows, grad_rows, tables, x_rows.reshape(ROWS, D), g_rows.reshape(ROWS, D),
        hidden.reshape(ROWS, FF), grads.reshape(2, ROWS, FF),
    )
    product = marks[:, :EXPERTS] + marks[:, EXPERTS:]
    chosen = route_ids[:, :, None] == jnp.arange(EXPERTS, dtype=jnp.int32)[None, None, :]
    grad_probs = jnp.sum(jnp.where(chosen, product[:, None, :], 0.0), axis=2) / route_probs
    return (mixed, grad_tokens, grad_probs, grad_gate, grad_up, grad_down)


def solution(mesh):
    both = P(("dp", "expert"), None)
    mine = P("expert", None, None)
    split = P("expert", None, "dp")
    return jax.shard_map(
        body,
        mesh=mesh,
        in_specs=(both, both, both, both, mine, mine, mine),
        out_specs=(both, both, both, split, split, split),
        check_vma=False,
    )
```

```python
import functools

import jax
import jax.numpy as jnp
from jax import lax
from jax.experimental import pallas as pl
from jax.experimental.pallas import tpu as pltpu
from jax.sharding import PartitionSpec as P

D = 2048
FF = 768
TOP = 8
TOK = 128
CAP = 28
SIDE = 4
EXPERTS = 64
GROUP = SIDE * CAP
ROWS = 16 * GROUP
WIDE = D + 128
LATE = 1536
PIECES = ((0, 768), (768, 768), (1536, 512))
RINGS = 24
TURN_ORDER = "0101010101010011"
START_AHEAD = 4
PASS_AHEAD = 2
EXPERTS_AFTER = (9, 15, 15, 15)
MESH = pl.DeviceIdType.MESH
VMEM_LIMIT = 63 * 1024 * 1024


def where_am_i():
    e = lax.axis_index("expert")
    return lax.axis_index("dp"), e // 16, (e // 4) % 4, e % 4


class Way:
    def __init__(self, t):
        self.t = t
        self.dp, z, self.x, y = where_am_i()
        self.a, self.b = (y, z) if t == 0 else (z, y)

    def dev(self, a, b, x):
        z, y = (b, a) if self.t == 0 else (a, b)
        return (self.dp, z * 16 + x * 4 + y)

    def block(self, a, b):
        return a * 4 + b if self.t == 0 else b * 4 + a


def step(v, d):
    return lax.rem(v + d + SIDE, SIDE)


def greet_lines():
    dp, z, x, y = where_am_i()
    barrier = pltpu.get_barrier_semaphore()
    for d in (1, 2, 3):
        for to in (
            step(z, d) * 16 + x * 4 + y,
            z * 16 + step(x, d) * 4 + y,
            z * 16 + x * 4 + step(y, d),
        ):
            pl.semaphore_signal(barrier, inc=1, device_id=(dp, to), device_id_type=MESH)
    pl.semaphore_signal(barrier, inc=1, device_id=(1 - dp, z * 16 + x * 4 + y), device_id_type=MESH)
    pl.semaphore_wait(barrier, 10)


def remote(src, dst, send, recv, dev):
    return pltpu.make_async_remote_copy(
        src_ref=src, dst_ref=dst, send_sem=send, recv_sem=recv, device_id=dev, device_id_type=MESH
    )


def own_table(t, ids_ref, probs_ref):
    row = lax.broadcasted_iota(jnp.int32, (TOK, TOK), 0)
    b, x, kind, a = row // 32, (row // 8) % 4, (row // 4) % 2, row % 4
    expert = b * 16 + x * 4 + a if t == 0 else a * 16 + x * 4 + b
    hit = jnp.zeros((TOK, TOK), jnp.float32)
    weight = jnp.zeros((TOK, TOK), jnp.float32)
    for k in range(TOP):
        same = expert == ids_ref[k : k + 1, :]
        hit = jnp.where(same, 1.0, hit)
        weight = jnp.where(same, probs_ref[k : k + 1, :], weight)
    before = lax.broadcasted_iota(jnp.int32, (TOK, TOK), 0) < lax.broadcasted_iota(
        jnp.int32, (TOK, TOK), 1
    )
    before = jnp.where(before, 1.0, 0.0).astype(jnp.bfloat16)
    slot = jnp.dot(hit.astype(jnp.bfloat16), before, preferred_element_type=jnp.float32)
    slot = jnp.where(hit > 0.5, slot, -1000.0)
    return jnp.where(kind == 0, slot, weight)


def lane_rows(tables, kind, a):
    return [tables[xs, kind * 4 + a : kind * 4 + a + 1, :] for xs in range(SIDE)]


def hits_of(tables, a):
    slots = jnp.concatenate(
        [v + float(CAP * xs) for xs, v in enumerate(lane_rows(tables, 0, a))], axis=1
    )
    row = lax.broadcasted_iota(jnp.int32, (GROUP, SIDE * TOK), 0).astype(jnp.float32)
    return row == slots


class Gather:
    def __init__(self, n, sems, me, dev, block, half):
        self.send, self.recv = sems
        self.n, self.me, self.dev, self.block, self.half = n, me, dev, block, half

    def copy(self, ref, at, s):
        return remote(ref, ref, self.send.at[self.n, at], self.recv.at[self.n, at],
                      self.dev(step(self.me, s)))

    def near(self, s):
        return self.copy(self.block(self.me), 0 if s > 0 else 1, s)

    def far(self, s):
        return self.copy(self.half(step(self.me, -s), 0 if s > 0 else 1), 2 if s > 0 else 3, s)

    def start(self):
        for s in (1, -1):
            self.near(s).start()

    def pass_on(self):
        for s in (1, -1):
            self.near(s).wait_recv()
            self.far(s).start()

    def finish(self):
        for s in (1, -1):
            self.far(s).wait_recv()

    def drain(self):
        for s in (1, -1):
            self.near(s).wait_send()
            self.far(s).wait_send()


def column_tiles(start, width, tile):
    def one(c, _):
        tile(pl.ds(pl.multiple_of(start + c * 256, 128), 256))
        return 0

    lax.fori_loop(0, width // 256, one, 0)
    if width % 256:
        tile(pl.ds(start + width // 256 * 256, width % 256))


def dispatch_kernel(
    ids_ref, probs_ref, tok_ref, cot_ref, w_gate, w_up, w_down,
    x_rows, g_rows, tab_out, out_rows, grad_rows, hid_rows, gu_rows,
    gath, stage, own_tab, tab_a, tab_b, pick, scale,
    x_here, g_here, wg, wu, wd, out_st, grad_st, hid_st, gu_st,
    gs, gr, s3, r3, ts1, tr1, ts2, tr2, ls, wsem, xsem, osem,
):
    ways = (Way(0), Way(1))
    rows_out = (x_here, g_here)
    sems = (gs, gr)
    weight_loads = [pltpu.make_async_copy(src.at[0], dst, wsem.at[n])
                    for n, (src, dst) in enumerate(((w_gate, wg), (w_up, wu), (w_down, wd)))]
    for copy in weight_loads:
        copy.start()

    for t, src in ((0, tok_ref), (1, cot_ref)):
        w = ways[t]
        own_tab[t] = own_table(t, ids_ref, probs_ref).reshape(16, 8, TOK)
        gath[t, w.b, w.x] = src[...]
        tab_a[t, w.b] = own_tab[t, pl.ds(w.b * 4, 4)]
    greet_lines()

    count = iter(range(RINGS))

    def along_b(t, piece):
        w, cols = ways[t], pl.ds(*PIECES[piece])
        return Gather(next(count), sems, w.b, lambda i: w.dev(w.a, i, w.x),
                      lambda i: gath.at[t, i, w.x, :, cols],
                      lambda i, u: gath.at[t, i, w.x, pl.ds(u * 64, 64), cols])

    def along_x(t, kk, piece):
        w, cols = ways[t], pl.ds(*PIECES[piece])
        bs = step(w.b, -kk)
        return Gather(next(count), sems, w.x, lambda i: w.dev(w.a, w.b, i),
                      lambda i: gath.at[t, bs, i, :, cols],
                      lambda i, u: gath.at[t, bs, i, pl.ds(u * 64, 64), cols])

    def lines_b(t):
        w, cols = ways[t], pl.ds(*PIECES[2])
        return Gather(next(count), sems, w.b, lambda i: w.dev(w.a, i, w.x),
                      lambda i: gath.at[t, i, :, :, cols],
                      lambda i, u: gath.at[t, i, pl.ds(u * 2, 2), :, cols])

    both = (0, 1)
    order = (0, 1, 3, 2)
    slot_of = lambda kk: order.index(kk) % 2
    b_first = [[along_b(t, h) for h in both] for t in both]
    x_then = [{(kk, h): along_x(t, kk, h) for kk in range(SIDE) for h in both} for t in both]
    x_first = [along_x(t, 0, 2) for t in both]
    b_then = [lines_b(t) for t in both]

    def first_tab(t, d):
        w = ways[t]
        to = step(w.b, d)
        return remote(own_tab.at[t, pl.ds(to * 4, 4)], tab_a.at[t, w.b],
                      ts1.at[t, d - 1], tr1.at[t, d - 1], w.dev(w.a, to, w.x))

    def second_tab(t, kk, d):
        w = ways[t]
        bs = step(w.b, -kk)
        to = step(w.x, d)
        return remote(tab_a.at[t, bs, to], tab_b.at[t, bs, w.x],
                      ts2.at[t, kk, d - 1], tr2.at[t, kk, d - 1], w.dev(w.a, w.b, to))

    def third(t, kk, piece, d):
        w = ways[t]
        bs = step(w.b, -kk)
        to = step(w.a, d)
        cols = pl.ds(*PIECES[piece])
        return remote(stage.at[t, slot_of(kk), to, :, cols],
                      rows_out[t].at[w.block(w.a, bs), :, cols],
                      s3.at[t, kk, piece, d - 1], r3.at[t, kk, piece, d - 1],
                      w.dev(to, w.b, w.x))

    def kept(t, kk, piece):
        w = ways[t]
        bs = step(w.b, -kk)
        cols = pl.ds(*PIECES[piece])
        return pltpu.make_async_copy(stage.at[t, slot_of(kk), w.a, :, cols],
                                     rows_out[t].at[w.block(w.a, bs), :, cols],
                                     ls.at[t, kk, piece])

    def share_tab(t, kk):
        w = ways[t]
        bs = step(w.b, -kk)
        if kk > 0:
            first_tab(t, kk).wait_recv()
        tab_b[t, bs, w.x] = tab_a[t, bs, w.x]
        for d in (1, 2, 3):
            second_tab(t, kk, d).start()

    def make_pick(t, kk):
        for d in (1, 2, 3):
            second_tab(t, kk, d).wait_recv()
        tables = tab_b[t, step(ways[t].b, -kk)]
        for a in range(SIDE):
            at = slice(a * GROUP, (a + 1) * GROUP)
            hit = hits_of(tables, a)
            pick[t, at, :] = jnp.where(hit, 1.0, 0.0).astype(jnp.bfloat16)
            if t == 1:
                weight = jnp.concatenate(lane_rows(tables, 1, a), axis=1)
                weight = jnp.sum(jnp.where(hit, weight, 0.0), axis=1, keepdims=True)
                scale[at, :] = jnp.broadcast_to(weight, (GROUP, 128))

    def send_rows(t, kk, piece):
        bs = step(ways[t].b, -kk)

        def tile(cols):
            block = gath[t, bs, :, :, cols].reshape(SIDE * TOK, cols.size)
            rows = jnp.dot(pick[t], block, preferred_element_type=jnp.float32)
            if t == 1:
                rows = rows * jnp.concatenate([scale[...]] * (cols.size // 128), axis=1)
            stage[t, slot_of(kk), :, :, cols] = rows.astype(jnp.bfloat16).reshape(SIDE, GROUP, cols.size)

        if order.index(kk) >= 2:
            leave(t, order[order.index(kk) - 2], piece)
        column_tiles(*PIECES[piece], tile)
        for d in (1, 2, 3):
            third(t, kk, piece, d).start()
        kept(t, kk, piece).start()

    settled = set()

    def settle(t, kk, piece):
        if (t, kk, piece) not in settled:
            settled.add((t, kk, piece))
            kept(t, kk, piece).wait()

    def leave(t, kk, piece):
        for d in (1, 2, 3):
            third(t, kk, piece, d).wait_send()
        settle(t, kk, piece)

    def arrive(t, kk):
        for piece in range(3):
            for d in (1, 2, 3):
                third(t, kk, piece, d).wait_recv()
            settle(t, kk, piece)

    dp, z, x, y = where_am_i()
    kept_rows = [pltpu.make_async_copy(here, rows, xsem.at[n])
                 for n, (here, rows) in enumerate(((x_here, x_rows), (g_here, g_rows)))]

    def results(blocks):
        copies = []
        for u, at in enumerate(blocks):
            pairs = ((out_st.at[u], out_rows.at[at]), (grad_st.at[u], grad_rows.at[at]),
                     (hid_st.at[u], hid_rows.at[at]), (gu_st.at[:, u], gu_rows.at[:, at]))
            copies += [pltpu.make_async_copy(src, dst, osem.at[u, n])
                       for n, (src, dst) in enumerate(pairs)]
        return copies

    def block_of(m_y, m_z):
        turn = lambda m: m + m // 2 - 2 * (m // 3)
        return step(y, -turn(m_y)) * 4 + step(z, -turn(m_z))

    def experts(m):
        if m == 1:
            for copy in weight_loads:
                copy.wait()
        needs = {
            1: [(t, k2) for k2 in order[:2] for t in both],
            2: [(t, order[2]) for t in both],
            3: [(0, order[3])],
            4: [(1, order[3])],
        }
        for t, k2 in needs[m]:
            arrive(t, k2)
        if m >= 3:
            kept_rows[m - 3].start()
        many = 2 * GROUP

        def some(p, _):
            if m == 1:
                blocks = (block_of(0, 1 - p), block_of(1, p))
            elif m == 2:
                blocks = (block_of(p, 2), block_of(2, p))
            elif m == 3:
                blocks = (block_of(2 * p, 3), block_of(1 + p, 3 - p))
            else:
                blocks = (block_of(3, 2 * p), block_of(3, 2 * p + 1))
            rows = jnp.concatenate([x_here[at] for at in blocks], axis=0)
            gate_pre = jnp.dot(rows, wg[...], preferred_element_type=jnp.float32)
            up_pre = jnp.dot(rows, wu[...], preferred_element_type=jnp.float32)
            sigmoid = jax.nn.sigmoid(gate_pre)
            activation = gate_pre * sigmoid
            derivative = sigmoid * (1.0 + gate_pre * (1.0 - sigmoid))
            hidden = (activation * up_pre).astype(jnp.bfloat16)

            def settle_results():
                for copy in results(blocks):
                    copy.wait()

            if m == 1:
                pl.when(p > 0)(settle_results)
            else:
                settle_results()
            hid_st[...] = hidden.reshape(2, GROUP, FF)
            out = jnp.dot(hidden, wd[...], preferred_element_type=jnp.float32)
            out_st[...] = out.astype(jnp.bfloat16).reshape(2, GROUP, D)
            grads = jnp.concatenate([g_here[at] for at in blocks], axis=0)
            grad_hidden = contract_last(grads, wd[...])
            gate_grad = (grad_hidden * up_pre * derivative).astype(jnp.bfloat16)
            up_grad = (grad_hidden * activation).astype(jnp.bfloat16)
            for half in range(2):
                cols = slice(half * FF // 2, (half + 1) * FF // 2)
                gu_st[half, :, :, : FF // 2] = gate_grad[:, cols].reshape(2, GROUP, FF // 2)
                gu_st[half, :, :, FF // 2 :] = up_grad[:, cols].reshape(2, GROUP, FF // 2)
            grad = contract_last(gate_grad, wg[...]) + contract_last(up_grad, wu[...])
            grad_st[:, :, :D] = grad.astype(jnp.bfloat16).reshape(2, GROUP, D)
            product = jnp.sum(hidden.astype(jnp.float32) * grad_hidden, axis=1, keepdims=True)
            high = product.astype(jnp.bfloat16).astype(jnp.float32)
            low = product - high
            lane = lax.broadcasted_iota(jnp.int32, (many, 128), 1)
            me = lax.axis_index("expert")
            marks = jnp.where(lane == me, high, 0.0)
            marks = jnp.where(lane == me + EXPERTS, low, marks)
            grad_st[:, :, D:] = marks.astype(jnp.bfloat16).reshape(2, GROUP, 128)
            for copy in results(blocks):
                copy.start()
            return 0

        lax.fori_loop(0, 2, some, 0)
        if m == 4:
            for copy in results((0, 1)):
                copy.wait()
            for copy in kept_rows:
                copy.wait()

    turns = [[(t, kk, h) for kk in order for h in both] for t in both]
    plan = []
    for c in TURN_ORDER:
        plan.append(turns[int(c)].pop(0))
    begun = {(t, 0, h) for t in both for h in both}
    passed = {(t, 0, 0) for t in both}

    def begin(t, kk, h):
        if (t, kk, h) in begun:
            return
        begun.add((t, kk, h))
        if kk == 2:
            b_first[t][h].finish()
        if h == 0 and kk != 0:
            share_tab(t, kk)
        x_then[t][kk, h].start()

    def pass_on(t, kk, h):
        if (t, kk, h) not in passed:
            passed.add((t, kk, h))
            x_then[t][kk, h].pass_on()

    for t in both:
        for d in (1, 2, 3):
            first_tab(t, d).start()
        share_tab(t, 0)
        x_first[t].start()
    for h in both:
        for t in both:
            x_then[t][0, h].start()
        for t in both:
            b_first[t][h].start()
    for t in both:
        x_first[t].pass_on()
    for t in both:
        x_then[t][0, 0].pass_on()
    for t in both:
        b_first[t][0].pass_on()
    for t in both:
        x_first[t].finish()
        b_then[t].start()
    for t in both:
        b_first[t][1].pass_on()
    for n, (t, kk, h) in enumerate(plan):
        if n + START_AHEAD < len(plan):
            begin(*plan[n + START_AHEAD])
        for item in plan[: n + PASS_AHEAD + 1]:
            pass_on(*item)
        x_then[t][kk, h].finish()
        if h == 0:
            make_pick(t, kk)
        send_rows(t, kk, h)
        if h == 1:
            if kk == 1:
                b_then[t].pass_on()
            if kk == 2:
                b_then[t].finish()
            send_rows(t, kk, 2)
        for m, after in enumerate(EXPERTS_AFTER):
            if after == n:
                experts(m + 1)

    tab_out[...] = tab_b[...]
    for t in both:
        for kk in range(SIDE):
            for d in (1, 2, 3):
                second_tab(t, kk, d).wait_send()
                if kk in order[2:]:
                    for piece in range(3):
                        third(t, kk, piece, d).wait_send()
        for d in (1, 2, 3):
            first_tab(t, d).wait_send()
        for ring in (*b_first[t], *x_then[t].values(), x_first[t], b_then[t]):
            ring.drain()


def dispatch(ids_t, probs_t, tokens, cotangent, w_gate, w_up, w_down):
    dma = pltpu.SemaphoreType.DMA
    vmem = pl.BlockSpec(memory_space=pltpu.VMEM)
    hbm = pl.BlockSpec(memory_space=pl.ANY)
    buf = lambda *shape: pltpu.VMEM(shape, jnp.bfloat16)
    return pl.pallas_call(
        dispatch_kernel,
        name="dispatch",
        out_shape=(
            jax.ShapeDtypeStruct((16, GROUP, D), jnp.bfloat16),
            jax.ShapeDtypeStruct((16, GROUP, D), jnp.bfloat16),
            jax.ShapeDtypeStruct((2, SIDE, SIDE, 8, TOK), jnp.float32),
            jax.ShapeDtypeStruct((16, GROUP, D), jnp.bfloat16),
            jax.ShapeDtypeStruct((16, GROUP, WIDE), jnp.bfloat16),
            jax.ShapeDtypeStruct((16, GROUP, FF), jnp.bfloat16),
            jax.ShapeDtypeStruct((2, 16, GROUP, FF), jnp.bfloat16),
        ),
        in_specs=[vmem] * 4 + [hbm] * 3,
        out_specs=(hbm, hbm, vmem, hbm, hbm, hbm, hbm),
        scratch_shapes=[
            pltpu.VMEM((2, SIDE, SIDE, TOK, D), jnp.bfloat16),
            pltpu.VMEM((2, 2, SIDE, GROUP, D), jnp.bfloat16),
            pltpu.VMEM((2, 16, 8, TOK), jnp.float32),
            pltpu.VMEM((2, SIDE, SIDE, 8, TOK), jnp.float32),
            pltpu.VMEM((2, SIDE, SIDE, 8, TOK), jnp.float32),
            pltpu.VMEM((2, SIDE * GROUP, SIDE * TOK), jnp.bfloat16),
            pltpu.VMEM((SIDE * GROUP, 128), jnp.float32),
            buf(16, GROUP, D), buf(16, GROUP, D), buf(D, FF), buf(D, FF), buf(FF, D),
            buf(2, GROUP, D), buf(2, GROUP, WIDE), buf(2, GROUP, FF), buf(2, 2, GROUP, FF),
            dma((RINGS, 4)), dma((RINGS, 4)),
            dma((2, SIDE, 3, 3)), dma((2, SIDE, 3, 3)),
            dma((2, 3)), dma((2, 3)),
            dma((2, SIDE, 3)), dma((2, SIDE, 3)),
            dma((2, SIDE, 3)), dma((3,)), dma((2,)), dma((2, 4)),
        ],
        compiler_params=pltpu.CompilerParams(
            collective_id=1, has_side_effects=True, vmem_limit_bytes=VMEM_LIMIT
        ),
    )(ids_t, probs_t, tokens, cotangent, w_gate, w_up, w_down)


def contract_last(left_side, right_side):
    return lax.dot_general(
        left_side, right_side, (((1,), (1,)), ((), ())), preferred_element_type=jnp.float32
    )


def contract_rows(left_side, right_side):
    return lax.dot_general(
        left_side, right_side, (((0,), (0,)), ((), ())), preferred_element_type=jnp.float32
    )


class WeightGrads:
    JOBS = 12

    def __init__(self, x_rows, g_rows, hid, grads, outs, lands, bufs, sems):
        self.x_rows, self.g_rows = x_rows, g_rows
        self.out_gate, self.out_up, self.out_down = outs
        self.land = lands
        (self.grads, self.hid, self.tile, self.made, self.mine, self.got, self.done_gu,
         self.done_d) = bufs
        self.load, self.send, self.recv, self.back, self.store, self.whole = sems
        self.dp, self.e = lax.axis_index("dp"), lax.axis_index("expert")
        self.other = 1 - self.dp
        self.next = 0
        self.fill = (pltpu.make_async_copy(grads, self.grads, self.whole.at[0]),
                     pltpu.make_async_copy(hid, self.hid, self.whole.at[1]))

    def loads(self, i):
        if i < 8:
            cols = pl.ds(i * 256, 256)
            return [pltpu.make_async_copy(self.x_rows.at[:, cols], self.tile.at[i % 2, 0],
                                          self.load.at[i, 0])]
        return [
            pltpu.make_async_copy(
                self.g_rows.at[:, pl.ds(pl.multiple_of(side * (D // 2) + (i - 8) * 256, 256), 256)],
                self.tile.at[i % 2, u], self.load.at[i, u])
            for u, side in enumerate((self.other, self.dp))
        ]

    def away(self, i):
        return remote(self.made.at[i % 2], self.land.at[i], self.send.at[i], self.recv.at[i],
                      (self.other, self.e))

    def fetch(self, i):
        return pltpu.make_async_copy(self.land.at[i], self.got, self.back.at[i])

    def stores(self, i):
        if i < 8:
            at = pl.ds(i * 256, 256)
            return [pltpu.make_async_copy(self.done_gu.at[i % 2, u], out.at[0, at],
                                          self.store.at[i, u])
                    for u, out in enumerate((self.out_gate, self.out_up))]
        return [pltpu.make_async_copy(self.done_d.at[i % 2],
                                      self.out_down.at[0, :, pl.ds((i - 8) * 256, 256)],
                                      self.store.at[i, 0])]

    def begin(self):
        for copy in self.fill:
            copy.start()
        for copy in self.loads(0):
            copy.start()

    def finish(self, i):
        self.fetch(i).wait()
        if i >= 2 and (i < 8 or i >= 10):
            for copy in self.stores(i - 2):
                copy.wait()
        slot = i % 2
        total = self.mine[slot].astype(jnp.float32) + self.got[...].astype(jnp.float32)
        if i < 8:
            total = total.astype(jnp.bfloat16)
            self.done_gu[slot, 0] = total[:, : FF // 2]
            self.done_gu[slot, 1] = total[:, FF // 2 :]
        else:
            self.done_d[slot] = jnp.transpose(total).astype(jnp.bfloat16)
        for copy in self.stores(i):
            copy.start()

    def job(self):
        i = self.next
        self.next += 1
        if i > self.JOBS:
            return
        if 0 < i:
            self.away(i - 1).wait_recv()
            self.fetch(i - 1).start()
        if i < self.JOBS:
            slot = i % 2
            if i == 0:
                self.fill[0].wait()
            if i == 8:
                self.fill[1].wait()
            for copy in self.loads(i):
                copy.wait()
            if i + 1 < self.JOBS:
                for copy in self.loads(i + 1):
                    copy.start()
            if i >= 2:
                self.away(i - 2).wait_send()
            def product(u, side):
                rows = self.tile[slot, 0 if i < 8 else u]
                right = self.grads[side] if i < 8 else self.hid[...]
                return contract_rows(rows, right).astype(jnp.bfloat16)

            self.made[slot] = product(0, self.other)
            self.away(i).start()
            self.mine[slot] = product(1, self.dp)
        if 0 < i:
            self.finish(i - 1)

    def end(self):
        while self.next <= self.JOBS:
            self.job()
        for i in (10, 11):
            self.away(i).wait_send()
        for i in (6, 7, 10, 11):
            for copy in self.stores(i):
                copy.wait()


class Scatter:
    def __init__(self, n, sems, me, dev, part, half, near_at, far_at, add):
        self.send, self.recv = sems
        self.n, self.me, self.dev, self.add = n, me, dev, add
        self.part, self.half, self.near_at, self.far_at = part, half, near_at, far_at

    def copy(self, src, dst, at, s):
        return remote(src, dst, self.send.at[self.n, at], self.recv.at[self.n, at],
                      self.dev(step(self.me, s)))

    def near(self, s):
        u = 0 if s > 0 else 1
        return self.copy(self.part(s), self.near_at(u), u, s)

    def far(self, s):
        u = 0 if s > 0 else 1
        return self.copy(self.half(2, u), self.far_at(u), 2 + u, s)

    def first(self):
        for s in (1, -1):
            self.far(s).start()

    def second(self, s):
        u = 0 if s > 0 else 1
        self.far(s).wait_recv()
        self.add(self.half(s, u), self.far_at(u))
        self.near(s).start()

    def third(self):
        for s in (1, -1):
            self.near(s).wait_recv()

    def drain(self):
        for s in (1, -1):
            self.near(s).wait_send()
            self.far(s).wait_send()


def add_flat(to, more):
    width = to.shape[-1]

    def tile(cols):
        total = to[:, cols].astype(jnp.float32) + more[:, cols].astype(jnp.float32)
        to[:, cols] = total.astype(jnp.bfloat16)

    column_tiles(0, width, tile)


def add_lines(to, more):
    for i in range(2):
        add_flat(to.at[i], more.at[i])


def return_kernel(
    out_rows, grad_rows, tab_ref, x_rows, g_rows, hid, grads,
    mixed_ref, gtok_ref, mark_ref, out_gate, out_up, out_down, land,
    back0, back1, pick, lpart, lnear, lfar, zpart, znear, zfar,
    fpart0, fpart1, fnear0, fnear1, ffar0, ffar1, fsum0, fsum1, xnear0, xnear1, xfar0, xfar1,
    gs, gr, sa, ra, la, *weight_scratch,
):
    ways = (Way(0), Way(1))
    weights = WeightGrads(x_rows, g_rows, hid, grads, (out_gate, out_up, out_down),
                          land, weight_scratch[:8], weight_scratch[8:])
    rows_in = (out_rows, grad_rows)
    back, fpart, fnear, ffar = (back0, back1), (fpart0, fpart1), (fnear0, fnear1), (ffar0, ffar1)
    fsum, xnear, xfar = (fsum0, fsum1), (xnear0, xnear1), (xfar0, xfar1)
    tails = (D - LATE, WIDE - LATE)
    sems = (gs, gr)
    both = (0, 1)
    order = (2, 1, 3, 0)
    greet_lines()

    def piece_cols(t, piece):
        return pl.ds(*PIECES[piece]) if piece < 2 else pl.ds(LATE, tails[t])

    def home(t, kk, piece, d):
        w = ways[t]
        bs = step(w.b, kk)
        to = step(w.a, d)
        cols = piece_cols(t, piece)
        return remote(rows_in[t].at[w.block(to, bs), :, cols], back[t].at[bs, w.a, :, cols],
                      sa.at[t, kk, piece, d - 1], ra.at[t, kk, piece, d - 1],
                      w.dev(to, w.b, w.x))

    def stay(t, kk):
        w = ways[t]
        bs = step(w.b, kk)
        return pltpu.make_async_copy(rows_in[t].at[w.block(w.a, bs)], back[t].at[bs, w.a],
                                     la.at[t, kk])

    def send_home(kk):
        for t in both:
            stay(t, kk).start()
        for piece in range(3):
            for t in both:
                for d in (1, 2, 3):
                    home(t, kk, piece, d).start()

    send_home(order[0])
    weights.begin()
    count = iter(range(RINGS))

    def along_x(t, n, kk, h):
        w, cols = ways[t], pl.ds(*PIECES[h])
        at = n % 2
        return Scatter(next(count), sems, w.x, lambda i: w.dev(w.a, w.b, i),
                       lambda o: lpart.at[t, at, step(w.x, o), :, cols],
                       lambda o, u: lpart.at[t, at, step(w.x, o), pl.ds(u * 64, 64), cols],
                       lambda u: lnear.at[t, kk, u, :, cols],
                       lambda u: lfar.at[t, kk, u, :, cols], add_flat)

    def along_b(t):
        w = ways[t]
        return Scatter(next(count), sems, w.b, lambda i: w.dev(w.a, i, w.x),
                       lambda o: zpart.at[t, o % 4],
                       lambda o, u: zpart.at[t, o % 4, pl.ds(u * 64, 64)],
                       lambda u: znear.at[t, u], lambda u: zfar.at[t, u], add_flat)

    def lines_b(t):
        w = ways[t]
        return Scatter(next(count), sems, w.b, lambda i: w.dev(w.a, i, w.x),
                       lambda o: fpart[t].at[o % 4],
                       lambda o, u: fpart[t].at[o % 4, pl.ds(u * 2, 2)],
                       lambda u: fnear[t].at[u], lambda u: ffar[t].at[u], add_lines)

    def late_x(t):
        w = ways[t]
        return Scatter(next(count), sems, w.x, lambda i: w.dev(w.a, w.b, i),
                       lambda o: fsum[t].at[step(w.x, o)],
                       lambda o, u: fsum[t].at[step(w.x, o), pl.ds(u * 64, 64)],
                       lambda u: xnear[t].at[u], lambda u: xfar[t].at[u], add_flat)

    x_first = [{(kk, h): along_x(t, n, kk, h) for n, kk in enumerate(order) for h in both}
               for t in both]
    b_then = [along_b(t) for t in both]
    b_first = [lines_b(t) for t in both]
    x_then = [late_x(t) for t in both]

    def make_pick(t, kk):
        tables = tab_ref[t, step(ways[t].b, kk)]
        parts = []
        for a in range(SIDE):
            hit = hits_of(tables, a)
            weight = jnp.concatenate(lane_rows(tables, 1, a), axis=1) if t == 0 else 1.0
            parts.append(jnp.where(hit, weight, 0.0))
        pick[...] = jnp.transpose(jnp.concatenate(parts, axis=0)).astype(jnp.bfloat16)

    def sum_experts(t, n, kk, piece):
        bs = step(ways[t].b, kk)
        for d in (1, 2, 3):
            home(t, kk, piece, d).wait_recv()

        def tile(cols):
            rows = back[t][bs, :, :, cols].reshape(SIDE * GROUP, cols.size)
            sums = jnp.dot(pick[...], rows, preferred_element_type=jnp.float32).astype(jnp.bfloat16)
            sums = sums.reshape(SIDE, TOK, cols.size)
            if piece < 2:
                lpart[t, n % 2, :, :, cols] = sums
            else:
                fpart[t][kk, :, :, pl.ds(cols.start - LATE, cols.size)] = sums

        start, width = PIECES[piece] if piece < 2 else (LATE, tails[t])
        column_tiles(start, width, tile)

    def collect_x(t, n, kk):
        w = ways[t]
        for h in both:
            x_first[t][kk, h].third()

        def tile(cols):
            total = lpart[t, n % 2, w.x, :, cols].astype(jnp.float32)
            total = total + jnp.sum(lnear[t, kk, :, :, cols].astype(jnp.float32), axis=0)
            zpart[t, kk, :, cols] = total.astype(jnp.bfloat16)

        column_tiles(0, LATE, tile)
        if kk == 2:
            b_then[t].first()
        if kk in (1, 3):
            b_then[t].second(1 if kk == 1 else -1)

    for n, kk in enumerate(order):
        if n + 1 < SIDE:
            send_home(order[n + 1])
        for t in both:
            stay(t, kk).wait()
            make_pick(t, kk)
            weights.job()
            if n >= 2:
                for h in both:
                    x_first[t][order[n - 2], h].drain()
            for h in both:
                sum_experts(t, n, kk, h)
                x_first[t][kk, h].first()
            sum_experts(t, n, kk, 2)
            if kk == 2:
                b_first[t].first()
            if kk in (1, 3):
                b_first[t].second(1 if kk == 1 else -1)
        for t in both:
            for h in both:
                x_first[t][kk, h].second(1)
                x_first[t][kk, h].second(-1)
        weights.job()
        if n >= 1:
            for t in both:
                collect_x(t, n - 1, order[n - 1])

    for t in both:
        b_first[t].third()
        for i in range(SIDE):

            def tile(cols, t=t, i=i):
                total = fpart[t][0, i, :, cols].astype(jnp.float32)
                total = total + jnp.sum(fnear[t][:, i, :, cols].astype(jnp.float32), axis=0)
                fsum[t][i, :, cols] = total.astype(jnp.bfloat16)

            column_tiles(0, tails[t], tile)
        x_then[t].first()
    weights.end()
    for t in both:
        x_then[t].second(1)
        x_then[t].second(-1)
    results = (mixed_ref, gtok_ref)
    for t in both:
        collect_x(t, 3, 0)
        b_then[t].third()

        def tile(cols, t=t):
            total = zpart[t, 0, :, cols].astype(jnp.float32)
            total = total + jnp.sum(znear[t, :, :, cols].astype(jnp.float32), axis=0)
            results[t][:, cols] = total.astype(jnp.bfloat16)

        column_tiles(0, LATE, tile)
    for t in both:
        w = ways[t]
        x_then[t].third()

        def late(cols, t=t, w=w):
            total = fsum[t][w.x, :, cols].astype(jnp.float32)
            return total + jnp.sum(xnear[t][:, :, cols].astype(jnp.float32), axis=0)

        def tile(cols, t=t, late=late):
            results[t][:, pl.ds(cols.start + LATE, cols.size)] = late(cols).astype(jnp.bfloat16)

        column_tiles(0, D - LATE, tile)
        if t == 1:
            mark_ref[...] = late(pl.ds(D - LATE, 128))

    for t in both:
        for n, kk in enumerate(order):
            for piece in range(3):
                for d in (1, 2, 3):
                    home(t, kk, piece, d).wait_send()
            if n >= 2:
                for h in both:
                    x_first[t][kk, h].drain()
        b_then[t].drain()
        b_first[t].drain()
        x_then[t].drain()


def bring_back(out_rows, grad_rows, tables, x_rows, g_rows, hid, grads):
    dma = pltpu.SemaphoreType.DMA
    vmem = pl.BlockSpec(memory_space=pltpu.VMEM)
    hbm = pl.BlockSpec(memory_space=pl.ANY)
    buf = lambda *shape: pltpu.VMEM(shape, jnp.bfloat16)
    pair = lambda *lead: [buf(*lead, D - LATE), buf(*lead, WIDE - LATE)]
    return pl.pallas_call(
        return_kernel,
        name="bring_back",
        out_shape=(
            jax.ShapeDtypeStruct((TOK, D), jnp.bfloat16),
            jax.ShapeDtypeStruct((TOK, D), jnp.bfloat16),
            jax.ShapeDtypeStruct((TOK, 128), jnp.float32),
            jax.ShapeDtypeStruct((1, D, FF // 2), jnp.bfloat16),
            jax.ShapeDtypeStruct((1, D, FF // 2), jnp.bfloat16),
            jax.ShapeDtypeStruct((1, FF, D // 2), jnp.bfloat16),
            jax.ShapeDtypeStruct((WeightGrads.JOBS, 256, FF), jnp.bfloat16),
        ),
        in_specs=[hbm, hbm, vmem, hbm, hbm, hbm, hbm],
        out_specs=(vmem, vmem, vmem, hbm, hbm, hbm, hbm),
        scratch_shapes=[
            buf(SIDE, SIDE, GROUP, D), buf(SIDE, SIDE, GROUP, WIDE),
            buf(SIDE * TOK, SIDE * GROUP),
            buf(2, 2, SIDE, TOK, LATE), buf(2, SIDE, 2, TOK, LATE), buf(2, SIDE, 2, TOK // 2, LATE),
            buf(2, SIDE, TOK, LATE), buf(2, 2, TOK, LATE), buf(2, 2, TOK // 2, LATE),
            *pair(SIDE, SIDE, TOK), *pair(2, SIDE, TOK), *pair(2, 2, TOK),
            *pair(SIDE, TOK), *pair(2, TOK), *pair(2, TOK // 2),
            dma((RINGS, 4)), dma((RINGS, 4)),
            dma((2, SIDE, 3, 3)), dma((2, SIDE, 3, 3)),
            dma((2, SIDE)),
            buf(2, ROWS, FF), buf(ROWS, FF), buf(2, 2, ROWS, 256),
            buf(2, 256, FF), buf(2, 256, FF), buf(256, FF), buf(2, 2, 256, FF // 2),
            buf(2, FF, 256),
            dma((12, 2)), dma((12,)), dma((12,)), dma((12,)), dma((12, 2)), dma((2,)),
        ],
        compiler_params=pltpu.CompilerParams(
            collective_id=3, has_side_effects=True, vmem_limit_bytes=VMEM_LIMIT
        ),
    )(out_rows, grad_rows, tables, x_rows, g_rows, hid, grads)


def body(tokens, route_ids, route_probs, cotangent, w_gate, w_up, w_down):
    x_rows, g_rows, tables, out_rows, grad_rows, hidden, grads = dispatch(
        route_ids.T, route_probs.T, tokens, cotangent, w_gate, w_up, w_down
    )
    mixed, grad_tokens, marks, grad_gate, grad_up, grad_down, _ = bring_back(
        out_rows, grad_rows, tables, x_rows.reshape(ROWS, D), g_rows.reshape(ROWS, D),
        hidden.reshape(ROWS, FF), grads.reshape(2, ROWS, FF),
    )
    product = marks[:, :EXPERTS] + marks[:, EXPERTS:]
    chosen = route_ids[:, :, None] == jnp.arange(EXPERTS, dtype=jnp.int32)[None, None, :]
    grad_probs = jnp.sum(jnp.where(chosen, product[:, None, :], 0.0), axis=2) / route_probs
    return (mixed, grad_tokens, grad_probs, grad_gate, grad_up, grad_down)


def solution(mesh):
    both = P(("dp", "expert"), None)
    mine = P("expert", None, None)
    split = P("expert", None, "dp")
    return jax.shard_map(
        body,
        mesh=mesh,
        in_specs=(both, both, both, both, mine, mine, mine),
        out_specs=(both, both, both, split, split, split),
        check_vma=False,
    )
```

```python
import functools

import jax
import jax.numpy as jnp
from jax import lax
from jax.experimental import pallas as pl
from jax.experimental.pallas import tpu as pltpu
from jax.sharding import PartitionSpec as P

D = 2048
FF = 768
TOP = 8
TOK = 128
CAP = 28
SIDE = 4
EXPERTS = 64
GROUP = SIDE * CAP
ROWS = 16 * GROUP
WIDE = D + 128
LATE = 1536
PIECES = ((0, 768), (768, 768), (1536, 512))
RINGS = 24
TURN_ORDER = "0101010101010011"
START_AHEAD = 4
PASS_AHEAD = 2
EXPERTS_AFTER = (9, 15, 15, 15)
MESH = pl.DeviceIdType.MESH
VMEM_LIMIT = 63 * 1024 * 1024


def where_am_i():
    e = lax.axis_index("expert")
    return lax.axis_index("dp"), e // 16, (e // 4) % 4, e % 4


class Way:
    def __init__(self, t):
        self.t = t
        self.dp, z, self.x, y = where_am_i()
        self.a, self.b = (y, z) if t == 0 else (z, y)

    def dev(self, a, b, x):
        z, y = (b, a) if self.t == 0 else (a, b)
        return (self.dp, z * 16 + x * 4 + y)

    def block(self, a, b):
        return a * 4 + b if self.t == 0 else b * 4 + a


def step(v, d):
    return lax.rem(v + d + SIDE, SIDE)


def greet_lines():
    dp, z, x, y = where_am_i()
    barrier = pltpu.get_barrier_semaphore()
    for d in (1, 2, 3):
        for to in (
            step(z, d) * 16 + x * 4 + y,
            z * 16 + step(x, d) * 4 + y,
            z * 16 + x * 4 + step(y, d),
        ):
            pl.semaphore_signal(barrier, inc=1, device_id=(dp, to), device_id_type=MESH)
    pl.semaphore_signal(barrier, inc=1, device_id=(1 - dp, z * 16 + x * 4 + y), device_id_type=MESH)
    pl.semaphore_wait(barrier, 10)


def remote(src, dst, send, recv, dev):
    return pltpu.make_async_remote_copy(
        src_ref=src, dst_ref=dst, send_sem=send, recv_sem=recv, device_id=dev, device_id_type=MESH
    )


def own_table(t, ids_ref, probs_ref):
    row = lax.broadcasted_iota(jnp.int32, (TOK, TOK), 0)
    b, x, kind, a = row // 32, (row // 8) % 4, (row // 4) % 2, row % 4
    expert = b * 16 + x * 4 + a if t == 0 else a * 16 + x * 4 + b
    hit = jnp.zeros((TOK, TOK), jnp.float32)
    weight = jnp.zeros((TOK, TOK), jnp.float32)
    for k in range(TOP):
        same = expert == ids_ref[k : k + 1, :]
        hit = jnp.where(same, 1.0, hit)
        weight = jnp.where(same, probs_ref[k : k + 1, :], weight)
    before = lax.broadcasted_iota(jnp.int32, (TOK, TOK), 0) < lax.broadcasted_iota(
        jnp.int32, (TOK, TOK), 1
    )
    before = jnp.where(before, 1.0, 0.0).astype(jnp.bfloat16)
    slot = jnp.dot(hit.astype(jnp.bfloat16), before, preferred_element_type=jnp.float32)
    slot = jnp.where(hit > 0.5, slot, -1000.0)
    return jnp.where(kind == 0, slot, weight)


def lane_rows(tables, kind, a):
    return [tables[xs, kind * 4 + a : kind * 4 + a + 1, :] for xs in range(SIDE)]


def hits_of(tables, a):
    slots = jnp.concatenate(
        [v + float(CAP * xs) for xs, v in enumerate(lane_rows(tables, 0, a))], axis=1
    )
    row = lax.broadcasted_iota(jnp.int32, (GROUP, SIDE * TOK), 0).astype(jnp.float32)
    return row == slots


class Gather:
    def __init__(self, n, sems, me, dev, block, half):
        self.send, self.recv = sems
        self.n, self.me, self.dev, self.block, self.half = n, me, dev, block, half

    def copy(self, ref, at, s):
        return remote(ref, ref, self.send.at[self.n, at], self.recv.at[self.n, at],
                      self.dev(step(self.me, s)))

    def near(self, s):
        return self.copy(self.block(self.me), 0 if s > 0 else 1, s)

    def far(self, s):
        return self.copy(self.half(step(self.me, -s), 0 if s > 0 else 1), 2 if s > 0 else 3, s)

    def start(self):
        for s in (1, -1):
            self.near(s).start()

    def pass_on(self):
        for s in (1, -1):
            self.near(s).wait_recv()
            self.far(s).start()

    def finish(self):
        for s in (1, -1):
            self.far(s).wait_recv()

    def drain(self):
        for s in (1, -1):
            self.near(s).wait_send()
            self.far(s).wait_send()


def column_tiles(start, width, tile):
    def one(c, _):
        tile(pl.ds(pl.multiple_of(start + c * 256, 128), 256))
        return 0

    lax.fori_loop(0, width // 256, one, 0)
    if width % 256:
        tile(pl.ds(start + width // 256 * 256, width % 256))


def dispatch_kernel(
    ids_ref, probs_ref, tok_ref, cot_ref, w_gate, w_up, w_down,
    x_rows, g_rows, tab_out, out_rows, grad_rows, hid_rows, gu_rows,
    gath, stage, own_tab, tab_a, tab_b, pick, scale,
    x_here, g_here, wgu, wd, out_st, grad_st, hid_st, gu_st,
    gs, gr, s3, r3, ts1, tr1, ts2, tr2, ls, wsem, xsem, osem,
):
    ways = (Way(0), Way(1))
    rows_out = (x_here, g_here)
    sems = (gs, gr)
    weight_loads = [pltpu.make_async_copy(src.at[0], dst, wsem.at[n])
                    for n, (src, dst) in enumerate(((w_gate, wgu.at[:, pl.ds(0, FF)]),
                                               (w_up, wgu.at[:, pl.ds(FF, FF)]), (w_down, wd)))]
    for copy in weight_loads:
        copy.start()

    for t, src in ((0, tok_ref), (1, cot_ref)):
        w = ways[t]
        own_tab[t] = own_table(t, ids_ref, probs_ref).reshape(16, 8, TOK)
        gath[t, w.b, w.x] = src[...]
        tab_a[t, w.b] = own_tab[t, pl.ds(w.b * 4, 4)]
    greet_lines()

    count = iter(range(RINGS))

    def along_b(t, piece):
        w, cols = ways[t], pl.ds(*PIECES[piece])
        return Gather(next(count), sems, w.b, lambda i: w.dev(w.a, i, w.x),
                      lambda i: gath.at[t, i, w.x, :, cols],
                      lambda i, u: gath.at[t, i, w.x, pl.ds(u * 64, 64), cols])

    def along_x(t, kk, piece):
        w, cols = ways[t], pl.ds(*PIECES[piece])
        bs = step(w.b, -kk)
        return Gather(next(count), sems, w.x, lambda i: w.dev(w.a, w.b, i),
                      lambda i: gath.at[t, bs, i, :, cols],
                      lambda i, u: gath.at[t, bs, i, pl.ds(u * 64, 64), cols])

    def lines_b(t):
        w, cols = ways[t], pl.ds(*PIECES[2])
        return Gather(next(count), sems, w.b, lambda i: w.dev(w.a, i, w.x),
                      lambda i: gath.at[t, i, :, :, cols],
                      lambda i, u: gath.at[t, i, pl.ds(u * 2, 2), :, cols])

    both = (0, 1)
    order = (0, 1, 3, 2)
    slot_of = lambda kk: order.index(kk) % 2
    b_first = [[along_b(t, h) for h in both] for t in both]
    x_then = [{(kk, h): along_x(t, kk, h) for kk in range(SIDE) for h in both} for t in both]
    x_first = [along_x(t, 0, 2) for t in both]
    b_then = [lines_b(t) for t in both]

    def first_tab(t, d):
        w = ways[t]
        to = step(w.b, d)
        return remote(own_tab.at[t, pl.ds(to * 4, 4)], tab_a.at[t, w.b],
                      ts1.at[t, d - 1], tr1.at[t, d - 1], w.dev(w.a, to, w.x))

    def second_tab(t, kk, d):
        w = ways[t]
        bs = step(w.b, -kk)
        to = step(w.x, d)
        return remote(tab_a.at[t, bs, to], tab_b.at[t, bs, w.x],
                      ts2.at[t, kk, d - 1], tr2.at[t, kk, d - 1], w.dev(w.a, w.b, to))

    def third(t, kk, piece, d):
        w = ways[t]
        bs = step(w.b, -kk)
        to = step(w.a, d)
        cols = pl.ds(*PIECES[piece])
        return remote(stage.at[t, slot_of(kk), to, :, cols],
                      rows_out[t].at[w.block(w.a, bs), :, cols],
                      s3.at[t, kk, piece, d - 1], r3.at[t, kk, piece, d - 1],
                      w.dev(to, w.b, w.x))

    def kept(t, kk, piece):
        w = ways[t]
        bs = step(w.b, -kk)
        cols = pl.ds(*PIECES[piece])
        return pltpu.make_async_copy(stage.at[t, slot_of(kk), w.a, :, cols],
                                     rows_out[t].at[w.block(w.a, bs), :, cols],
                                     ls.at[t, kk, piece])

    def share_tab(t, kk):
        w = ways[t]
        bs = step(w.b, -kk)
        if kk > 0:
            first_tab(t, kk).wait_recv()
        tab_b[t, bs, w.x] = tab_a[t, bs, w.x]
        for d in (1, 2, 3):
            second_tab(t, kk, d).start()

    def make_pick(t, kk):
        for d in (1, 2, 3):
            second_tab(t, kk, d).wait_recv()
        tables = tab_b[t, step(ways[t].b, -kk)]
        for a in range(SIDE):
            at = slice(a * GROUP, (a + 1) * GROUP)
            hit = hits_of(tables, a)
            pick[t, at, :] = jnp.where(hit, 1.0, 0.0).astype(jnp.bfloat16)
            if t == 1:
                weight = jnp.concatenate(lane_rows(tables, 1, a), axis=1)
                weight = jnp.sum(jnp.where(hit, weight, 0.0), axis=1, keepdims=True)
                scale[at, :] = jnp.broadcast_to(weight, (GROUP, 128))

    def send_rows(t, kk, piece):
        bs = step(ways[t].b, -kk)

        def tile(cols):
            block = gath[t, bs, :, :, cols].reshape(SIDE * TOK, cols.size)
            rows = jnp.dot(pick[t], block, preferred_element_type=jnp.float32)
            if t == 1:
                rows = rows * jnp.concatenate([scale[...]] * (cols.size // 128), axis=1)
            stage[t, slot_of(kk), :, :, cols] = rows.astype(jnp.bfloat16).reshape(SIDE, GROUP, cols.size)

        if order.index(kk) >= 2:
            leave(t, order[order.index(kk) - 2], piece)
        column_tiles(*PIECES[piece], tile)
        for d in (1, 2, 3):
            third(t, kk, piece, d).start()
        kept(t, kk, piece).start()

    settled = set()

    def settle(t, kk, piece):
        if (t, kk, piece) not in settled:
            settled.add((t, kk, piece))
            kept(t, kk, piece).wait()

    def leave(t, kk, piece):
        for d in (1, 2, 3):
            third(t, kk, piece, d).wait_send()
        settle(t, kk, piece)

    def arrive(t, kk):
        for piece in range(3):
            for d in (1, 2, 3):
                third(t, kk, piece, d).wait_recv()
            settle(t, kk, piece)

    dp, z, x, y = where_am_i()
    kept_rows = [pltpu.make_async_copy(here, rows, xsem.at[n])
                 for n, (here, rows) in enumerate(((x_here, x_rows), (g_here, g_rows)))]

    def results(blocks):
        copies = []
        for u, at in enumerate(blocks):
            pairs = ((out_st.at[u], out_rows.at[at]), (grad_st.at[u], grad_rows.at[at]),
                     (hid_st.at[u], hid_rows.at[at]), (gu_st.at[:, u], gu_rows.at[:, at]))
            copies += [pltpu.make_async_copy(src, dst, osem.at[u, n])
                       for n, (src, dst) in enumerate(pairs)]
        return copies

    def block_of(m_y, m_z):
        turn = lambda m: m + m // 2 - 2 * (m // 3)
        return step(y, -turn(m_y)) * 4 + step(z, -turn(m_z))

    def experts(m):
        if m == 1:
            for copy in weight_loads:
                copy.wait()
        needs = {
            1: [(t, k2) for k2 in order[:2] for t in both],
            2: [(t, order[2]) for t in both],
            3: [(0, order[3])],
            4: [(1, order[3])],
        }
        for t, k2 in needs[m]:
            arrive(t, k2)
        if m >= 3:
            kept_rows[m - 3].start()
        many = 2 * GROUP

        def some(p, _):
            if m == 1:
                blocks = (block_of(0, 1 - p), block_of(1, p))
            elif m == 2:
                blocks = (block_of(p, 2), block_of(2, p))
            elif m == 3:
                blocks = (block_of(2 * p, 3), block_of(1 + p, 3 - p))
            else:
                blocks = (block_of(3, 2 * p), block_of(3, 2 * p + 1))
            rows = jnp.concatenate([x_here[at] for at in blocks], axis=0)
            pre = jnp.dot(rows, wgu[...], preferred_element_type=jnp.float32)
            gate_pre, up_pre = pre[:, :FF], pre[:, FF:]
            sigmoid = jax.nn.sigmoid(gate_pre)
            activation = gate_pre * sigmoid
            derivative = sigmoid * (1.0 + gate_pre * (1.0 - sigmoid))
            hidden = (activation * up_pre).astype(jnp.bfloat16)

            def settle_results():
                for copy in results(blocks):
                    copy.wait()

            if m == 1:
                pl.when(p > 0)(settle_results)
            else:
                settle_results()
            hid_st[...] = hidden.reshape(2, GROUP, FF)
            out = jnp.dot(hidden, wd[...], preferred_element_type=jnp.float32)
            out_st[...] = out.astype(jnp.bfloat16).reshape(2, GROUP, D)
            grads = jnp.concatenate([g_here[at] for at in blocks], axis=0)
            grad_hidden = contract_last(grads, wd[...])
            gate_grad = (grad_hidden * up_pre * derivative).astype(jnp.bfloat16)
            up_grad = (grad_hidden * activation).astype(jnp.bfloat16)
            for half in range(2):
                cols = slice(half * FF // 2, (half + 1) * FF // 2)
                gu_st[half, :, :, : FF // 2] = gate_grad[:, cols].reshape(2, GROUP, FF // 2)
                gu_st[half, :, :, FF // 2 :] = up_grad[:, cols].reshape(2, GROUP, FF // 2)
            grad = contract_last(jnp.concatenate([gate_grad, up_grad], axis=1), wgu[...])
            grad_st[:, :, :D] = grad.astype(jnp.bfloat16).reshape(2, GROUP, D)
            product = jnp.sum(hidden.astype(jnp.float32) * grad_hidden, axis=1, keepdims=True)
            high = product.astype(jnp.bfloat16).astype(jnp.float32)
            low = product - high
            lane = lax.broadcasted_iota(jnp.int32, (many, 128), 1)
            me = lax.axis_index("expert")
            marks = jnp.where(lane == me, high, 0.0)
            marks = jnp.where(lane == me + EXPERTS, low, marks)
            grad_st[:, :, D:] = marks.astype(jnp.bfloat16).reshape(2, GROUP, 128)
            for copy in results(blocks):
                copy.start()
            return 0

        lax.fori_loop(0, 2, some, 0)
        if m == 4:
            for copy in results((0, 1)):
                copy.wait()
            for copy in kept_rows:
                copy.wait()

    turns = [[(t, kk, h) for kk in order for h in both] for t in both]
    plan = []
    for c in TURN_ORDER:
        plan.append(turns[int(c)].pop(0))
    begun = {(t, 0, h) for t in both for h in both}
    passed = {(t, 0, 0) for t in both}

    def begin(t, kk, h):
        if (t, kk, h) in begun:
            return
        begun.add((t, kk, h))
        if kk == 2:
            b_first[t][h].finish()
        if h == 0 and kk != 0:
            share_tab(t, kk)
        x_then[t][kk, h].start()

    def pass_on(t, kk, h):
        if (t, kk, h) not in passed:
            passed.add((t, kk, h))
            x_then[t][kk, h].pass_on()

    for t in both:
        for d in (1, 2, 3):
            first_tab(t, d).start()
        share_tab(t, 0)
        x_first[t].start()
    for h in both:
        for t in both:
            x_then[t][0, h].start()
        for t in both:
            b_first[t][h].start()
    for t in both:
        x_first[t].pass_on()
    for t in both:
        x_then[t][0, 0].pass_on()
    for t in both:
        b_first[t][0].pass_on()
    for t in both:
        x_first[t].finish()
        b_then[t].start()
    for t in both:
        b_first[t][1].pass_on()
    for n, (t, kk, h) in enumerate(plan):
        if n + START_AHEAD < len(plan):
            begin(*plan[n + START_AHEAD])
        for item in plan[: n + PASS_AHEAD + 1]:
            pass_on(*item)
        x_then[t][kk, h].finish()
        if h == 0:
            make_pick(t, kk)
        send_rows(t, kk, h)
        if h == 1:
            if kk == 1:
                b_then[t].pass_on()
            if kk == 2:
                b_then[t].finish()
            send_rows(t, kk, 2)
        for m, after in enumerate(EXPERTS_AFTER):
            if after == n:
                experts(m + 1)

    tab_out[...] = tab_b[...]
    for t in both:
        for kk in range(SIDE):
            for d in (1, 2, 3):
                second_tab(t, kk, d).wait_send()
                if kk in order[2:]:
                    for piece in range(3):
                        third(t, kk, piece, d).wait_send()
        for d in (1, 2, 3):
            first_tab(t, d).wait_send()
        for ring in (*b_first[t], *x_then[t].values(), x_first[t], b_then[t]):
            ring.drain()


def dispatch(ids_t, probs_t, tokens, cotangent, w_gate, w_up, w_down):
    dma = pltpu.SemaphoreType.DMA
    vmem = pl.BlockSpec(memory_space=pltpu.VMEM)
    hbm = pl.BlockSpec(memory_space=pl.ANY)
    buf = lambda *shape: pltpu.VMEM(shape, jnp.bfloat16)
    return pl.pallas_call(
        dispatch_kernel,
        name="dispatch",
        out_shape=(
            jax.ShapeDtypeStruct((16, GROUP, D), jnp.bfloat16),
            jax.ShapeDtypeStruct((16, GROUP, D), jnp.bfloat16),
            jax.ShapeDtypeStruct((2, SIDE, SIDE, 8, TOK), jnp.float32),
            jax.ShapeDtypeStruct((16, GROUP, D), jnp.bfloat16),
            jax.ShapeDtypeStruct((16, GROUP, WIDE), jnp.bfloat16),
            jax.ShapeDtypeStruct((16, GROUP, FF), jnp.bfloat16),
            jax.ShapeDtypeStruct((2, 16, GROUP, FF), jnp.bfloat16),
        ),
        in_specs=[vmem] * 4 + [hbm] * 3,
        out_specs=(hbm, hbm, vmem, hbm, hbm, hbm, hbm),
        scratch_shapes=[
            pltpu.VMEM((2, SIDE, SIDE, TOK, D), jnp.bfloat16),
            pltpu.VMEM((2, 2, SIDE, GROUP, D), jnp.bfloat16),
            pltpu.VMEM((2, 16, 8, TOK), jnp.float32),
            pltpu.VMEM((2, SIDE, SIDE, 8, TOK), jnp.float32),
            pltpu.VMEM((2, SIDE, SIDE, 8, TOK), jnp.float32),
            pltpu.VMEM((2, SIDE * GROUP, SIDE * TOK), jnp.bfloat16),
            pltpu.VMEM((SIDE * GROUP, 128), jnp.float32),
            buf(16, GROUP, D), buf(16, GROUP, D), buf(D, 2 * FF), buf(FF, D),
            buf(2, GROUP, D), buf(2, GROUP, WIDE), buf(2, GROUP, FF), buf(2, 2, GROUP, FF),
            dma((RINGS, 4)), dma((RINGS, 4)),
            dma((2, SIDE, 3, 3)), dma((2, SIDE, 3, 3)),
            dma((2, 3)), dma((2, 3)),
            dma((2, SIDE, 3)), dma((2, SIDE, 3)),
            dma((2, SIDE, 3)), dma((3,)), dma((2,)), dma((2, 4)),
        ],
        compiler_params=pltpu.CompilerParams(
            collective_id=1, has_side_effects=True, vmem_limit_bytes=VMEM_LIMIT
        ),
    )(ids_t, probs_t, tokens, cotangent, w_gate, w_up, w_down)


def contract_last(left_side, right_side):
    return lax.dot_general(
        left_side, right_side, (((1,), (1,)), ((), ())), preferred_element_type=jnp.float32
    )


def contract_rows(left_side, right_side):
    return lax.dot_general(
        left_side, right_side, (((0,), (0,)), ((), ())), preferred_element_type=jnp.float32
    )


class WeightGrads:
    JOBS = 12

    def __init__(self, x_rows, g_rows, hid, grads, outs, lands, bufs, sems):
        self.x_rows, self.g_rows = x_rows, g_rows
        self.out_gate, self.out_up, self.out_down = outs
        self.land = lands
        (self.grads, self.hid, self.tile, self.made, self.mine, self.got, self.done_gu,
         self.done_d) = bufs
        self.load, self.send, self.recv, self.back, self.store, self.whole = sems
        self.dp, self.e = lax.axis_index("dp"), lax.axis_index("expert")
        self.other = 1 - self.dp
        self.next = 0
        self.fill = (pltpu.make_async_copy(grads, self.grads, self.whole.at[0]),
                     pltpu.make_async_copy(hid, self.hid, self.whole.at[1]))

    def loads(self, i):
        if i < 8:
            cols = pl.ds(i * 256, 256)
            return [pltpu.make_async_copy(self.x_rows.at[:, cols], self.tile.at[i % 2, 0],
                                          self.load.at[i, 0])]
        return [
            pltpu.make_async_copy(
                self.g_rows.at[:, pl.ds(pl.multiple_of(side * (D // 2) + (i - 8) * 256, 256), 256)],
                self.tile.at[i % 2, u], self.load.at[i, u])
            for u, side in enumerate((self.other, self.dp))
        ]

    def away(self, i):
        return remote(self.made.at[i % 2], self.land.at[i], self.send.at[i], self.recv.at[i],
                      (self.other, self.e))

    def fetch(self, i):
        return pltpu.make_async_copy(self.land.at[i], self.got, self.back.at[i])

    def stores(self, i):
        if i < 8:
            at = pl.ds(i * 256, 256)
            return [pltpu.make_async_copy(self.done_gu.at[i % 2, u], out.at[0, at],
                                          self.store.at[i, u])
                    for u, out in enumerate((self.out_gate, self.out_up))]
        return [pltpu.make_async_copy(self.done_d.at[i % 2],
                                      self.out_down.at[0, :, pl.ds((i - 8) * 256, 256)],
                                      self.store.at[i, 0])]

    def begin(self):
        for copy in self.fill:
            copy.start()
        for copy in self.loads(0):
            copy.start()

    def finish(self, i):
        self.fetch(i).wait()
        if i >= 2 and (i < 8 or i >= 10):
            for copy in self.stores(i - 2):
                copy.wait()
        slot = i % 2
        total = self.mine[slot].astype(jnp.float32) + self.got[...].astype(jnp.float32)
        if i < 8:
            total = total.astype(jnp.bfloat16)
            self.done_gu[slot, 0] = total[:, : FF // 2]
            self.done_gu[slot, 1] = total[:, FF // 2 :]
        else:
            self.done_d[slot] = jnp.transpose(total).astype(jnp.bfloat16)
        for copy in self.stores(i):
            copy.start()

    def job(self):
        i = self.next
        self.next += 1
        if i > self.JOBS:
            return
        if 0 < i:
            self.away(i - 1).wait_recv()
            self.fetch(i - 1).start()
        if i < self.JOBS:
            slot = i % 2
            if i == 0:
                self.fill[0].wait()
            if i == 8:
                self.fill[1].wait()
            for copy in self.loads(i):
                copy.wait()
            if i + 1 < self.JOBS:
                for copy in self.loads(i + 1):
                    copy.start()
            if i >= 2:
                self.away(i - 2).wait_send()
            def product(u, side):
                rows = self.tile[slot, 0 if i < 8 else u]
                right = self.grads[side] if i < 8 else self.hid[...]
                return contract_rows(rows, right).astype(jnp.bfloat16)

            self.made[slot] = product(0, self.other)
            self.away(i).start()
            self.mine[slot] = product(1, self.dp)
        if 0 < i:
            self.finish(i - 1)

    def end(self):
        while self.next <= self.JOBS:
            self.job()
        for i in (10, 11):
            self.away(i).wait_send()
        for i in (6, 7, 10, 11):
            for copy in self.stores(i):
                copy.wait()


class Scatter:
    def __init__(self, n, sems, me, dev, part, half, near_at, far_at, add):
        self.send, self.recv = sems
        self.n, self.me, self.dev, self.add = n, me, dev, add
        self.part, self.half, self.near_at, self.far_at = part, half, near_at, far_at

    def copy(self, src, dst, at, s):
        return remote(src, dst, self.send.at[self.n, at], self.recv.at[self.n, at],
                      self.dev(step(self.me, s)))

    def near(self, s):
        u = 0 if s > 0 else 1
        return self.copy(self.part(s), self.near_at(u), u, s)

    def far(self, s):
        u = 0 if s > 0 else 1
        return self.copy(self.half(2, u), self.far_at(u), 2 + u, s)

    def first(self):
        for s in (1, -1):
            self.far(s).start()

    def second(self, s):
        u = 0 if s > 0 else 1
        self.far(s).wait_recv()
        self.add(self.half(s, u), self.far_at(u))
        self.near(s).start()

    def third(self):
        for s in (1, -1):
            self.near(s).wait_recv()

    def drain(self):
        for s in (1, -1):
            self.near(s).wait_send()
            self.far(s).wait_send()


def add_flat(to, more):
    width = to.shape[-1]

    def tile(cols):
        total = to[:, cols].astype(jnp.float32) + more[:, cols].astype(jnp.float32)
        to[:, cols] = total.astype(jnp.bfloat16)

    column_tiles(0, width, tile)


def add_lines(to, more):
    for i in range(2):
        add_flat(to.at[i], more.at[i])


def return_kernel(
    out_rows, grad_rows, tab_ref, x_rows, g_rows, hid, grads,
    mixed_ref, gtok_ref, mark_ref, out_gate, out_up, out_down, land,
    back0, back1, pick, lpart, lnear, lfar, zpart, znear, zfar,
    fpart0, fpart1, fnear0, fnear1, ffar0, ffar1, fsum0, fsum1, xnear0, xnear1, xfar0, xfar1,
    gs, gr, sa, ra, la, *weight_scratch,
):
    ways = (Way(0), Way(1))
    weights = WeightGrads(x_rows, g_rows, hid, grads, (out_gate, out_up, out_down),
                          land, weight_scratch[:8], weight_scratch[8:])
    rows_in = (out_rows, grad_rows)
    back, fpart, fnear, ffar = (back0, back1), (fpart0, fpart1), (fnear0, fnear1), (ffar0, ffar1)
    fsum, xnear, xfar = (fsum0, fsum1), (xnear0, xnear1), (xfar0, xfar1)
    tails = (D - LATE, WIDE - LATE)
    sems = (gs, gr)
    both = (0, 1)
    order = (2, 1, 3, 0)
    greet_lines()

    def piece_cols(t, piece):
        return pl.ds(*PIECES[piece]) if piece < 2 else pl.ds(LATE, tails[t])

    def home(t, kk, piece, d):
        w = ways[t]
        bs = step(w.b, kk)
        to = step(w.a, d)
        cols = piece_cols(t, piece)
        return remote(rows_in[t].at[w.block(to, bs), :, cols], back[t].at[bs, w.a, :, cols],
                      sa.at[t, kk, piece, d - 1], ra.at[t, kk, piece, d - 1],
                      w.dev(to, w.b, w.x))

    def stay(t, kk):
        w = ways[t]
        bs = step(w.b, kk)
        return pltpu.make_async_copy(rows_in[t].at[w.block(w.a, bs)], back[t].at[bs, w.a],
                                     la.at[t, kk])

    def send_home(kk):
        for t in both:
            stay(t, kk).start()
        for piece in range(3):
            for t in both:
                for d in (1, 2, 3):
                    home(t, kk, piece, d).start()

    send_home(order[0])
    weights.begin()
    count = iter(range(RINGS))

    def along_x(t, n, kk, h):
        w, cols = ways[t], pl.ds(*PIECES[h])
        at = n % 2
        return Scatter(next(count), sems, w.x, lambda i: w.dev(w.a, w.b, i),
                       lambda o: lpart.at[t, at, step(w.x, o), :, cols],
                       lambda o, u: lpart.at[t, at, step(w.x, o), pl.ds(u * 64, 64), cols],
                       lambda u: lnear.at[t, kk, u, :, cols],
                       lambda u: lfar.at[t, kk, u, :, cols], add_flat)

    def along_b(t):
        w = ways[t]
        return Scatter(next(count), sems, w.b, lambda i: w.dev(w.a, i, w.x),
                       lambda o: zpart.at[t, o % 4],
                       lambda o, u: zpart.at[t, o % 4, pl.ds(u * 64, 64)],
                       lambda u: znear.at[t, u], lambda u: zfar.at[t, u], add_flat)

    def lines_b(t):
        w = ways[t]
        return Scatter(next(count), sems, w.b, lambda i: w.dev(w.a, i, w.x),
                       lambda o: fpart[t].at[o % 4],
                       lambda o, u: fpart[t].at[o % 4, pl.ds(u * 2, 2)],
                       lambda u: fnear[t].at[u], lambda u: ffar[t].at[u], add_lines)

    def late_x(t):
        w = ways[t]
        return Scatter(next(count), sems, w.x, lambda i: w.dev(w.a, w.b, i),
                       lambda o: fsum[t].at[step(w.x, o)],
                       lambda o, u: fsum[t].at[step(w.x, o), pl.ds(u * 64, 64)],
                       lambda u: xnear[t].at[u], lambda u: xfar[t].at[u], add_flat)

    x_first = [{(kk, h): along_x(t, n, kk, h) for n, kk in enumerate(order) for h in both}
               for t in both]
    b_then = [along_b(t) for t in both]
    b_first = [lines_b(t) for t in both]
    x_then = [late_x(t) for t in both]

    def make_pick(t, kk):
        tables = tab_ref[t, step(ways[t].b, kk)]
        parts = []
        for a in range(SIDE):
            hit = hits_of(tables, a)
            weight = jnp.concatenate(lane_rows(tables, 1, a), axis=1) if t == 0 else 1.0
            parts.append(jnp.where(hit, weight, 0.0))
        pick[...] = jnp.transpose(jnp.concatenate(parts, axis=0)).astype(jnp.bfloat16)

    def sum_experts(t, n, kk, piece):
        bs = step(ways[t].b, kk)
        for d in (1, 2, 3):
            home(t, kk, piece, d).wait_recv()

        def tile(cols):
            rows = back[t][bs, :, :, cols].reshape(SIDE * GROUP, cols.size)
            sums = jnp.dot(pick[...], rows, preferred_element_type=jnp.float32).astype(jnp.bfloat16)
            sums = sums.reshape(SIDE, TOK, cols.size)
            if piece < 2:
                lpart[t, n % 2, :, :, cols] = sums
            else:
                fpart[t][kk, :, :, pl.ds(cols.start - LATE, cols.size)] = sums

        start, width = PIECES[piece] if piece < 2 else (LATE, tails[t])
        column_tiles(start, width, tile)

    def collect_x(t, n, kk):
        w = ways[t]
        for h in both:
            x_first[t][kk, h].third()

        def tile(cols):
            total = lpart[t, n % 2, w.x, :, cols].astype(jnp.float32)
            total = total + jnp.sum(lnear[t, kk, :, :, cols].astype(jnp.float32), axis=0)
            zpart[t, kk, :, cols] = total.astype(jnp.bfloat16)

        column_tiles(0, LATE, tile)
        if kk == 2:
            b_then[t].first()
        if kk in (1, 3):
            b_then[t].second(1 if kk == 1 else -1)

    for n, kk in enumerate(order):
        if n + 1 < SIDE:
            send_home(order[n + 1])
        for t in both:
            stay(t, kk).wait()
            make_pick(t, kk)
            weights.job()
            if n >= 2:
                for h in both:
                    x_first[t][order[n - 2], h].drain()
            for h in both:
                sum_experts(t, n, kk, h)
                x_first[t][kk, h].first()
            sum_experts(t, n, kk, 2)
            if kk == 2:
                b_first[t].first()
            if kk in (1, 3):
                b_first[t].second(1 if kk == 1 else -1)
        for t in both:
            for h in both:
                x_first[t][kk, h].second(1)
                x_first[t][kk, h].second(-1)
        weights.job()
        if n >= 1:
            for t in both:
                collect_x(t, n - 1, order[n - 1])

    for t in both:
        b_first[t].third()
        for i in range(SIDE):

            def tile(cols, t=t, i=i):
                total = fpart[t][0, i, :, cols].astype(jnp.float32)
                total = total + jnp.sum(fnear[t][:, i, :, cols].astype(jnp.float32), axis=0)
                fsum[t][i, :, cols] = total.astype(jnp.bfloat16)

            column_tiles(0, tails[t], tile)
        x_then[t].first()
    weights.end()
    for t in both:
        x_then[t].second(1)
        x_then[t].second(-1)
    results = (mixed_ref, gtok_ref)
    for t in both:
        collect_x(t, 3, 0)
        b_then[t].third()

        def tile(cols, t=t):
            total = zpart[t, 0, :, cols].astype(jnp.float32)
            total = total + jnp.sum(znear[t, :, :, cols].astype(jnp.float32), axis=0)
            results[t][:, cols] = total.astype(jnp.bfloat16)

        column_tiles(0, LATE, tile)
    for t in both:
        w = ways[t]
        x_then[t].third()

        def late(cols, t=t, w=w):
            total = fsum[t][w.x, :, cols].astype(jnp.float32)
            return total + jnp.sum(xnear[t][:, :, cols].astype(jnp.float32), axis=0)

        def tile(cols, t=t, late=late):
            results[t][:, pl.ds(cols.start + LATE, cols.size)] = late(cols).astype(jnp.bfloat16)

        column_tiles(0, D - LATE, tile)
        if t == 1:
            mark_ref[...] = late(pl.ds(D - LATE, 128))

    for t in both:
        for n, kk in enumerate(order):
            for piece in range(3):
                for d in (1, 2, 3):
                    home(t, kk, piece, d).wait_send()
            if n >= 2:
                for h in both:
                    x_first[t][kk, h].drain()
        b_then[t].drain()
        b_first[t].drain()
        x_then[t].drain()


def bring_back(out_rows, grad_rows, tables, x_rows, g_rows, hid, grads):
    dma = pltpu.SemaphoreType.DMA
    vmem = pl.BlockSpec(memory_space=pltpu.VMEM)
    hbm = pl.BlockSpec(memory_space=pl.ANY)
    buf = lambda *shape: pltpu.VMEM(shape, jnp.bfloat16)
    pair = lambda *lead: [buf(*lead, D - LATE), buf(*lead, WIDE - LATE)]
    return pl.pallas_call(
        return_kernel,
        name="bring_back",
        out_shape=(
            jax.ShapeDtypeStruct((TOK, D), jnp.bfloat16),
            jax.ShapeDtypeStruct((TOK, D), jnp.bfloat16),
            jax.ShapeDtypeStruct((TOK, 128), jnp.float32),
            jax.ShapeDtypeStruct((1, D, FF // 2), jnp.bfloat16),
            jax.ShapeDtypeStruct((1, D, FF // 2), jnp.bfloat16),
            jax.ShapeDtypeStruct((1, FF, D // 2), jnp.bfloat16),
            jax.ShapeDtypeStruct((WeightGrads.JOBS, 256, FF), jnp.bfloat16),
        ),
        in_specs=[hbm, hbm, vmem, hbm, hbm, hbm, hbm],
        out_specs=(vmem, vmem, vmem, hbm, hbm, hbm, hbm),
        scratch_shapes=[
            buf(SIDE, SIDE, GROUP, D), buf(SIDE, SIDE, GROUP, WIDE),
            buf(SIDE * TOK, SIDE * GROUP),
            buf(2, 2, SIDE, TOK, LATE), buf(2, SIDE, 2, TOK, LATE), buf(2, SIDE, 2, TOK // 2, LATE),
            buf(2, SIDE, TOK, LATE), buf(2, 2, TOK, LATE), buf(2, 2, TOK // 2, LATE),
            *pair(SIDE, SIDE, TOK), *pair(2, SIDE, TOK), *pair(2, 2, TOK),
            *pair(SIDE, TOK), *pair(2, TOK), *pair(2, TOK // 2),
            dma((RINGS, 4)), dma((RINGS, 4)),
            dma((2, SIDE, 3, 3)), dma((2, SIDE, 3, 3)),
            dma((2, SIDE)),
            buf(2, ROWS, FF), buf(ROWS, FF), buf(2, 2, ROWS, 256),
            buf(2, 256, FF), buf(2, 256, FF), buf(256, FF), buf(2, 2, 256, FF // 2),
            buf(2, FF, 256),
            dma((12, 2)), dma((12,)), dma((12,)), dma((12,)), dma((12, 2)), dma((2,)),
        ],
        compiler_params=pltpu.CompilerParams(
            collective_id=3, has_side_effects=True, vmem_limit_bytes=VMEM_LIMIT
        ),
    )(out_rows, grad_rows, tables, x_rows, g_rows, hid, grads)


def body(tokens, route_ids, route_probs, cotangent, w_gate, w_up, w_down):
    x_rows, g_rows, tables, out_rows, grad_rows, hidden, grads = dispatch(
        route_ids.T, route_probs.T, tokens, cotangent, w_gate, w_up, w_down
    )
    mixed, grad_tokens, marks, grad_gate, grad_up, grad_down, _ = bring_back(
        out_rows, grad_rows, tables, x_rows.reshape(ROWS, D), g_rows.reshape(ROWS, D),
        hidden.reshape(ROWS, FF), grads.reshape(2, ROWS, FF),
    )
    product = marks[:, :EXPERTS] + marks[:, EXPERTS:]
    chosen = route_ids[:, :, None] == jnp.arange(EXPERTS, dtype=jnp.int32)[None, None, :]
    grad_probs = jnp.sum(jnp.where(chosen, product[:, None, :], 0.0), axis=2) / route_probs
    return (mixed, grad_tokens, grad_probs, grad_gate, grad_up, grad_down)


def solution(mesh):
    both = P(("dp", "expert"), None)
    mine = P("expert", None, None)
    split = P("expert", None, "dp")
    return jax.shard_map(
        body,
        mesh=mesh,
        in_specs=(both, both, both, both, mine, mine, mine),
        out_specs=(both, both, both, split, split, split),
        check_vma=False,
    )
```
